32 devices in a mesh: expert: 16 (over z, y, x), dp: 2 (over core).
Axes of the slice: x: 2, y: 2, z: 4, core: 2. Of those that a mesh axis runs over, the one named last changes fastest.
Arguments:
- tokens: bfloat16 [512, 3584], P(('dp', 'expert')), parts along dimension 0, may hold values from -6 to 6
- expert_ids: int32 [512, 2], P(('dp', 'expert')), parts along dimension 0, may hold values from 0 to 2, as said below
- gate_weights: float32 [512, 2], P(('dp', 'expert')), parts along dimension 0, may hold values from 0.1 to 1
- replica_pick: int32 [512, 2], P(('dp', 'expert')), parts along dimension 0, may hold values from 0 to 1
- placement: int32 [4], replicated, may hold values from 0 to 2, as said below
- w_in: bfloat16 [2, 3584, 4096], P(None, None, 'expert')
- w_out: bfloat16 [4096, 3584], P('expert')
Outputs:
- moe_out: bfloat16 [512, 3584], P(('dp', 'expert')), parts along dimension 0
The draws below stay inside these ranges and needn't reach their ends.
There are 2 independent parts, one for each index of `dp`. The reference program is written for one: setup_inputs(seed, part) draws one part's arguments, and reference() takes and returns one part's arrays. A program takes and returns all parts, laid end to end along the dimension named above; an argument that names none is the same for every part. Nothing has to cross between parts.
Inputs may be any that keep to these rules, and one draw needn't show every extreme that they name: `expert_ids`: each row names 2 different experts. `placement`: every expert is named once or twice, 1 of them twice, at any positions.
All inputs are finite; a program needn't handle non-finite values.
Results may differ from the reference program's by a relative error of at most 0.012.
Values may be sent and summed in bfloat16 or wider, within the bound.
No kernel may reach another device: no remote copies, remote signals or barrier semaphores. Data moves between devices by JAX's collectives and lax.ppermute only.
A program may use at most 64 MiB of HBM per device.

```python
import jax
import jax.numpy as jnp
from jax import lax

D = 3584
F = 1024
TOP = 2
T_DEV = 16
SPLIT = 4
F_DEV = 256
PHYS = 4
REPL = 1
LOG = 3
CAP = 8
TOKENS = 256
N_EXPERT = 16


def layout(key):
    base_key = jax.random.fold_in(key, 11)
    every_expert = jnp.arange(LOG, dtype=jnp.int32)
    hot_experts = jax.random.permutation(jax.random.fold_in(base_key, 2), LOG)[:REPL].astype(jnp.int32)
    listed = jnp.concatenate([every_expert, hot_experts]).astype(jnp.int32)
    order = jax.random.permutation(jax.random.fold_in(base_key, 3), PHYS).astype(jnp.int32)
    return jnp.take(listed, order).astype(jnp.int32)


def draw_placement(key, part):
    return layout(key)


def draw_expert_ids(key, part):
    scores = jax.random.randint(jax.random.fold_in(key, 41), (TOKENS, LOG), 0, 1000, dtype=jnp.int32)
    expert_index = jnp.arange(LOG, dtype=jnp.int32)
    ranking = jax.random.permutation(jax.random.fold_in(key, 43), LOG).astype(jnp.int32)
    favour = jnp.where(ranking < REPL, 600, 0).astype(jnp.int32)
    distinct = (scores + favour[None, :]) * LOG + expert_index[None, :]
    return lax.top_k(distinct, TOP)[1].astype(jnp.int32)


def weight_base(key, shape):
    return jax.random.normal(key, shape, jnp.float32)


def draw_w_in(key, part):
    places = layout(key)
    base = weight_base(jax.random.fold_in(key, 21), (2, D, LOG, F)) * D ** (-0.5)
    taken = jnp.take(base, places, axis=2)
    return taken.reshape(2, D, PHYS * F).astype(jnp.bfloat16)


def draw_w_out(key, part):
    places = layout(key)
    base = weight_base(jax.random.fold_in(key, 31), (LOG, F, D)) * F ** (-0.5)
    taken = jnp.take(base, places, axis=0)
    return taken.reshape(PHYS * F, D).astype(jnp.bfloat16)


def place_ends(array, stream_key, least, largest):
    dims = array.shape
    place = [jax.random.randint(jax.random.fold_in(stream_key, axis), (), 0, dims[axis]) for axis in range(len(dims))]
    array = array.at[tuple(place)].set(least)
    longest = dims.index(max(dims))
    place[longest] = (place[longest] + 1) % dims[longest]
    return array.at[tuple(place)].set(largest)


def shard_levels(own_key, extent, split, low, high):
    loudness, own = 1.0, jax.random.fold_in(own_key, 6)
    for position, parts in split:
        draws = jnp.exp(jax.random.uniform(jax.random.fold_in(own, position), (parts,), jnp.float32, low / len(split), high / len(split)))
        loudness = loudness * jnp.repeat(draws, extent[position] // parts).reshape([-1 if axis == position else 1 for axis in range(len(extent))])
    return loudness


def gaussian(rng, dims, scale, limit, shards=(), kind=jnp.bfloat16):
    array = scale * jax.random.normal(rng, dims, jnp.float32)
    if shards:
        array = array * shard_levels(rng, dims, shards, -0.22, 0.18)
    return jnp.clip(array, -limit, limit).astype(kind)


def setup_inputs(seed: int = 0, part: int = 0) -> dict:
    seeds = jax.random.split(jax.random.key(seed), 8)
    own_keys = jax.random.split(jax.random.fold_in(seeds[7], part), 8)
    tokens = gaussian(own_keys[0], (TOKENS, D), 1.0, 6.0, ((0, 16),))
    expert_ids = draw_expert_ids(jax.random.fold_in(jax.random.fold_in(seeds[7], part), 71), part)
    gate_weights = jnp.clip(0.1 + 0.9 * jax.random.uniform(own_keys[2], (TOKENS, TOP), jnp.float32) ** shard_levels(own_keys[2], (TOKENS, TOP), ((0, 16),), -0.2, 0.2), 0.1, 1.0)
    replica_pick = place_ends(jax.random.randint(own_keys[3], (TOKENS, TOP), 0, 2), jax.random.fold_in(own_keys[3], 1), 0, 1).astype(jnp.int32)
    placement = draw_placement(jax.random.fold_in(seeds[7], 71), part)
    w_in = draw_w_in(jax.random.fold_in(seeds[7], 71), part)
    w_out = draw_w_out(jax.random.fold_in(seeds[7], 71), part)
    return dict(tokens=tokens, expert_ids=expert_ids, gate_weights=gate_weights, replica_pick=replica_pick, placement=placement, w_in=w_in, w_out=w_out)


def route_block(expert_ids, replica_pick, gate_weights, placement, slot_count, capacity):
    tok_count, top_count = expert_ids.shape
    copy_index = jnp.arange(slot_count, dtype=jnp.int32)
    same_expert = placement[:, None] == placement[None, :]
    before = jnp.sum((same_expert & (copy_index[:, None] < copy_index[None, :])).astype(jnp.int32), axis=0)
    matches = placement[None, None, :] == expert_ids[:, :, None]
    copies = jnp.sum(matches.astype(jnp.int32), axis=-1)
    wanted = replica_pick % copies
    chosen = (matches & (before[None, None, :] == wanted[:, :, None])).astype(jnp.int32)
    flat_hot = chosen.reshape(tok_count * top_count, slot_count)
    earlier = jnp.cumsum(flat_hot, axis=0) - flat_hot
    slot_rank = jnp.sum(earlier * flat_hot, axis=-1).reshape(tok_count, top_count)
    slot_index = jnp.arange(capacity, dtype=jnp.int32)
    in_slot = chosen[:, :, :, None] * (slot_rank[:, :, None, None] == slot_index[None, None, None, :]).astype(jnp.int32)
    in_slot = in_slot.astype(jnp.float32)
    pick_rows = jnp.sum(in_slot, axis=1).reshape(tok_count, slot_count * capacity).T
    combine_rows = jnp.sum(in_slot * gate_weights[:, :, None, None], axis=1).reshape(tok_count, slot_count * capacity)
    return pick_rows, combine_rows


def expert_copy(args):
    received, gate_w, up_w, down_w = args
    gate = jnp.dot(received, gate_w, preferred_element_type=jnp.float32)
    upper = jnp.dot(received, up_w, preferred_element_type=jnp.float32)
    hidden = (jax.nn.silu(gate) * upper).astype(jnp.bfloat16)
    hidden_blocks = hidden.reshape(received.shape[0], SPLIT, F_DEV).astype(jnp.float32)
    down_blocks = down_w.reshape(SPLIT, F_DEV, D).astype(jnp.float32)
    partial_value = jnp.einsum("rjf,jfd->jrd", hidden_blocks, down_blocks).astype(jnp.bfloat16)
    return jnp.sum(partial_value.astype(jnp.float32), axis=0)


def reference(tokens, expert_ids, gate_weights, replica_pick, placement, w_in, w_out):
    tok_blocks = tokens.reshape(N_EXPERT, T_DEV, D)
    id_blocks = expert_ids.reshape(N_EXPERT, T_DEV, TOP)
    pick_blocks = replica_pick.reshape(N_EXPERT, T_DEV, TOP)
    gate_blocks = gate_weights.reshape(N_EXPERT, T_DEV, TOP)
    pick_rows, combine_rows = jax.vmap(lambda a, b, c: route_block(a, b, c, placement, PHYS, CAP))(id_blocks, pick_blocks, gate_blocks)
    slot_rows = jnp.einsum("spt,std->spd", pick_rows, tok_blocks.astype(jnp.float32)).astype(jnp.bfloat16)
    slot_rows = slot_rows.reshape(N_EXPERT, PHYS, CAP, D).transpose(1, 0, 2, 3).reshape(PHYS, N_EXPERT * CAP, D)
    gate_all = w_in[0].reshape(D, PHYS, F).transpose(1, 0, 2)
    up_all = w_in[1].reshape(D, PHYS, F).transpose(1, 0, 2)
    down_all = w_out.reshape(PHYS, F, D)
    expert_out = lax.map(expert_copy, (slot_rows, gate_all, up_all, down_all))
    expert_out = expert_out.reshape(PHYS, N_EXPERT, CAP, D).transpose(1, 0, 2, 3).reshape(N_EXPERT, PHYS * CAP, D)
    moe_out = jnp.einsum("stk,skd->std", combine_rows, expert_out, precision=lax.Precision.HIGHEST)
    return moe_out.reshape(TOKENS, D).astype(jnp.bfloat16)
```

```python
import functools

import jax
import jax.numpy as jnp
from jax import lax
from jax.experimental import pallas as pl
from jax.experimental.pallas import tpu as pltpu
from jax.sharding import PartitionSpec as P

VMEM = pl.BlockSpec(memory_space=pltpu.VMEM)
SMEM = pl.BlockSpec(memory_space=pltpu.SMEM)
MIB = 1 << 20


def iota(shape, axis):
    return lax.broadcasted_iota(jnp.int32, shape, axis)


def route_kernel(group_size, placement, expert_ids, replica_pick, gate_weights, tokens, *outs):
    row_outs, combine_out = outs[:-1], outs[-1]
    slot_count, capacity = len(row_outs), row_outs[0].shape[0]
    top_count, tok_count = expert_ids.shape
    own = lax.axis_index("expert") // group_size
    copy_row = iota((slot_count, tok_count), 0)
    named = jnp.zeros_like(copy_row)
    before = jnp.zeros_like(copy_row)
    relative = jnp.zeros_like(copy_row)
    for p in range(slot_count):
        here = copy_row == p
        named = jnp.where(here, placement[p], named)
        relative = jnp.where(here, lax.bitwise_xor(own, p), relative)
        seen = jnp.int32(0)
        for q in range(p):
            seen = seen + (placement[q] == placement[p]).astype(jnp.int32)
        before = jnp.where(here, seen, before)
    chosen = []
    for k in range(top_count):
        matches = named == expert_ids[pl.ds(k, 1), :]
        copies = jnp.sum(matches.astype(jnp.int32), axis=0, keepdims=True)
        pick = replica_pick[pl.ds(k, 1), :]
        wanted = jnp.where(pick >= copies, pick - copies, pick)
        chosen.append((matches & (before == wanted)).astype(jnp.int32))
    total = sum(chosen[1:], chosen[0])
    ahead = (iota((tok_count, tok_count), 0) < iota((tok_count, tok_count), 1)).astype(jnp.bfloat16)
    earlier = jnp.dot(
        total.astype(jnp.bfloat16), ahead, preferred_element_type=jnp.float32
    ).astype(jnp.int32)
    slot_row = iota((slot_count * capacity, tok_count), 0)
    pick_rows = jnp.zeros((slot_count * capacity, tok_count), jnp.float32)
    combine = jnp.zeros((slot_count * capacity, tok_count), jnp.float32)
    for k in range(top_count):
        rank = jnp.sum(chosen[k] * earlier, axis=0, keepdims=True)
        place = jnp.sum(chosen[k] * relative, axis=0, keepdims=True)
        slot = jnp.where(rank < capacity, place * capacity + rank, -1)
        hot = slot_row == slot
        pick_rows = pick_rows + hot.astype(jnp.float32)
        combine = combine + jnp.where(hot, gate_weights[pl.ds(k, 1), :], 0.0)
        earlier = earlier + chosen[k]
    combine_out[...] = combine
    rows = jnp.dot(pick_rows.astype(jnp.bfloat16), tokens[...], preferred_element_type=jnp.float32)
    for d in range(slot_count):
        row_outs[d][...] = rows[d * capacity : (d + 1) * capacity].astype(jnp.bfloat16)


def expert_kernel(count, group_size, *refs):
    chunks, (w_in, w_out), outs = refs[:count], refs[count : count + 2], refs[count + 2 :]
    rows = jnp.concatenate([c[...].astype(jnp.float32) for c in chunks], axis=0)
    rows = rows.astype(jnp.bfloat16)
    gate = jnp.dot(rows, w_in[0], preferred_element_type=jnp.float32)
    upper = jnp.dot(rows, w_in[1], preferred_element_type=jnp.float32)
    hidden = (gate / (1.0 + jnp.exp(-gate)) * upper).astype(jnp.bfloat16)
    partial_value = jnp.dot(hidden, w_out[...], preferred_element_type=jnp.float32)
    each = partial_value.shape[0] // group_size
    for q in range(group_size):
        outs[q][...] = partial_value[q * each : (q + 1) * each].astype(jnp.bfloat16)


def reduce_kernel(count, *refs):
    total = refs[0][...].astype(jnp.float32)
    for r in refs[1:count]:
        total = total + r[...].astype(jnp.float32)
    capacity = refs[count].shape[0]
    for d, out in enumerate(refs[count:]):
        out[...] = total[d * capacity : (d + 1) * capacity].astype(jnp.bfloat16)


def combine_kernel(combine, *refs):
    parts, out = refs[:-1], refs[-1]
    values = jnp.concatenate([p[...].astype(jnp.float32) for p in parts], axis=0)
    out[...] = lax.dot_general(
        combine[...],
        values,
        (((0,), (0,)), ((), ())),
        precision=lax.Precision.HIGHEST,
        preferred_element_type=jnp.float32,
    ).astype(jnp.bfloat16)


def call(kernel, inputs, in_specs, outs, limit):
    return pl.pallas_call(
        kernel,
        out_shape=outs,
        in_specs=in_specs,
        out_specs=jax.tree.map(lambda _: VMEM, outs),
        compiler_params=pltpu.CompilerParams(vmem_limit_bytes=limit),
    )(*inputs)


def body(tokens, expert_ids, gate_weights, replica_pick, placement, w_in, w_out):
    n_devices = lax.axis_size("expert")
    group_size = min(8, n_devices // 4)
    slot_count = n_devices // group_size
    tok_count, width = tokens.shape
    capacity = tok_count * expert_ids.shape[1] // slot_count
    chunk = jax.ShapeDtypeStruct((capacity, width), jnp.bfloat16)

    def swap(value, offset):
        return lax.ppermute(value, "expert", [(e, e ^ offset) for e in range(n_devices)])

    *slot_rows, combine = call(
        functools.partial(route_kernel, group_size),
        (placement, expert_ids.T, replica_pick.T, gate_weights.T, tokens),
        [SMEM] + [VMEM] * 4,
        [chunk] * slot_count
        + [jax.ShapeDtypeStruct((slot_count * capacity, tok_count), jnp.float32)],
        16 * MIB,
    )
    held = {}
    for d in range(slot_count):
        held[0, d] = slot_rows[0] if d == 0 else swap(slot_rows[d], d * group_size)
    for d in range(slot_count):
        for q in range(1, group_size):
            held[q, d] = swap(held[0, d], q)
    order = [(q, d) for q in range(group_size) for d in range(slot_count)]
    partial_value = call(
        functools.partial(expert_kernel, n_devices, group_size),
        [held[i] for i in order] + [w_in, w_out],
        [VMEM] * (n_devices + 2),
        [jax.ShapeDtypeStruct((slot_count * capacity, width), jnp.bfloat16)] * group_size,
        40 * MIB,
    )
    partial_value = [v if q == 0 else swap(v, q) for q, v in enumerate(partial_value)]
    summed = call(
        functools.partial(reduce_kernel, group_size),
        partial_value,
        [VMEM] * group_size,
        [chunk] * slot_count,
        16 * MIB,
    )
    returned = [v if d == 0 else swap(v, d * group_size) for d, v in enumerate(summed)]
    return call(
        combine_kernel,
        [combine] + returned,
        [VMEM] * (slot_count + 1),
        jax.ShapeDtypeStruct((tok_count, width), jnp.bfloat16),
        16 * MIB,
    )


def solution(mesh):
    in_specs = (
        P(("dp", "expert"), None),
        P(("dp", "expert"), None),
        P(("dp", "expert"), None),
        P(("dp", "expert"), None),
        P(),
        P(None, None, "expert"),
        P("expert", None),
    )
    out_specs = P(("dp", "expert"), None)
    return jax.shard_map(body, mesh=mesh, in_specs=in_specs, out_specs=out_specs, check_vma=False)
```

```python
import functools

import jax
import jax.numpy as jnp
from jax import lax
from jax.experimental import pallas as pl
from jax.experimental.pallas import tpu as pltpu
from jax.sharding import PartitionSpec as P

VMEM = pl.BlockSpec(memory_space=pltpu.VMEM)
HBM = pl.BlockSpec(memory_space=pltpu.HBM)
MIB = 1 << 20


def iota(shape, axis):
    return lax.broadcasted_iota(jnp.int32, shape, axis)


def fetch(sources, targets, sems):
    copies = [
        pltpu.make_async_copy(s, t, sems.at[i]) for i, (s, t) in enumerate(zip(sources, targets))
    ]
    for c in copies:
        c.start()
    for c in copies:
        c.wait()


def route_kernel(slot_count, capacity, *refs):
    sources, out, scratch, sems = refs[:5], refs[5], refs[6:11], refs[11]
    fetch(sources, scratch, sems)
    placement, expert_ids, replica_pick, gate_weights, tokens = scratch
    top_count, tok_count = expert_ids.shape
    width = tokens.shape[1]
    copy_row = iota((slot_count, tok_count), 0)
    named = jnp.zeros_like(copy_row)
    before = jnp.zeros_like(copy_row)
    for p in range(slot_count):
        here = copy_row == p
        named = jnp.where(here, placement[p], named)
        seen = jnp.int32(0)
        for q in range(p):
            seen = seen + (placement[q] == placement[p]).astype(jnp.int32)
        before = jnp.where(here, seen, before)
    chosen = []
    for k in range(top_count):
        matches = named == expert_ids[pl.ds(k, 1), :]
        copies = jnp.sum(matches.astype(jnp.int32), axis=0, keepdims=True)
        pick = replica_pick[pl.ds(k, 1), :]
        wanted = jnp.where(pick >= copies, pick - copies, pick)
        chosen.append((matches & (before == wanted)).astype(jnp.int32))
    total = sum(chosen[1:], chosen[0])
    ahead = (iota((tok_count, tok_count), 0) < iota((tok_count, tok_count), 1)).astype(jnp.bfloat16)
    earlier = jnp.dot(
        total.astype(jnp.bfloat16), ahead, preferred_element_type=jnp.float32
    ).astype(jnp.int32)
    weight = jnp.zeros((slot_count, tok_count), jnp.float32)
    for k in range(top_count):
        kept = (chosen[k] > 0) & (earlier < capacity)
        weight = weight + jnp.where(kept, gate_weights[pl.ds(k, 1), :], 0.0)
        earlier = earlier + chosen[k]
    terms = []
    for _ in range(3):
        terms.append(weight.astype(jnp.bfloat16).astype(jnp.float32))
        weight = weight - terms[-1]
    terms = jnp.concatenate(terms, axis=0)
    spread = (iota((3 * slot_count, 128), 0) == iota((3 * slot_count, 128), 1)).astype(jnp.float32)
    out[:, pl.ds(0, width)] = tokens[...]
    out[:, pl.ds(width, 128)] = lax.dot_general(
        terms, spread, (((0,), (0,)), ((), ())), preferred_element_type=jnp.float32
    ).astype(jnp.bfloat16)


def weight_kernel(w_in, w_out, w_in_held, w_out_held, sems):
    fetch((w_in, w_out), (w_in_held, w_out_held), sems)


def expert_kernel(slot_count, group_size, gathered, w_in, w_out, out):
    width = w_out.shape[1]
    own = lax.axis_index("expert") // group_size
    terms = gathered[:, pl.ds(width, 128)].astype(jnp.float32)
    lane = iota(terms.shape, 1)
    wanted = (lane < 3 * slot_count) & (lane % slot_count == own)
    weight = jnp.sum(jnp.where(wanted, terms, 0.0), axis=1, keepdims=True)
    rows = gathered[:, pl.ds(0, width)]
    gate = jnp.dot(rows, w_in[0], preferred_element_type=jnp.float32)
    upper = jnp.dot(rows, w_in[1], preferred_element_type=jnp.float32)
    hidden = (gate / (1.0 + jnp.exp(-gate)) * upper).astype(jnp.bfloat16)
    step = 512
    for c in range(0, width, step):
        value = jnp.dot(hidden, w_out[:, pl.ds(c, step)], preferred_element_type=jnp.float32)
        out[:, pl.ds(c, step)] = jnp.where(weight > 0.0, weight * value, 0.0).astype(jnp.bfloat16)


def call(kernel, inputs, in_specs, outs, limit, scratch=(), moved=0):
    return pl.pallas_call(
        kernel,
        out_shape=outs,
        in_specs=in_specs,
        out_specs=jax.tree.map(lambda _: VMEM, outs),
        scratch_shapes=scratch,
        compiler_params=pltpu.CompilerParams(vmem_limit_bytes=limit),
        cost_estimate=pl.CostEstimate(flops=0, bytes_accessed=moved, transcendentals=0)
        if moved
        else None,
    )(*inputs)


def body(tokens, expert_ids, gate_weights, replica_pick, placement, w_in, w_out):
    n_devices = lax.axis_size("expert")
    group_size = min(8, n_devices // 4)
    slot_count = n_devices // group_size
    tok_count, width = tokens.shape
    capacity = tok_count * expert_ids.shape[1] // slot_count
    sources = (placement, expert_ids.T, replica_pick.T, gate_weights.T, tokens)
    sources = [pltpu.with_memory_space_constraint(s, pltpu.HBM) for s in sources]
    w_in = pltpu.with_memory_space_constraint(w_in, pltpu.HBM)
    w_out = pltpu.with_memory_space_constraint(w_out, pltpu.HBM)
    marked = call(
        functools.partial(route_kernel, slot_count, capacity),
        sources,
        [HBM] * 5,
        jax.ShapeDtypeStruct((tok_count, width + 128), jnp.bfloat16),
        16 * MIB,
        [pltpu.SMEM(placement.shape, jnp.int32)]
        + [pltpu.VMEM(s.shape, s.dtype) for s in sources[1:]]
        + [pltpu.SemaphoreType.DMA((5,))],
    )
    gathered = lax.all_gather(marked, "expert", axis=0, tiled=True)
    w_in, w_out = call(
        weight_kernel,
        (w_in, w_out),
        [HBM] * 2,
        [jax.ShapeDtypeStruct(w.shape, w.dtype) for w in (w_in, w_out)],
        16 * MIB,
        [pltpu.SemaphoreType.DMA((2,))],
        2 * (w_in.size + w_out.size),
    )
    partial_value = call(
        functools.partial(expert_kernel, slot_count, group_size),
        (gathered, w_in, w_out),
        [VMEM] * 3,
        jax.ShapeDtypeStruct((gathered.shape[0], width), jnp.bfloat16),
        40 * MIB,
    )
    return lax.psum_scatter(partial_value, "expert", scatter_dimension=0, tiled=True)


def solution(mesh):
    in_specs = (
        P(("dp", "expert"), None),
        P(("dp", "expert"), None),
        P(("dp", "expert"), None),
        P(("dp", "expert"), None),
        P(),
        P(None, None, "expert"),
        P("expert", None),
    )
    out_specs = P(("dp", "expert"), None)
    return jax.shard_map(body, mesh=mesh, in_specs=in_specs, out_specs=out_specs, check_vma=False)
```

```python
import functools

import jax
import jax.numpy as jnp
from jax import lax
from jax.experimental import pallas as pl
from jax.experimental.pallas import tpu as pltpu
from jax.sharding import PartitionSpec as P

VMEM = pl.BlockSpec(memory_space=pltpu.VMEM)
HBM = pl.BlockSpec(memory_space=pltpu.HBM)
MIB = 1 << 20


def iota(shape, axis):
    return lax.broadcasted_iota(jnp.int32, shape, axis)


def stack(refs):
    return jnp.concatenate([r[...].astype(jnp.float32) for r in refs], axis=0)


def unstack(value, outs):
    start = 0
    for out in outs:
        out[...] = value[start : start + out.shape[0]].astype(out.dtype)
        start += out.shape[0]


def route_kernel(group_size, slot_count, *refs):
    sources, refs = refs[:5], refs[5:]
    row_outs, combine_out, refs = refs[:slot_count], refs[slot_count], refs[slot_count + 1 :]
    scratch, sems = refs[:5], refs[5]
    copies_in = [
        pltpu.make_async_copy(s, t, sems.at[i]) for i, (s, t) in enumerate(zip(sources, scratch))
    ]
    for c in copies_in:
        c.start()
    placement, expert_ids, replica_pick, gate_weights, tokens = scratch
    capacity = row_outs[0].shape[0]
    top_count, tok_count = expert_ids.shape
    own = lax.axis_index("expert") // group_size
    copy_row = iota((slot_count, tok_count), 0)
    named = jnp.zeros_like(copy_row)
    before = jnp.zeros_like(copy_row)
    relative = jnp.zeros_like(copy_row)
    for c in copies_in[:4]:
        c.wait()
    for p in range(slot_count):
        here = copy_row == p
        named = jnp.where(here, placement[p], named)
        relative = jnp.where(here, lax.bitwise_xor(own, p), relative)
        seen = jnp.int32(0)
        for q in range(p):
            seen = seen + (placement[q] == placement[p]).astype(jnp.int32)
        before = jnp.where(here, seen, before)
    chosen = []
    for k in range(top_count):
        matches = named == expert_ids[pl.ds(k, 1), :]
        copies = jnp.sum(matches.astype(jnp.int32), axis=0, keepdims=True)
        pick = replica_pick[pl.ds(k, 1), :]
        wanted = jnp.where(pick >= copies, pick - copies, pick)
        chosen.append((matches & (before == wanted)).astype(jnp.int32))
    total = sum(chosen[1:], chosen[0])
    ahead = (iota((tok_count, tok_count), 0) < iota((tok_count, tok_count), 1)).astype(jnp.bfloat16)
    earlier = jnp.dot(
        total.astype(jnp.bfloat16), ahead, preferred_element_type=jnp.float32
    ).astype(jnp.int32)
    slot_row = iota((slot_count * capacity, tok_count), 0)
    pick_rows = jnp.zeros((slot_count * capacity, tok_count), jnp.float32)
    combine = jnp.zeros((slot_count * capacity, tok_count), jnp.float32)
    for k in range(top_count):
        rank = jnp.sum(chosen[k] * earlier, axis=0, keepdims=True)
        place = jnp.sum(chosen[k] * relative, axis=0, keepdims=True)
        slot = jnp.where(rank < capacity, place * capacity + rank, -1)
        hot = slot_row == slot
        pick_rows = pick_rows + hot.astype(jnp.float32)
        combine = combine + jnp.where(hot, gate_weights[pl.ds(k, 1), :], 0.0)
        earlier = earlier + chosen[k]
    combine_out[...] = combine
    copies_in[4].wait()
    rows = jnp.dot(pick_rows.astype(jnp.bfloat16), tokens[...], preferred_element_type=jnp.float32)
    unstack(rows, row_outs)


def prepare_kernel(w_in, w_out, combine, w_in_held, w_out_held, terms_out, sems):
    first = pltpu.make_async_copy(w_in, w_in_held, sems.at[0])
    second = pltpu.make_async_copy(w_out, w_out_held, sems.at[1])
    first.start()
    second.start()
    rest = combine[...]
    slots = rest.shape[0]
    same = (iota((slots, slots), 0) == iota((slots, slots), 1)).astype(jnp.float32)
    terms = []
    for _ in range(3):
        term = rest.astype(jnp.bfloat16).astype(jnp.float32)
        rest = rest - term
        terms.append(
            lax.dot_general(
                term, same, (((0,), (0,)), ((), ())), preferred_element_type=jnp.float32
            )
        )
    terms_out[...] = jnp.concatenate(terms, axis=0).astype(jnp.bfloat16)
    first.wait()
    second.wait()


def stack_kernel(*refs):
    refs[-1][...] = stack(refs[:-1]).astype(jnp.bfloat16)


def expert_kernel(count, *refs):
    blocks, (w_in, w_out), outs = refs[:count], refs[count : count + 2], refs[count + 2 :]
    rows = stack(blocks).astype(jnp.bfloat16)
    gate = jnp.dot(rows, w_in[0], preferred_element_type=jnp.float32)
    upper = jnp.dot(rows, w_in[1], preferred_element_type=jnp.float32)
    hidden = (gate / (1.0 + jnp.exp(-gate)) * upper).astype(jnp.bfloat16)
    unstack(jnp.dot(hidden, w_out[...], preferred_element_type=jnp.float32), outs)


def sum_kernel(count, *refs):
    total = refs[0][...].astype(jnp.float32)
    for r in refs[1:count]:
        total = total + r[...].astype(jnp.float32)
    unstack(total, refs[count:])


def combine_kernel(terms, *refs):
    parts, out = refs[:-1], refs[-1]
    values = stack(parts).astype(jnp.bfloat16)
    product = jnp.dot(terms[...], values, preferred_element_type=jnp.float32)
    rows = out.shape[0]
    total = product[2 * rows :] + product[rows : 2 * rows] + product[:rows]
    out[...] = total.astype(jnp.bfloat16)


def call(kernel, inputs, in_specs, outs, limit, scratch=(), moved=0):
    return pl.pallas_call(
        kernel,
        out_shape=outs,
        in_specs=in_specs,
        out_specs=jax.tree.map(lambda _: VMEM, outs),
        scratch_shapes=scratch,
        compiler_params=pltpu.CompilerParams(vmem_limit_bytes=limit),
        cost_estimate=pl.CostEstimate(flops=0, bytes_accessed=moved, transcendentals=0)
        if moved
        else None,
    )(*inputs)


def body(tokens, expert_ids, gate_weights, replica_pick, placement, w_in, w_out):
    n_devices = lax.axis_size("expert")
    group_size = min(8, n_devices // 4)
    slot_count = n_devices // group_size
    tok_count, width = tokens.shape
    capacity = tok_count * expert_ids.shape[1] // slot_count
    slots = slot_count * capacity
    near, far = range(slot_count // 2), range(slot_count // 2, slot_count)
    bf16 = jnp.bfloat16
    chunk = jax.ShapeDtypeStruct((capacity, width), bf16)
    half = jax.ShapeDtypeStruct((slots // 2, width), bf16)

    def swap(value, offset):
        return lax.ppermute(value, "expert", [(e, e ^ offset) for e in range(n_devices)])

    def local(kernel, inputs, outs, limit=16 * MIB):
        return call(kernel, inputs, [VMEM] * len(inputs), outs, limit)

    def in_hbm(*arrays):
        return [pltpu.with_memory_space_constraint(a, pltpu.HBM) for a in arrays]

    sources = in_hbm(placement, expert_ids.T, replica_pick.T, gate_weights.T, tokens)
    *chunks, combine = call(
        functools.partial(route_kernel, group_size, slot_count),
        sources,
        [HBM] * 5,
        [chunk] * slot_count + [jax.ShapeDtypeStruct((slots, tok_count), jnp.float32)],
        16 * MIB,
        [pltpu.SMEM(placement.shape, jnp.int32)]
        + [pltpu.VMEM(s.shape, s.dtype) for s in sources[1:]]
        + [pltpu.SemaphoreType.DMA((5,))],
    )
    chunks = [c if d == 0 else swap(c, d * group_size) for d, c in enumerate(chunks)]
    w_in, w_out, terms = call(
        prepare_kernel,
        (*in_hbm(w_in, w_out), combine),
        [HBM] * 2 + [VMEM],
        [
            jax.ShapeDtypeStruct(w_in.shape, bf16),
            jax.ShapeDtypeStruct(w_out.shape, bf16),
            jax.ShapeDtypeStruct((3 * tok_count, slots), bf16),
        ],
        16 * MIB,
        [pltpu.SemaphoreType.DMA((2,))],
        2 * (w_in.size + w_out.size),
    )

    own = [local(stack_kernel, [chunks[d] for d in part], half) for part in (near, far)]
    held = [own] + [[None, None] for _ in range(1, group_size)]
    square = group_size == 4
    for h in range(2):
        for q in (1, 2) if square else range(1, group_size):
            held[q][h] = swap(own[h], q)
    if square:
        held[3] = [swap(held[1][0], 2), swap(held[2][1], 1)]

    result = local(
        functools.partial(expert_kernel, 2 * group_size),
        [held[q][h] for h in range(2) for q in range(group_size)] + [w_in, w_out],
        [half] * (2 * group_size),
        40 * MIB,
    )
    near_sent, far_sent = result[:group_size], result[group_size:]
    if square:
        far_cross, near_cross = swap(far_sent[3], 1), swap(near_sent[3], 2)
        far_terms = [
            far_sent[0],
            swap(far_sent[1], 1),
            swap(local(functools.partial(sum_kernel, 2), [far_sent[2], far_cross], [half])[0], 2),
        ]
        near_terms = [
            near_sent[0],
            swap(near_sent[2], 2),
            swap(local(functools.partial(sum_kernel, 2), [near_sent[1], near_cross], [half])[0], 1),
        ]
    else:
        far_terms = [v if q == 0 else swap(v, q) for q, v in enumerate(far_sent)]
        near_terms = [v if q == 0 else swap(v, q) for q, v in enumerate(near_sent)]
    summed = [
        local(functools.partial(sum_kernel, len(t)), t, [chunk] * (slot_count // 2))
        for t in (near_terms, far_terms)
    ]
    returned = [
        v if d == 0 else swap(v, d * group_size) for d, v in enumerate(summed[0] + summed[1])
    ]
    return local(
        combine_kernel, [terms] + returned, jax.ShapeDtypeStruct((tok_count, width), bf16)
    )


def solution(mesh):
    in_specs = (
        P(("dp", "expert"), None),
        P(("dp", "expert"), None),
        P(("dp", "expert"), None),
        P(("dp", "expert"), None),
        P(),
        P(None, None, "expert"),
        P("expert", None),
    )
    out_specs = P(("dp", "expert"), None)
    return jax.shard_map(body, mesh=mesh, in_specs=in_specs, out_specs=out_specs, check_vma=False)
```

```python
import functools

import jax
import jax.numpy as jnp
from jax import lax
from jax.experimental import pallas as pl
from jax.experimental.pallas import tpu as pltpu
from jax.sharding import PartitionSpec as P

VMEM = pl.BlockSpec(memory_space=pltpu.VMEM)
HBM = pl.BlockSpec(memory_space=pltpu.HBM)
MIB = 1 << 20


def iota(shape, axis):
    return lax.broadcasted_iota(jnp.int32, shape, axis)


def stack(refs):
    return jnp.concatenate([r[...].astype(jnp.float32) for r in refs], axis=0)


def unstack(value, outs):
    start = 0
    for out in outs:
        out[...] = value[start : start + out.shape[0]].astype(out.dtype)
        start += out.shape[0]


def route_kernel(group_size, slot_count, *refs):
    sources, refs = refs[:5], refs[5:]
    row_outs, combine_out, refs = refs[:slot_count], refs[slot_count], refs[slot_count + 1 :]
    scratch, sems = refs[:5], refs[5]
    copies_in = [
        pltpu.make_async_copy(s, t, sems.at[i]) for i, (s, t) in enumerate(zip(sources, scratch))
    ]
    for c in copies_in:
        c.start()
    placement, expert_ids, replica_pick, gate_weights, tokens = scratch
    capacity = row_outs[0].shape[0]
    top_count, tok_count = expert_ids.shape
    own = lax.axis_index("expert") // group_size
    copy_row = iota((slot_count, tok_count), 0)
    named = jnp.zeros_like(copy_row)
    before = jnp.zeros_like(copy_row)
    relative = jnp.zeros_like(copy_row)
    for c in copies_in[:4]:
        c.wait()
    for p in range(slot_count):
        here = copy_row == p
        named = jnp.where(here, placement[p], named)
        relative = jnp.where(here, lax.bitwise_xor(own, p), relative)
        seen = jnp.int32(0)
        for q in range(p):
            seen = seen + (placement[q] == placement[p]).astype(jnp.int32)
        before = jnp.where(here, seen, before)
    chosen = []
    for k in range(top_count):
        matches = named == expert_ids[pl.ds(k, 1), :]
        copies = jnp.sum(matches.astype(jnp.int32), axis=0, keepdims=True)
        pick = replica_pick[pl.ds(k, 1), :]
        wanted = jnp.where(pick >= copies, pick - copies, pick)
        chosen.append((matches & (before == wanted)).astype(jnp.int32))
    total = sum(chosen[1:], chosen[0])
    ahead = (iota((tok_count, tok_count), 0) < iota((tok_count, tok_count), 1)).astype(jnp.bfloat16)
    earlier = jnp.dot(
        total.astype(jnp.bfloat16), ahead, preferred_element_type=jnp.float32
    ).astype(jnp.int32)
    slot_row = iota((slot_count * capacity, tok_count), 0)
    pick_rows = jnp.zeros((slot_count * capacity, tok_count), jnp.float32)
    combine = jnp.zeros((slot_count * capacity, tok_count), jnp.float32)
    for k in range(top_count):
        rank = jnp.sum(chosen[k] * earlier, axis=0, keepdims=True)
        place = jnp.sum(chosen[k] * relative, axis=0, keepdims=True)
        slot = jnp.where(rank < capacity, place * capacity + rank, -1)
        hot = slot_row == slot
        pick_rows = pick_rows + hot.astype(jnp.float32)
        combine = combine + jnp.where(hot, gate_weights[pl.ds(k, 1), :], 0.0)
        earlier = earlier + chosen[k]
    combine_out[...] = combine
    copies_in[4].wait()
    rows = jnp.dot(pick_rows.astype(jnp.bfloat16), tokens[...], preferred_element_type=jnp.float32)
    unstack(rows, row_outs)


def prepare_kernel(w_in, w_out, combine, w_in_held, w_out_held, terms_out, sems):
    first = pltpu.make_async_copy(w_in, w_in_held, sems.at[0])
    second = pltpu.make_async_copy(w_out, w_out_held, sems.at[1])
    first.start()
    second.start()
    rest = combine[...]
    slots = rest.shape[0]
    same = (iota((slots, slots), 0) == iota((slots, slots), 1)).astype(jnp.float32)
    terms = []
    for _ in range(3):
        term = rest.astype(jnp.bfloat16).astype(jnp.float32)
        rest = rest - term
        terms.append(
            lax.dot_general(
                term, same, (((0,), (0,)), ((), ())), preferred_element_type=jnp.float32
            )
        )
    terms_out[...] = jnp.concatenate(terms, axis=0).astype(jnp.bfloat16)
    first.wait()
    second.wait()


def stack_kernel(count, *refs):
    refs[-1][...] = stack(refs[:count]).astype(jnp.bfloat16)


def expert_kernel(count, *refs):
    blocks, (w_in, w_out), outs = refs[:count], refs[count : count + 2], refs[count + 2 :]
    rows = stack(blocks).astype(jnp.bfloat16)
    gate = jnp.dot(rows, w_in[0], preferred_element_type=jnp.float32)
    upper = jnp.dot(rows, w_in[1], preferred_element_type=jnp.float32)
    hidden = (gate / (1.0 + jnp.exp(-gate)) * upper).astype(jnp.bfloat16)
    unstack(jnp.dot(hidden, w_out[...], preferred_element_type=jnp.float32), outs)


def sum_kernel(count, *refs):
    total = refs[0][...].astype(jnp.float32)
    for r in refs[1:count]:
        total = total + r[...].astype(jnp.float32)
    unstack(total, refs[count:])


def combine_kernel(terms, *refs):
    parts, out = refs[:-1], refs[-1]
    values = stack(parts).astype(jnp.bfloat16)
    product = jnp.dot(terms[...], values, preferred_element_type=jnp.float32)
    rows = out.shape[0]
    total = product[2 * rows :] + product[rows : 2 * rows] + product[:rows]
    out[...] = total.astype(jnp.bfloat16)


def call(kernel, inputs, in_specs, outs, limit, scratch=(), moved=0):
    return pl.pallas_call(
        kernel,
        out_shape=outs,
        in_specs=in_specs,
        out_specs=jax.tree.map(lambda _: VMEM, outs),
        scratch_shapes=scratch,
        compiler_params=pltpu.CompilerParams(vmem_limit_bytes=limit),
        cost_estimate=pl.CostEstimate(flops=0, bytes_accessed=moved, transcendentals=0)
        if moved
        else None,
    )(*inputs)


def body(tokens, expert_ids, gate_weights, replica_pick, placement, w_in, w_out):
    n_devices = lax.axis_size("expert")
    group_size = min(8, n_devices // 4)
    slot_count = n_devices // group_size
    tok_count, width = tokens.shape
    capacity = tok_count * expert_ids.shape[1] // slot_count
    slots = slot_count * capacity
    bf16 = jnp.bfloat16
    chunk = jax.ShapeDtypeStruct((capacity, width), bf16)
    block = jax.ShapeDtypeStruct((slots, width), bf16)

    def swap(value, offset):
        return lax.ppermute(value, "expert", [(e, e ^ offset) for e in range(n_devices)])

    def local(kernel, inputs, outs, limit=16 * MIB):
        return call(kernel, inputs, [VMEM] * len(inputs), outs, limit)

    def in_hbm(*arrays):
        return [pltpu.with_memory_space_constraint(a, pltpu.HBM) for a in arrays]

    sources = in_hbm(placement, expert_ids.T, replica_pick.T, gate_weights.T, tokens)
    *chunks, combine = call(
        functools.partial(route_kernel, group_size, slot_count),
        sources,
        [HBM] * 5,
        [chunk] * slot_count + [jax.ShapeDtypeStruct((slots, tok_count), jnp.float32)],
        16 * MIB,
        [pltpu.SMEM(placement.shape, jnp.int32)]
        + [pltpu.VMEM(s.shape, s.dtype) for s in sources[1:]]
        + [pltpu.SemaphoreType.DMA((5,))],
    )
    chunks = [c if d == 0 else swap(c, d * group_size) for d, c in enumerate(chunks)]
    w_in, w_out, terms = call(
        prepare_kernel,
        (*in_hbm(w_in, w_out), combine),
        [HBM] * 2 + [VMEM],
        [
            jax.ShapeDtypeStruct(w_in.shape, bf16),
            jax.ShapeDtypeStruct(w_out.shape, bf16),
            jax.ShapeDtypeStruct((3 * tok_count, slots), bf16),
        ],
        16 * MIB,
        [pltpu.SemaphoreType.DMA((2,))],
        2 * (w_in.size + w_out.size),
    )
    own = local(functools.partial(stack_kernel, slot_count), chunks + [terms], block)
    held = [own if q == 0 else swap(own, q) for q in range(group_size)]
    result = local(
        functools.partial(expert_kernel, group_size),
        held + [w_in, w_out],
        [block] * group_size,
        40 * MIB,
    )
    result = [v if q == 0 else swap(v, q) for q, v in enumerate(result)]
    summed = local(functools.partial(sum_kernel, group_size), result, [chunk] * slot_count)
    returned = [v if d == 0 else swap(v, d * group_size) for d, v in enumerate(summed)]
    return local(
        combine_kernel, [terms] + returned, jax.ShapeDtypeStruct((tok_count, width), bf16)
    )


def solution(mesh):
    in_specs = (
        P(("dp", "expert"), None),
        P(("dp", "expert"), None),
        P(("dp", "expert"), None),
        P(("dp", "expert"), None),
        P(),
        P(None, None, "expert"),
        P("expert", None),
    )
    out_specs = P(("dp", "expert"), None)
    return jax.shard_map(body, mesh=mesh, in_specs=in_specs, out_specs=out_specs, check_vma=False)
```

```python
import functools

import jax
import jax.numpy as jnp
from jax import lax
from jax.experimental import pallas as pl
from jax.experimental.pallas import tpu as pltpu
from jax.sharding import PartitionSpec as P

VMEM = pl.BlockSpec(memory_space=pltpu.VMEM)
HBM = pl.BlockSpec(memory_space=pltpu.HBM)
MIB = 1 << 20


def iota(shape, axis):
    return lax.broadcasted_iota(jnp.int32, shape, axis)


def stack(refs):
    return jnp.concatenate([r[...].astype(jnp.float32) for r in refs], axis=0)


def unstack(value, outs):
    start = 0
    for out in outs:
        out[...] = value[start : start + out.shape[0]].astype(out.dtype)
        start += out.shape[0]


def route_kernel(group_size, slot_count, *refs):
    sources, refs = refs[:5], refs[5:]
    row_outs, combine_out, refs = refs[:slot_count], refs[slot_count], refs[slot_count + 1 :]
    scratch, sems = refs[:5], refs[5]
    copies_in = [
        pltpu.make_async_copy(s, t, sems.at[i]) for i, (s, t) in enumerate(zip(sources, scratch))
    ]
    for c in copies_in:
        c.start()
    placement, expert_ids, replica_pick, gate_weights, tokens = scratch
    capacity = row_outs[0].shape[0]
    top_count, tok_count = expert_ids.shape
    own = lax.axis_index("expert") // group_size
    copy_row = iota((slot_count, tok_count), 0)
    named = jnp.zeros_like(copy_row)
    before = jnp.zeros_like(copy_row)
    relative = jnp.zeros_like(copy_row)
    for c in copies_in[:4]:
        c.wait()
    for p in range(slot_count):
        here = copy_row == p
        named = jnp.where(here, placement[p], named)
        relative = jnp.where(here, lax.bitwise_xor(own, p), relative)
        seen = jnp.int32(0)
        for q in range(p):
            seen = seen + (placement[q] == placement[p]).astype(jnp.int32)
        before = jnp.where(here, seen, before)
    chosen = []
    for k in range(top_count):
        matches = named == expert_ids[pl.ds(k, 1), :]
        copies = jnp.sum(matches.astype(jnp.int32), axis=0, keepdims=True)
        pick = replica_pick[pl.ds(k, 1), :]
        wanted = jnp.where(pick >= copies, pick - copies, pick)
        chosen.append((matches & (before == wanted)).astype(jnp.int32))
    total = sum(chosen[1:], chosen[0])
    ahead = (iota((tok_count, tok_count), 0) < iota((tok_count, tok_count), 1)).astype(jnp.bfloat16)
    earlier = jnp.dot(
        total.astype(jnp.bfloat16), ahead, preferred_element_type=jnp.float32
    ).astype(jnp.int32)
    slot_row = iota((slot_count * capacity, tok_count), 0)
    pick_rows = jnp.zeros((slot_count * capacity, tok_count), jnp.float32)
    combine = jnp.zeros((slot_count * capacity, tok_count), jnp.float32)
    for k in range(top_count):
        rank = jnp.sum(chosen[k] * earlier, axis=0, keepdims=True)
        place = jnp.sum(chosen[k] * relative, axis=0, keepdims=True)
        slot = jnp.where(rank < capacity, place * capacity + rank, -1)
        hot = slot_row == slot
        pick_rows = pick_rows + hot.astype(jnp.float32)
        combine = combine + jnp.where(hot, gate_weights[pl.ds(k, 1), :], 0.0)
        earlier = earlier + chosen[k]
    combine_out[...] = combine
    copies_in[4].wait()
    rows = jnp.dot(pick_rows.astype(jnp.bfloat16), tokens[...], preferred_element_type=jnp.float32)
    unstack(rows, row_outs)


def prepare_kernel(w_in, w_out, combine, w_in_held, w_out_held, terms_out, sems):
    half = w_in.shape[1] // 2
    rows = [pl.ds(0, half), pl.ds(half, half)]
    copies = [
        pltpu.make_async_copy(w_in.at[i, r], w_in_held.at[i, r], sems.at[2 * i + j])
        for i in range(2)
        for j, r in enumerate(rows)
    ] + [pltpu.make_async_copy(w_out, w_out_held, sems.at[4])]
    for c in copies:
        c.start()
    rest = combine[...]
    slots = rest.shape[0]
    same = (iota((slots, slots), 0) == iota((slots, slots), 1)).astype(jnp.float32)
    terms = []
    for _ in range(3):
        term = rest.astype(jnp.bfloat16).astype(jnp.float32)
        rest = rest - term
        terms.append(
            lax.dot_general(
                term, same, (((0,), (0,)), ((), ())), preferred_element_type=jnp.float32
            )
        )
    terms_out[...] = jnp.concatenate(terms, axis=0).astype(jnp.bfloat16)
    for c in copies:
        c.wait()


def stack_kernel(count, *refs):
    refs[-1][...] = stack(refs[:count]).astype(jnp.bfloat16)


def expert_kernel(count, *refs):
    blocks, (w_in, w_out), outs = refs[:count], refs[count : count + 2], refs[count + 2 :]
    rows = stack(blocks).astype(jnp.bfloat16)
    gate = jnp.dot(rows, w_in[0], preferred_element_type=jnp.float32)
    upper = jnp.dot(rows, w_in[1], preferred_element_type=jnp.float32)
    hidden = (gate / (1.0 + jnp.exp(-gate)) * upper).astype(jnp.bfloat16)
    unstack(jnp.dot(hidden, w_out[...], preferred_element_type=jnp.float32), outs)


def sum_kernel(count, *refs):
    total = refs[0][...].astype(jnp.float32)
    for r in refs[1:count]:
        total = total + r[...].astype(jnp.float32)
    unstack(total, refs[count:])


def combine_kernel(terms, *refs):
    parts, out = refs[:-1], refs[-1]
    values = stack(parts).astype(jnp.bfloat16)
    product = jnp.dot(terms[...], values, preferred_element_type=jnp.float32)
    rows = out.shape[0]
    total = product[2 * rows :] + product[rows : 2 * rows] + product[:rows]
    out[...] = total.astype(jnp.bfloat16)


def call(kernel, inputs, in_specs, outs, limit, scratch=(), moved=0):
    return pl.pallas_call(
        kernel,
        out_shape=outs,
        in_specs=in_specs,
        out_specs=jax.tree.map(lambda _: VMEM, outs),
        scratch_shapes=scratch,
        compiler_params=pltpu.CompilerParams(vmem_limit_bytes=limit),
        cost_estimate=pl.CostEstimate(flops=0, bytes_accessed=moved, transcendentals=0)
        if moved
        else None,
    )(*inputs)


def body(tokens, expert_ids, gate_weights, replica_pick, placement, w_in, w_out):
    n_devices = lax.axis_size("expert")
    group_size = min(8, n_devices // 4)
    slot_count = n_devices // group_size
    tok_count, width = tokens.shape
    capacity = tok_count * expert_ids.shape[1] // slot_count
    slots = slot_count * capacity
    square = group_size == 4
    bf16 = jnp.bfloat16
    chunk = jax.ShapeDtypeStruct((capacity, width), bf16)
    block = jax.ShapeDtypeStruct((slots, width), bf16)

    def swap(value, offset):
        return lax.ppermute(value, "expert", [(e, e ^ offset) for e in range(n_devices)])

    def turn(value, even, odd):
        parts = lax.axis_size("dp")
        pairs = [
            (e * parts + part, (e ^ (odd if part % 2 else even)) * parts + part)
            for e in range(n_devices)
            for part in range(parts)
        ]
        return lax.ppermute(value, ("expert", "dp"), pairs)

    def local(kernel, inputs, outs, limit=16 * MIB):
        return call(kernel, inputs, [VMEM] * len(inputs), outs, limit)

    def in_hbm(*arrays):
        return [pltpu.with_memory_space_constraint(a, pltpu.HBM) for a in arrays]

    sources = in_hbm(placement, expert_ids.T, replica_pick.T, gate_weights.T, tokens)
    *chunks, combine = call(
        functools.partial(route_kernel, group_size, slot_count),
        sources,
        [HBM] * 5,
        [chunk] * slot_count + [jax.ShapeDtypeStruct((slots, tok_count), jnp.float32)],
        16 * MIB,
        [pltpu.SMEM(placement.shape, jnp.int32)]
        + [pltpu.VMEM(s.shape, s.dtype) for s in sources[1:]]
        + [pltpu.SemaphoreType.DMA((5,))],
    )
    chunks = [c if d == 0 else swap(c, d * group_size) for d, c in enumerate(chunks)]
    w_in, w_out, terms = call(
        prepare_kernel,
        (*in_hbm(w_in, w_out), combine),
        [HBM] * 2 + [VMEM],
        [
            jax.ShapeDtypeStruct(w_in.shape, bf16),
            jax.ShapeDtypeStruct(w_out.shape, bf16),
            jax.ShapeDtypeStruct((3 * tok_count, slots), bf16),
        ],
        16 * MIB,
        [pltpu.SemaphoreType.DMA((5,))],
        2 * (w_in.size + w_out.size),
    )
    own = local(functools.partial(stack_kernel, slot_count), chunks + [terms], block)
    if square:
        first, second = turn(own, 1, 2), turn(own, 2, 1)
        held = [own, first, second, turn(first, 2, 1)]
    else:
        held = [own if q == 0 else swap(own, q) for q in range(group_size)]
    result = local(
        functools.partial(expert_kernel, group_size),
        held + [w_in, w_out],
        [block] * group_size,
        40 * MIB,
    )
    if square:
        mine, first, second, cross = result
        cross = turn(cross, 1, 2)
        first = turn(first, 1, 2)
        second = local(functools.partial(sum_kernel, 2), [second, cross], [block])[0]
        result = [mine, first, turn(second, 2, 1)]
    else:
        result = [v if q == 0 else swap(v, q) for q, v in enumerate(result)]
    summed = local(functools.partial(sum_kernel, len(result)), result, [chunk] * slot_count)
    returned = [v if d == 0 else swap(v, d * group_size) for d, v in enumerate(summed)]
    return local(
        combine_kernel, [terms] + returned, jax.ShapeDtypeStruct((tok_count, width), bf16)
    )


def solution(mesh):
    in_specs = (
        P(("dp", "expert"), None),
        P(("dp", "expert"), None),
        P(("dp", "expert"), None),
        P(("dp", "expert"), None),
        P(),
        P(None, None, "expert"),
        P("expert", None),
    )
    out_specs = P(("dp", "expert"), None)
    return jax.shard_map(body, mesh=mesh, in_specs=in_specs, out_specs=out_specs, check_vma=False)
```

```python
import functools

import jax
import jax.numpy as jnp
from jax import lax
from jax.experimental import pallas as pl
from jax.experimental.pallas import tpu as pltpu
from jax.sharding import PartitionSpec as P

VMEM = pl.BlockSpec(memory_space=pltpu.VMEM)
HBM = pl.BlockSpec(memory_space=pltpu.HBM)
MIB = 1 << 20


def iota(shape, axis):
    return lax.broadcasted_iota(jnp.int32, shape, axis)


def stack(refs):
    return jnp.concatenate([r[...].astype(jnp.float32) for r in refs], axis=0)


def unstack(value, outs):
    start = 0
    for out in outs:
        out[...] = value[start : start + out.shape[0]].astype(out.dtype)
        start += out.shape[0]


def route_kernel(group_size, slot_count, *refs):
    sources, refs = refs[:5], refs[5:]
    row_outs, combine_out, refs = refs[:slot_count], refs[slot_count], refs[slot_count + 1 :]
    scratch, sems = refs[:5], refs[5]
    copies_in = [
        pltpu.make_async_copy(s, t, sems.at[i]) for i, (s, t) in enumerate(zip(sources, scratch))
    ]
    for c in copies_in:
        c.start()
    placement, expert_ids, replica_pick, gate_weights, tokens = scratch
    capacity = row_outs[0].shape[0]
    top_count, tok_count = expert_ids.shape
    own = lax.axis_index("expert") // group_size
    copy_row = iota((slot_count, tok_count), 0)
    named = jnp.zeros_like(copy_row)
    before = jnp.zeros_like(copy_row)
    relative = jnp.zeros_like(copy_row)
    for c in copies_in[:4]:
        c.wait()
    for p in range(slot_count):
        here = copy_row == p
        named = jnp.where(here, placement[p], named)
        relative = jnp.where(here, lax.bitwise_xor(own, p), relative)
        seen = jnp.int32(0)
        for q in range(p):
            seen = seen + (placement[q] == placement[p]).astype(jnp.int32)
        before = jnp.where(here, seen, before)
    chosen = []
    for k in range(top_count):
        matches = named == expert_ids[pl.ds(k, 1), :]
        copies = jnp.sum(matches.astype(jnp.int32), axis=0, keepdims=True)
        pick = replica_pick[pl.ds(k, 1), :]
        wanted = jnp.where(pick >= copies, pick - copies, pick)
        chosen.append((matches & (before == wanted)).astype(jnp.int32))
    total = sum(chosen[1:], chosen[0])
    ahead = (iota((tok_count, tok_count), 0) < iota((tok_count, tok_count), 1)).astype(jnp.bfloat16)
    earlier = jnp.dot(
        total.astype(jnp.bfloat16), ahead, preferred_element_type=jnp.float32
    ).astype(jnp.int32)
    slot_row = iota((slot_count * capacity, tok_count), 0)
    pick_rows = jnp.zeros((slot_count * capacity, tok_count), jnp.float32)
    combine = jnp.zeros((slot_count * capacity, tok_count), jnp.float32)
    for k in range(top_count):
        rank = jnp.sum(chosen[k] * earlier, axis=0, keepdims=True)
        place = jnp.sum(chosen[k] * relative, axis=0, keepdims=True)
        slot = jnp.where(rank < capacity, place * capacity + rank, -1)
        hot = slot_row == slot
        pick_rows = pick_rows + hot.astype(jnp.float32)
        combine = combine + jnp.where(hot, gate_weights[pl.ds(k, 1), :], 0.0)
        earlier = earlier + chosen[k]
    combine_out[...] = combine
    copies_in[4].wait()
    rows = jnp.dot(pick_rows.astype(jnp.bfloat16), tokens[...], preferred_element_type=jnp.float32)
    unstack(rows, row_outs)


def prepare_kernel(w_in, w_out, combine, w_in_held, w_out_held, terms_out, sems):
    half = w_in.shape[1] // 2
    rows = [pl.ds(0, half), pl.ds(half, half)]
    copies = [
        pltpu.make_async_copy(w_in.at[i, r], w_in_held.at[i, r], sems.at[2 * i + j])
        for i in range(2)
        for j, r in enumerate(rows)
    ] + [pltpu.make_async_copy(w_out, w_out_held, sems.at[4])]
    for c in copies:
        c.start()
    rest = combine[...]
    slots = rest.shape[0]
    same = (iota((slots, slots), 0) == iota((slots, slots), 1)).astype(jnp.float32)
    terms = []
    for _ in range(3):
        term = rest.astype(jnp.bfloat16).astype(jnp.float32)
        rest = rest - term
        terms.append(
            lax.dot_general(
                term, same, (((0,), (0,)), ((), ())), preferred_element_type=jnp.float32
            )
        )
    terms_out[...] = jnp.concatenate(terms, axis=0).astype(jnp.bfloat16)
    for c in copies:
        c.wait()


def stack_kernel(count, *refs):
    value, out = stack(refs[:count]).astype(jnp.bfloat16), refs[-1]
    rows = value.shape[0]
    for start in range(0, out.shape[0], rows):
        out[pl.ds(start, rows), :] = value


def expert_kernel(rows, w_in, w_out, out):
    gate = jnp.dot(rows[...], w_in[0], preferred_element_type=jnp.float32)
    upper = jnp.dot(rows[...], w_in[1], preferred_element_type=jnp.float32)
    hidden = (gate / (1.0 + jnp.exp(-gate)) * upper).astype(jnp.bfloat16)
    out[...] = jnp.dot(hidden, w_out[...], preferred_element_type=jnp.float32).astype(jnp.bfloat16)


def sum_kernel(values, *outs):
    rows = len(outs) * outs[0].shape[0]
    total = values[pl.ds(0, rows), :].astype(jnp.float32)
    for start in range(rows, values.shape[0], rows):
        total = total + values[pl.ds(start, rows), :].astype(jnp.float32)
    unstack(total, outs)


def combine_kernel(terms, *refs):
    parts, out = refs[:-1], refs[-1]
    values = stack(parts).astype(jnp.bfloat16)
    product = jnp.dot(terms[...], values, preferred_element_type=jnp.float32)
    rows = out.shape[0]
    total = product[2 * rows :] + product[rows : 2 * rows] + product[:rows]
    out[...] = total.astype(jnp.bfloat16)


def call(kernel, inputs, in_specs, outs, limit, scratch=(), moved=0):
    return pl.pallas_call(
        kernel,
        out_shape=outs,
        in_specs=in_specs,
        out_specs=jax.tree.map(lambda _: VMEM, outs),
        scratch_shapes=scratch,
        compiler_params=pltpu.CompilerParams(vmem_limit_bytes=limit),
        cost_estimate=pl.CostEstimate(flops=0, bytes_accessed=moved, transcendentals=0)
        if moved
        else None,
    )(*inputs)


def body(tokens, expert_ids, gate_weights, replica_pick, placement, w_in, w_out):
    n_devices = lax.axis_size("expert")
    group_size = min(8, n_devices // 4)
    slot_count = n_devices // group_size
    tok_count, width = tokens.shape
    capacity = tok_count * expert_ids.shape[1] // slot_count
    slots = slot_count * capacity
    bf16 = jnp.bfloat16
    chunk = jax.ShapeDtypeStruct((capacity, width), bf16)

    def swap(value, offset):
        return lax.ppermute(value, "expert", [(e, e ^ offset) for e in range(n_devices)])

    def exchange(value):
        groups = [list(range(e, e + group_size)) for e in range(0, n_devices, group_size)]
        return lax.all_to_all(value, "expert", 0, 0, axis_index_groups=groups, tiled=True)

    def local(kernel, inputs, outs, limit=16 * MIB):
        return call(kernel, inputs, [VMEM] * len(inputs), outs, limit)

    def in_hbm(*arrays):
        return [pltpu.with_memory_space_constraint(a, pltpu.HBM) for a in arrays]

    sources = in_hbm(placement, expert_ids.T, replica_pick.T, gate_weights.T, tokens)
    *chunks, combine = call(
        functools.partial(route_kernel, group_size, slot_count),
        sources,
        [HBM] * 5,
        [chunk] * slot_count + [jax.ShapeDtypeStruct((slots, tok_count), jnp.float32)],
        16 * MIB,
        [pltpu.SMEM(placement.shape, jnp.int32)]
        + [pltpu.VMEM(s.shape, s.dtype) for s in sources[1:]]
        + [pltpu.SemaphoreType.DMA((5,))],
    )
    chunks = [c if d == 0 else swap(c, d * group_size) for d, c in enumerate(chunks)]
    w_in, w_out, terms = call(
        prepare_kernel,
        (*in_hbm(w_in, w_out), combine),
        [HBM] * 2 + [VMEM],
        [
            jax.ShapeDtypeStruct(w_in.shape, bf16),
            jax.ShapeDtypeStruct(w_out.shape, bf16),
            jax.ShapeDtypeStruct((3 * tok_count, slots), bf16),
        ],
        16 * MIB,
        [pltpu.SemaphoreType.DMA((5,))],
        2 * (w_in.size + w_out.size),
    )
    everyone = jax.ShapeDtypeStruct((group_size * slots, width), bf16)
    own = local(functools.partial(stack_kernel, slot_count), chunks + [terms], everyone)
    result = local(expert_kernel, [exchange(own), w_in, w_out], everyone, 40 * MIB)
    summed = local(sum_kernel, [exchange(result)], [chunk] * slot_count)
    returned = [v if d == 0 else swap(v, d * group_size) for d, v in enumerate(summed)]
    return local(
        combine_kernel, [terms] + returned, jax.ShapeDtypeStruct((tok_count, width), bf16)
    )


def solution(mesh):
    in_specs = (
        P(("dp", "expert"), None),
        P(("dp", "expert"), None),
        P(("dp", "expert"), None),
        P(("dp", "expert"), None),
        P(),
        P(None, None, "expert"),
        P("expert", None),
    )
    out_specs = P(("dp", "expert"), None)
    return jax.shard_map(body, mesh=mesh, in_specs=in_specs, out_specs=out_specs, check_vma=False)
```

```python
import functools

import jax
import jax.numpy as jnp
from jax import lax
from jax.experimental import pallas as pl
from jax.experimental.pallas import tpu as pltpu
from jax.sharding import PartitionSpec as P

VMEM = pl.BlockSpec(memory_space=pltpu.VMEM)
HBM = pl.BlockSpec(memory_space=pltpu.HBM)
MIB = 1 << 20


def iota(shape, axis):
    return lax.broadcasted_iota(jnp.int32, shape, axis)


def stack(refs):
    return jnp.concatenate([r[...].astype(jnp.float32) for r in refs], axis=0)


def unstack(value, outs):
    start = 0
    for out in outs:
        out[...] = value[start : start + out.shape[0]].astype(out.dtype)
        start += out.shape[0]


def route_kernel(group_size, slot_count, *refs):
    sources, refs = refs[:5], refs[5:]
    row_outs, combine_out, refs = refs[:slot_count], refs[slot_count], refs[slot_count + 1 :]
    scratch, sems = refs[:5], refs[5]
    copies_in = [
        pltpu.make_async_copy(s, t, sems.at[i]) for i, (s, t) in enumerate(zip(sources, scratch))
    ]
    for c in copies_in:
        c.start()
    placement, expert_ids, replica_pick, gate_weights, tokens = scratch
    capacity = row_outs[0].shape[0]
    top_count, tok_count = expert_ids.shape
    own = lax.axis_index("expert") // group_size
    copy_row = iota((slot_count, tok_count), 0)
    named = jnp.zeros_like(copy_row)
    before = jnp.zeros_like(copy_row)
    relative = jnp.zeros_like(copy_row)
    for c in copies_in[:4]:
        c.wait()
    for p in range(slot_count):
        here = copy_row == p
        named = jnp.where(here, placement[p], named)
        d = lax.bitwise_xor(own, p)
        relative = jnp.where(here, d // 2 + d % 2 * (slot_count // 2), relative)
        seen = jnp.int32(0)
        for q in range(p):
            seen = seen + (placement[q] == placement[p]).astype(jnp.int32)
        before = jnp.where(here, seen, before)
    chosen = []
    for k in range(top_count):
        matches = named == expert_ids[pl.ds(k, 1), :]
        copies = jnp.sum(matches.astype(jnp.int32), axis=0, keepdims=True)
        pick = replica_pick[pl.ds(k, 1), :]
        wanted = jnp.where(pick >= copies, pick - copies, pick)
        chosen.append((matches & (before == wanted)).astype(jnp.int32))
    total = sum(chosen[1:], chosen[0])
    ahead = (iota((tok_count, tok_count), 0) < iota((tok_count, tok_count), 1)).astype(jnp.bfloat16)
    earlier = jnp.dot(
        total.astype(jnp.bfloat16), ahead, preferred_element_type=jnp.float32
    ).astype(jnp.int32)
    slot_row = iota((slot_count * capacity, tok_count), 0)
    pick_rows = jnp.zeros((slot_count * capacity, tok_count), jnp.float32)
    combine = jnp.zeros((slot_count * capacity, tok_count), jnp.float32)
    for k in range(top_count):
        rank = jnp.sum(chosen[k] * earlier, axis=0, keepdims=True)
        place = jnp.sum(chosen[k] * relative, axis=0, keepdims=True)
        slot = jnp.where(rank < capacity, place * capacity + rank, -1)
        hot = slot_row == slot
        pick_rows = pick_rows + hot.astype(jnp.float32)
        combine = combine + jnp.where(hot, gate_weights[pl.ds(k, 1), :], 0.0)
        earlier = earlier + chosen[k]
    combine_out[...] = combine
    copies_in[4].wait()
    rows = jnp.dot(pick_rows.astype(jnp.bfloat16), tokens[...], preferred_element_type=jnp.float32)
    unstack(rows, row_outs)


def prepare_kernel(w_in, w_out, combine, w_in_held, w_out_held, near_terms, far_terms, sems):
    half = w_in.shape[1] // 2
    rows = [pl.ds(0, half), pl.ds(half, half)]
    copies = [
        pltpu.make_async_copy(w_in.at[i, r], w_in_held.at[i, r], sems.at[2 * i + j])
        for i in range(2)
        for j, r in enumerate(rows)
    ] + [pltpu.make_async_copy(w_out, w_out_held, sems.at[4])]
    for c in copies:
        c.start()
    slots = combine.shape[0] // 2
    same = (iota((slots, slots), 0) == iota((slots, slots), 1)).astype(jnp.float32)
    for start, out in ((0, near_terms), (slots, far_terms)):
        rest = combine[pl.ds(start, slots), :]
        terms = []
        for _ in range(3):
            term = rest.astype(jnp.bfloat16).astype(jnp.float32)
            rest = rest - term
            terms.append(
                lax.dot_general(
                    term, same, (((0,), (0,)), ((), ())), preferred_element_type=jnp.float32
                )
            )
        out[...] = jnp.concatenate(terms, axis=0).astype(jnp.bfloat16)
    for c in copies:
        c.wait()


def stack_kernel(count, *refs):
    refs[-1][...] = stack(refs[:count]).astype(jnp.bfloat16)


def expert_kernel(count, *refs):
    blocks, (w_in, w_out), outs = refs[:count], refs[count : count + 2], refs[count + 2 :]
    rows = stack(blocks).astype(jnp.bfloat16)
    gate = jnp.dot(rows, w_in[0], preferred_element_type=jnp.float32)
    upper = jnp.dot(rows, w_in[1], preferred_element_type=jnp.float32)
    hidden = (gate / (1.0 + jnp.exp(-gate)) * upper).astype(jnp.bfloat16)
    unstack(jnp.dot(hidden, w_out[...], preferred_element_type=jnp.float32), outs)


def sum_kernel(count, *refs):
    total = refs[0][...].astype(jnp.float32)
    for r in refs[1:count]:
        total = total + r[...].astype(jnp.float32)
    unstack(total, refs[count:])


def combined(terms, parts, rows):
    values = stack(parts).astype(jnp.bfloat16)
    product = jnp.dot(terms[...], values, preferred_element_type=jnp.float32)
    return product[2 * rows :] + product[rows : 2 * rows] + product[:rows]


def near_kernel(terms, *refs):
    refs[-1][...] = combined(terms, refs[:-1], refs[-1].shape[0])


def far_kernel(terms, near, *refs):
    total = near[...] + combined(terms, refs[:-1], refs[-1].shape[0])
    refs[-1][...] = total.astype(jnp.bfloat16)


def call(kernel, inputs, in_specs, outs, limit, scratch=(), moved=0):
    return pl.pallas_call(
        kernel,
        out_shape=outs,
        in_specs=in_specs,
        out_specs=jax.tree.map(lambda _: VMEM, outs),
        scratch_shapes=scratch,
        compiler_params=pltpu.CompilerParams(vmem_limit_bytes=limit),
        cost_estimate=pl.CostEstimate(flops=0, bytes_accessed=moved, transcendentals=0)
        if moved
        else None,
    )(*inputs)


def body(tokens, expert_ids, gate_weights, replica_pick, placement, w_in, w_out):
    n_devices = lax.axis_size("expert")
    group_size = min(8, n_devices // 4)
    slot_count = n_devices // group_size
    tok_count, width = tokens.shape
    capacity = tok_count * expert_ids.shape[1] // slot_count
    slots = slot_count * capacity
    offsets = [*range(0, slot_count, 2), *range(1, slot_count, 2)]
    bf16 = jnp.bfloat16
    chunk = jax.ShapeDtypeStruct((capacity, width), bf16)
    half = jax.ShapeDtypeStruct((slots // 2, width), bf16)

    def swap(value, offset):
        return lax.ppermute(value, "expert", [(e, e ^ offset) for e in range(n_devices)])

    def local(kernel, inputs, outs, limit=16 * MIB):
        return call(kernel, inputs, [VMEM] * len(inputs), outs, limit)

    def in_hbm(*arrays):
        return [pltpu.with_memory_space_constraint(a, pltpu.HBM) for a in arrays]

    sources = in_hbm(placement, expert_ids.T, replica_pick.T, gate_weights.T, tokens)
    *chunks, combine = call(
        functools.partial(route_kernel, group_size, slot_count),
        sources,
        [HBM] * 5,
        [chunk] * slot_count + [jax.ShapeDtypeStruct((slots, tok_count), jnp.float32)],
        16 * MIB,
        [pltpu.SMEM(placement.shape, jnp.int32)]
        + [pltpu.VMEM(s.shape, s.dtype) for s in sources[1:]]
        + [pltpu.SemaphoreType.DMA((5,))],
    )
    chunks = [swap(c, d * group_size) if d else c for d, c in zip(offsets, chunks)]
    terms = jax.ShapeDtypeStruct((3 * tok_count, slots // 2), bf16)
    w_in, w_out, *terms = call(
        prepare_kernel,
        (*in_hbm(w_in, w_out), combine),
        [HBM] * 2 + [VMEM],
        [*(jax.ShapeDtypeStruct(w.shape, bf16) for w in (w_in, w_out)), terms, terms],
        16 * MIB,
        [pltpu.SemaphoreType.DMA((5,))],
        2 * (w_in.size + w_out.size),
    )

    square = group_size == 4
    count = slot_count // 2
    sides = ((1, 2), (2, 1))
    earlier = []
    summed = []
    for h in range(2):
        a, b = sides[h]
        own = local(
            functools.partial(stack_kernel, count), chunks[h * count :][:count] + earlier, half
        )
        if square:
            held = {a: swap(own, a), b: swap(own, b)}
            held = [own, held[a], held[b], swap(held[a], b)]
        else:
            held = [swap(own, q) if q else own for q in range(group_size)]
        earlier = [held[1]]
        result = local(
            functools.partial(expert_kernel, group_size),
            held + [w_in, w_out],
            [half] * group_size,
            40 * MIB,
        )
        if square:
            mine, first, second, cross = result
            cross = swap(cross, a)
            first = swap(first, a)
            second = local(functools.partial(sum_kernel, 2), [second, cross], [half])[0]
            result = [mine, first, swap(second, b)]
        else:
            result = [swap(v, q) if q else v for q, v in enumerate(result)]
        summed += local(functools.partial(sum_kernel, len(result)), result, [chunk] * count)
    summed = [swap(v, d * group_size) if d else v for d, v in zip(offsets, summed)]
    near = local(
        near_kernel,
        [terms[0]] + summed[:count],
        jax.ShapeDtypeStruct((tok_count, width), jnp.float32),
    )
    return local(
        far_kernel,
        [terms[1], near] + summed[count:],
        jax.ShapeDtypeStruct((tok_count, width), bf16),
    )


def solution(mesh):
    in_specs = (
        P(("dp", "expert"), None),
        P(("dp", "expert"), None),
        P(("dp", "expert"), None),
        P(("dp", "expert"), None),
        P(),
        P(None, None, "expert"),
        P("expert", None),
    )
    out_specs = P(("dp", "expert"), None)
    return jax.shard_map(body, mesh=mesh, in_specs=in_specs, out_specs=out_specs, check_vma=False)
```

```python
import functools

import jax
import jax.numpy as jnp
from jax import lax
from jax.experimental import pallas as pl
from jax.experimental.pallas import tpu as pltpu
from jax.sharding import PartitionSpec as P

VMEM = pl.BlockSpec(memory_space=pltpu.VMEM)
HBM = pl.BlockSpec(memory_space=pltpu.HBM)
MIB = 1 << 20


def iota(shape, axis):
    return lax.broadcasted_iota(jnp.int32, shape, axis)


def stack(refs):
    return jnp.concatenate([r[...].astype(jnp.float32) for r in refs], axis=0)


def unstack(value, outs):
    start = 0
    for out in outs:
        out[...] = value[start : start + out.shape[0]].astype(out.dtype)
        start += out.shape[0]


def route_kernel(group_size, slot_count, *refs):
    sources, refs = refs[:5], refs[5:]
    row_outs, combine_out, refs = refs[:slot_count], refs[slot_count], refs[slot_count + 1 :]
    scratch, sems = refs[:5], refs[5]
    copies_in = [
        pltpu.make_async_copy(s, t, sems.at[i]) for i, (s, t) in enumerate(zip(sources, scratch))
    ]
    for c in copies_in:
        c.start()
    placement, expert_ids, replica_pick, gate_weights, tokens = scratch
    capacity = row_outs[0].shape[0]
    top_count, tok_count = expert_ids.shape
    own = lax.axis_index("expert") // group_size
    copy_row = iota((slot_count, tok_count), 0)
    named = jnp.zeros_like(copy_row)
    before = jnp.zeros_like(copy_row)
    relative = jnp.zeros_like(copy_row)
    for c in copies_in[:4]:
        c.wait()
    for p in range(slot_count):
        here = copy_row == p
        named = jnp.where(here, placement[p], named)
        d = lax.bitwise_xor(own, p)
        relative = jnp.where(here, d // 2 + d % 2 * (slot_count // 2), relative)
        seen = jnp.int32(0)
        for q in range(p):
            seen = seen + (placement[q] == placement[p]).astype(jnp.int32)
        before = jnp.where(here, seen, before)
    chosen = []
    for k in range(top_count):
        matches = named == expert_ids[pl.ds(k, 1), :]
        copies = jnp.sum(matches.astype(jnp.int32), axis=0, keepdims=True)
        pick = replica_pick[pl.ds(k, 1), :]
        wanted = jnp.where(pick >= copies, pick - copies, pick)
        chosen.append((matches & (before == wanted)).astype(jnp.int32))
    total = sum(chosen[1:], chosen[0])
    ahead = (iota((tok_count, tok_count), 0) < iota((tok_count, tok_count), 1)).astype(jnp.bfloat16)
    earlier = jnp.dot(
        total.astype(jnp.bfloat16), ahead, preferred_element_type=jnp.float32
    ).astype(jnp.int32)
    slot_row = iota((slot_count * capacity, tok_count), 0)
    pick_rows = jnp.zeros((slot_count * capacity, tok_count), jnp.float32)
    combine = jnp.zeros((slot_count * capacity, tok_count), jnp.float32)
    for k in range(top_count):
        rank = jnp.sum(chosen[k] * earlier, axis=0, keepdims=True)
        place = jnp.sum(chosen[k] * relative, axis=0, keepdims=True)
        slot = jnp.where(rank < capacity, place * capacity + rank, -1)
        hot = slot_row == slot
        pick_rows = pick_rows + hot.astype(jnp.float32)
        combine = combine + jnp.where(hot, gate_weights[pl.ds(k, 1), :], 0.0)
        earlier = earlier + chosen[k]
    combine_out[...] = combine
    copies_in[4].wait()
    rows = jnp.dot(pick_rows.astype(jnp.bfloat16), tokens[...], preferred_element_type=jnp.float32)
    unstack(rows, row_outs)


def fetch_kernel(*refs):
    source, held, sems = refs[0], refs[-2], refs[-1]
    rows = held.shape[0] // sems.shape[0]
    copies = [
        pltpu.make_async_copy(source.at[pl.ds(i * rows, rows)], held.at[pl.ds(i * rows, rows)], sem)
        for i, sem in enumerate(sems.at[j] for j in range(sems.shape[0]))
    ]
    for c in copies:
        c.start()
    for c in copies:
        c.wait()


def terms_kernel(combine, near_terms, far_terms):
    slots = combine.shape[0] // 2
    same = (iota((slots, slots), 0) == iota((slots, slots), 1)).astype(jnp.float32)
    for start, out in ((0, near_terms), (slots, far_terms)):
        rest = combine[pl.ds(start, slots), :]
        terms = []
        for _ in range(3):
            term = rest.astype(jnp.bfloat16).astype(jnp.float32)
            rest = rest - term
            terms.append(
                lax.dot_general(
                    term, same, (((0,), (0,)), ((), ())), preferred_element_type=jnp.float32
                )
            )
        out[...] = jnp.concatenate(terms, axis=0).astype(jnp.bfloat16)


def stack_kernel(count, *refs):
    refs[-1][...] = stack(refs[:count]).astype(jnp.bfloat16)


def expert_kernel(count, *refs):
    blocks, (w_in, w_out), outs = refs[:count], refs[count : count + 2], refs[count + 2 :]
    rows = stack(blocks).astype(jnp.bfloat16)
    gate = jnp.dot(rows, w_in[0], preferred_element_type=jnp.float32)
    upper = jnp.dot(rows, w_in[1], preferred_element_type=jnp.float32)
    hidden = (gate / (1.0 + jnp.exp(-gate)) * upper).astype(jnp.bfloat16)
    unstack(jnp.dot(hidden, w_out[...], preferred_element_type=jnp.float32), outs)


def sum_kernel(count, *refs):
    total = refs[0][...].astype(jnp.float32)
    for r in refs[1:count]:
        total = total + r[...].astype(jnp.float32)
    unstack(total, refs[count:])


def combined(terms, parts, rows):
    values = stack(parts).astype(jnp.bfloat16)
    product = jnp.dot(terms[...], values, preferred_element_type=jnp.float32)
    return product[2 * rows :] + product[rows : 2 * rows] + product[:rows]


def near_kernel(terms, *refs):
    refs[-1][...] = combined(terms, refs[:-1], refs[-1].shape[0])


def far_kernel(terms, near, *refs):
    total = near[...] + combined(terms, refs[:-1], refs[-1].shape[0])
    refs[-1][...] = total.astype(jnp.bfloat16)


def call(kernel, inputs, in_specs, outs, limit, scratch=(), moved=0):
    return pl.pallas_call(
        kernel,
        out_shape=outs,
        in_specs=in_specs,
        out_specs=jax.tree.map(lambda _: VMEM, outs),
        scratch_shapes=scratch,
        compiler_params=pltpu.CompilerParams(vmem_limit_bytes=limit),
        cost_estimate=pl.CostEstimate(flops=0, bytes_accessed=moved, transcendentals=0)
        if moved
        else None,
    )(*inputs)


def body(tokens, expert_ids, gate_weights, replica_pick, placement, w_in, w_out):
    n_devices = lax.axis_size("expert")
    group_size = min(8, n_devices // 4)
    slot_count = n_devices // group_size
    tok_count, width = tokens.shape
    capacity = tok_count * expert_ids.shape[1] // slot_count
    slots = slot_count * capacity
    offsets = [*range(0, slot_count, 2), *range(1, slot_count, 2)]
    bf16 = jnp.bfloat16
    chunk = jax.ShapeDtypeStruct((capacity, width), bf16)
    half = jax.ShapeDtypeStruct((slots // 2, width), bf16)

    def swap(value, offset):
        return lax.ppermute(value, "expert", [(e, e ^ offset) for e in range(n_devices)])

    def local(kernel, inputs, outs, limit=16 * MIB):
        return call(kernel, inputs, [VMEM] * len(inputs), outs, limit)

    def in_hbm(*arrays):
        return [pltpu.with_memory_space_constraint(a, pltpu.HBM) for a in arrays]

    sources = in_hbm(placement, expert_ids.T, replica_pick.T, gate_weights.T, tokens)
    *chunks, combine = call(
        functools.partial(route_kernel, group_size, slot_count),
        sources,
        [HBM] * 5,
        [chunk] * slot_count + [jax.ShapeDtypeStruct((slots, tok_count), jnp.float32)],
        16 * MIB,
        [pltpu.SMEM(placement.shape, jnp.int32)]
        + [pltpu.VMEM(s.shape, s.dtype) for s in sources[1:]]
        + [pltpu.SemaphoreType.DMA((5,))],
    )
    chunks = [swap(c, d * group_size) if d else c for d, c in zip(offsets, chunks)]
    terms = jax.ShapeDtypeStruct((3 * tok_count, slots // 2), bf16)
    terms = local(terms_kernel, [combine], [terms, terms])

    def fetch(array, after):
        return call(
            fetch_kernel,
            (*in_hbm(array), after),
            [HBM, VMEM],
            jax.ShapeDtypeStruct(array.shape, bf16),
            16 * MIB,
            [pltpu.SemaphoreType.DMA((2,))],
            2 * array.size,
        )

    w_in = fetch(w_in, terms[0])
    w_out = fetch(w_out, terms[1])

    square = group_size == 4
    count = slot_count // 2
    sides = ((1, 2), (2, 1))
    earlier = chunks[count:] + [w_in]
    summed = []
    for h in range(2):
        a, b = sides[h]
        own = local(
            functools.partial(stack_kernel, count), chunks[h * count :][:count] + earlier, half
        )
        if square:
            held = {a: swap(own, a), b: swap(own, b)}
            held = [own, held[a], held[b], swap(held[a], b)]
        else:
            held = [swap(own, q) if q else own for q in range(group_size)]
        earlier = []
        result = local(
            functools.partial(expert_kernel, group_size),
            held + [w_in, w_out],
            [half] * group_size,
            40 * MIB,
        )
        if square:
            mine, first, second, cross = result
            cross = swap(cross, a)
            first = swap(first, a)
            second = local(functools.partial(sum_kernel, 2), [second, cross], [half])[0]
            result = [mine, first, swap(second, b)]
        else:
            result = [swap(v, q) if q else v for q, v in enumerate(result)]
        summed += local(functools.partial(sum_kernel, len(result)), result, [chunk] * count)
    summed = [swap(v, d * group_size) if d else v for d, v in zip(offsets, summed)]
    near = local(
        near_kernel,
        [terms[0]] + summed[:count],
        jax.ShapeDtypeStruct((tok_count, width), jnp.float32),
    )
    return local(
        far_kernel,
        [terms[1], near] + summed[count:],
        jax.ShapeDtypeStruct((tok_count, width), bf16),
    )


def solution(mesh):
    in_specs = (
        P(("dp", "expert"), None),
        P(("dp", "expert"), None),
        P(("dp", "expert"), None),
        P(("dp", "expert"), None),
        P(),
        P(None, None, "expert"),
        P("expert", None),
    )
    out_specs = P(("dp", "expert"), None)
    return jax.shard_map(body, mesh=mesh, in_specs=in_specs, out_specs=out_specs, check_vma=False)
```

```python
import functools

import jax
import jax.numpy as jnp
from jax import lax
from jax.experimental import pallas as pl
from jax.experimental.pallas import tpu as pltpu
from jax.sharding import PartitionSpec as P

VMEM = pl.BlockSpec(memory_space=pltpu.VMEM)
HBM = pl.BlockSpec(memory_space=pltpu.HBM)
MIB = 1 << 20


def iota(shape, axis):
    return lax.broadcasted_iota(jnp.int32, shape, axis)


def stack(refs):
    return jnp.concatenate([r[...].astype(jnp.float32) for r in refs], axis=0)


def unstack(value, outs):
    start = 0
    for out in outs:
        out[...] = value[start : start + out.shape[0]].astype(out.dtype)
        start += out.shape[0]


def route_kernel(group_size, slot_count, *refs):
    chain = slot_count // 2
    sources, refs = refs[:5], refs[5:]
    row_outs, combine_out, refs = refs[: chain + 1], refs[chain + 1], refs[chain + 2 :]
    scratch, sems = refs[:5], refs[5]
    copies_in = [
        pltpu.make_async_copy(s, t, sems.at[i]) for i, (s, t) in enumerate(zip(sources, scratch))
    ]
    for c in copies_in:
        c.start()
    placement, expert_ids, replica_pick, gate_weights, tokens = scratch
    capacity = row_outs[0].shape[0]
    top_count, tok_count = expert_ids.shape
    own = lax.axis_index("expert") // group_size
    core = lax.axis_index("dp") % 2
    copy_row = iota((slot_count, tok_count), 0)
    named = jnp.zeros_like(copy_row)
    before = jnp.zeros_like(copy_row)
    relative = jnp.zeros_like(copy_row)
    for c in copies_in[:4]:
        c.wait()
    for p in range(slot_count):
        here = copy_row == p
        named = jnp.where(here, placement[p], named)
        d = lax.bitwise_xor(own, p)
        step = jnp.where(d % 2 == 0, (d // 2 + chain - 1) % chain, d // 2)
        relative = jnp.where(here, step + jnp.where(d % 2 == core, 0, chain), relative)
        seen = jnp.int32(0)
        for q in range(p):
            seen = seen + (placement[q] == placement[p]).astype(jnp.int32)
        before = jnp.where(here, seen, before)
    chosen = []
    for k in range(top_count):
        matches = named == expert_ids[pl.ds(k, 1), :]
        copies = jnp.sum(matches.astype(jnp.int32), axis=0, keepdims=True)
        pick = replica_pick[pl.ds(k, 1), :]
        wanted = jnp.where(pick >= copies, pick - copies, pick)
        chosen.append((matches & (before == wanted)).astype(jnp.int32))
    total = sum(chosen[1:], chosen[0])
    ahead = (iota((tok_count, tok_count), 0) < iota((tok_count, tok_count), 1)).astype(jnp.bfloat16)
    earlier = jnp.dot(
        total.astype(jnp.bfloat16), ahead, preferred_element_type=jnp.float32
    ).astype(jnp.int32)
    slot_row = iota((slot_count * capacity, tok_count), 0)
    pick_rows = jnp.zeros((slot_count * capacity, tok_count), jnp.float32)
    combine = jnp.zeros((slot_count * capacity, tok_count), jnp.float32)
    for k in range(top_count):
        rank = jnp.sum(chosen[k] * earlier, axis=0, keepdims=True)
        place = jnp.sum(chosen[k] * relative, axis=0, keepdims=True)
        slot = jnp.where(rank < capacity, place * capacity + rank, -1)
        hot = slot_row == slot
        pick_rows = pick_rows + hot.astype(jnp.float32)
        combine = combine + jnp.where(hot, gate_weights[pl.ds(k, 1), :], 0.0)
        earlier = earlier + chosen[k]
    combine_out[...] = combine
    copies_in[4].wait()
    rows = jnp.dot(pick_rows.astype(jnp.bfloat16), tokens[...], preferred_element_type=jnp.float32)
    unstack(rows, row_outs)


def fetch_kernel(*refs):
    source, held, sems = refs[0], refs[-2], refs[-1]
    rows = held.shape[0] // sems.shape[0]
    copies = [
        pltpu.make_async_copy(source.at[pl.ds(i * rows, rows)], held.at[pl.ds(i * rows, rows)], sem)
        for i, sem in enumerate(sems.at[j] for j in range(sems.shape[0]))
    ]
    for c in copies:
        c.start()
    for c in copies:
        c.wait()


def terms_kernel(combine, near_terms, far_terms):
    slots = combine.shape[0] // 2
    same = (iota((slots, slots), 0) == iota((slots, slots), 1)).astype(jnp.float32)
    for start, out in ((0, near_terms), (slots, far_terms)):
        rest = combine[pl.ds(start, slots), :]
        terms = []
        for _ in range(3):
            term = rest.astype(jnp.bfloat16).astype(jnp.float32)
            rest = rest - term
            terms.append(
                lax.dot_general(
                    term, same, (((0,), (0,)), ((), ())), preferred_element_type=jnp.float32
                )
            )
        out[...] = jnp.concatenate(terms, axis=0).astype(jnp.bfloat16)


def message_kernel(chain, *refs):
    own, other, outs = refs[:chain], refs[chain][...].astype(jnp.float32), refs[chain + 1 :]
    capacity = own[0].shape[0]
    for j, out in enumerate(outs):
        rows = other[j * capacity : (j + 1) * capacity]
        out[...] = jnp.concatenate([own[j][...].astype(jnp.float32), rows], axis=0).astype(
            jnp.bfloat16
        )


def arrived(refs, kept):
    core = lax.axis_index("dp") % 2
    values = [r[...].astype(jnp.float32) for r in refs]
    values[-1] = jnp.where(core == 0, kept[...].astype(jnp.float32), values[-1])
    return values


def block_kernel(chain, *refs):
    values = arrived(refs[:chain], refs[chain])
    refs[-1][...] = jnp.concatenate(values, axis=0).astype(jnp.bfloat16)


def split_kernel(chain, *refs):
    values = arrived(refs[:chain], refs[chain])
    half = values[0].shape[0] // 2
    refs[-2][...] = jnp.concatenate([v[:half] for v in values], axis=0).astype(jnp.bfloat16)
    refs[-1][...] = jnp.concatenate([v[half:] for v in values], axis=0).astype(jnp.bfloat16)


def expert_kernel(count, *refs):
    blocks, (w_in, w_out), outs = refs[:count], refs[count : count + 2], refs[count + 2 :]
    rows = stack(blocks).astype(jnp.bfloat16)
    gate = jnp.dot(rows, w_in[0], preferred_element_type=jnp.float32)
    upper = jnp.dot(rows, w_in[1], preferred_element_type=jnp.float32)
    hidden = (gate / (1.0 + jnp.exp(-gate)) * upper).astype(jnp.bfloat16)
    unstack(jnp.dot(hidden, w_out[...], preferred_element_type=jnp.float32), outs)


def sum_kernel(count, *refs):
    total = refs[0][...].astype(jnp.float32)
    for r in refs[1:count]:
        total = total + r[...].astype(jnp.float32)
    unstack(total, refs[count:])


def combined(terms, parts, rows):
    values = stack(parts).astype(jnp.bfloat16)
    product = jnp.dot(terms[...], values, preferred_element_type=jnp.float32)
    return product[2 * rows :] + product[rows : 2 * rows] + product[:rows]


def near_kernel(terms, *refs):
    refs[-1][...] = combined(terms, refs[:-1], refs[-1].shape[0])


def far_kernel(terms, near, *refs):
    total = near[...] + combined(terms, refs[:-1], refs[-1].shape[0])
    refs[-1][...] = total.astype(jnp.bfloat16)


def call(kernel, inputs, in_specs, outs, limit, scratch=(), moved=0):
    return pl.pallas_call(
        kernel,
        out_shape=outs,
        in_specs=in_specs,
        out_specs=jax.tree.map(lambda _: VMEM, outs),
        scratch_shapes=scratch,
        compiler_params=pltpu.CompilerParams(vmem_limit_bytes=limit),
        cost_estimate=pl.CostEstimate(flops=0, bytes_accessed=moved, transcendentals=0)
        if moved
        else None,
    )(*inputs)


def body(tokens, expert_ids, gate_weights, replica_pick, placement, w_in, w_out):
    n_devices = lax.axis_size("expert")
    group_size = min(8, n_devices // 4)
    slot_count = n_devices // group_size
    tok_count, width = tokens.shape
    capacity = tok_count * expert_ids.shape[1] // slot_count
    slots = slot_count * capacity
    bf16 = jnp.bfloat16
    chain = slot_count // 2
    chunk = jax.ShapeDtypeStruct((capacity, width), bf16)
    pair = jax.ShapeDtypeStruct((2 * capacity, width), bf16)
    half = jax.ShapeDtypeStruct((chain * capacity, width), bf16)
    block = jax.ShapeDtypeStruct((slots, width), bf16)
    parts = lax.axis_size("dp")

    def move(value, even, odd):
        pairs = [
            (e * parts + part, (e ^ offset) * parts + part)
            for e in range(n_devices)
            for part in range(parts)
            for offset in [odd if part % 2 else even]
            if offset
        ]
        return lax.ppermute(value, ("expert", "dp"), pairs)

    def cross_cores(value):
        return lax.ppermute(value, "dp", [(part, part ^ 1) for part in range(parts)])

    def steps(values):
        even = [*range(2, slot_count, 2), 0]
        return [
            move(v, even[j] * group_size, (2 * j + 1) * group_size) for j, v in enumerate(values)
        ]

    def local(kernel, inputs, outs, limit=16 * MIB):
        return call(kernel, inputs, [VMEM] * len(inputs), outs, limit)

    def in_hbm(*arrays):
        return [pltpu.with_memory_space_constraint(a, pltpu.HBM) for a in arrays]

    sources = in_hbm(placement, expert_ids.T, replica_pick.T, gate_weights.T, tokens)
    *chunks, other, combine = call(
        functools.partial(route_kernel, group_size, slot_count),
        sources,
        [HBM] * 5,
        [chunk] * chain + [half, jax.ShapeDtypeStruct((slots, tok_count), jnp.float32)],
        16 * MIB,
        [pltpu.SMEM(placement.shape, jnp.int32)]
        + [pltpu.VMEM(s.shape, s.dtype) for s in sources[1:]]
        + [pltpu.SemaphoreType.DMA((5,))],
    )
    messages = local(
        functools.partial(message_kernel, chain), chunks + [cross_cores(other)], [pair] * chain
    )
    terms = jax.ShapeDtypeStruct((3 * tok_count, slots // 2), bf16)
    terms = local(terms_kernel, [combine], [terms, terms])

    def fetch(array, after):
        return call(
            fetch_kernel,
            (*in_hbm(array), after),
            [HBM, VMEM],
            jax.ShapeDtypeStruct(array.shape, bf16),
            16 * MIB,
            [pltpu.SemaphoreType.DMA((2,))],
            2 * array.size,
        )

    w_in = fetch(w_in, terms[0])
    w_out = fetch(w_out, terms[1])

    own = local(
        functools.partial(block_kernel, chain), steps(messages) + [messages[-1], w_in], block
    )
    square = group_size == 4
    if square:
        first = move(own, 1, 2)
        held = [own, first, move(own, 2, 1), move(first, 2, 1)]
    else:
        held = [move(own, q, q) if q else own for q in range(group_size)]
    result = local(
        functools.partial(expert_kernel, group_size),
        held + [w_in, w_out],
        [block] * group_size,
        40 * MIB,
    )
    if square:
        mine, first, second, cross = result
        cross = move(cross, 1, 2)
        first = move(first, 1, 2)
        second = local(functools.partial(sum_kernel, 2), [second, cross], [block])[0]
        result = [mine, first, move(second, 2, 1)]
    else:
        result = [move(v, q, q) if q else v for q, v in enumerate(result)]
    summed = local(functools.partial(sum_kernel, len(result)), result, [pair] * chain)
    mine, other = local(
        functools.partial(split_kernel, chain), steps(summed) + [summed[-1]], [half, half]
    )
    other = cross_cores(other)
    near = local(
        near_kernel, [terms[0], mine], jax.ShapeDtypeStruct((tok_count, width), jnp.float32)
    )
    return local(
        far_kernel, [terms[1], near, other], jax.ShapeDtypeStruct((tok_count, width), bf16)
    )


def solution(mesh):
    in_specs = (
        P(("dp", "expert"), None),
        P(("dp", "expert"), None),
        P(("dp", "expert"), None),
        P(("dp", "expert"), None),
        P(),
        P(None, None, "expert"),
        P("expert", None),
    )
    out_specs = P(("dp", "expert"), None)
    return jax.shard_map(body, mesh=mesh, in_specs=in_specs, out_specs=out_specs, check_vma=False)
```

```python
import functools

import jax
import jax.numpy as jnp
from jax import lax
from jax.experimental import pallas as pl
from jax.experimental.pallas import tpu as pltpu
from jax.sharding import PartitionSpec as P

VMEM = pl.BlockSpec(memory_space=pltpu.VMEM)
HBM = pl.BlockSpec(memory_space=pltpu.HBM)
MIB = 1 << 20


def iota(shape, axis):
    return lax.broadcasted_iota(jnp.int32, shape, axis)


def stack(refs):
    return jnp.concatenate([r[...].astype(jnp.float32) for r in refs], axis=0)


def unstack(value, outs):
    start = 0
    for out in outs:
        out[...] = value[start : start + out.shape[0]].astype(out.dtype)
        start += out.shape[0]


def route_kernel(group_size, slot_count, *refs):
    sources, refs = refs[:5], refs[5:]
    row_outs, combine_out, refs = refs[:slot_count], refs[slot_count], refs[slot_count + 1 :]
    scratch, sems = refs[:5], refs[5]
    copies_in = [
        pltpu.make_async_copy(s, t, sems.at[i]) for i, (s, t) in enumerate(zip(sources, scratch))
    ]
    for c in copies_in:
        c.start()
    placement, expert_ids, replica_pick, gate_weights, tokens = scratch
    capacity = row_outs[0].shape[0]
    top_count, tok_count = expert_ids.shape
    own = lax.axis_index("expert") // group_size
    copy_row = iota((slot_count, tok_count), 0)
    named = jnp.zeros_like(copy_row)
    before = jnp.zeros_like(copy_row)
    relative = jnp.zeros_like(copy_row)
    for c in copies_in[:4]:
        c.wait()
    for p in range(slot_count):
        here = copy_row == p
        named = jnp.where(here, placement[p], named)
        d = lax.bitwise_xor(own, p)
        relative = jnp.where(here, d // 2 + d % 2 * (slot_count // 2), relative)
        seen = jnp.int32(0)
        for q in range(p):
            seen = seen + (placement[q] == placement[p]).astype(jnp.int32)
        before = jnp.where(here, seen, before)
    chosen = []
    for k in range(top_count):
        matches = named == expert_ids[pl.ds(k, 1), :]
        copies = jnp.sum(matches.astype(jnp.int32), axis=0, keepdims=True)
        pick = replica_pick[pl.ds(k, 1), :]
        wanted = jnp.where(pick >= copies, pick - copies, pick)
        chosen.append((matches & (before == wanted)).astype(jnp.int32))
    total = sum(chosen[1:], chosen[0])
    ahead = (iota((tok_count, tok_count), 0) < iota((tok_count, tok_count), 1)).astype(jnp.bfloat16)
    earlier = jnp.dot(
        total.astype(jnp.bfloat16), ahead, preferred_element_type=jnp.float32
    ).astype(jnp.int32)
    slot_row = iota((slot_count * capacity, tok_count), 0)
    pick_rows = jnp.zeros((slot_count * capacity, tok_count), jnp.float32)
    combine = jnp.zeros((slot_count * capacity, tok_count), jnp.float32)
    for k in range(top_count):
        rank = jnp.sum(chosen[k] * earlier, axis=0, keepdims=True)
        place = jnp.sum(chosen[k] * relative, axis=0, keepdims=True)
        slot = jnp.where(rank < capacity, place * capacity + rank, -1)
        hot = slot_row == slot
        pick_rows = pick_rows + hot.astype(jnp.float32)
        combine = combine + jnp.where(hot, gate_weights[pl.ds(k, 1), :], 0.0)
        earlier = earlier + chosen[k]
    combine_out[...] = combine
    copies_in[4].wait()
    rows = jnp.dot(pick_rows.astype(jnp.bfloat16), tokens[...], preferred_element_type=jnp.float32)
    unstack(rows, row_outs)


def fetch_kernel(*refs):
    source, held, sems = refs[0], refs[-2], refs[-1]
    rows = held.shape[0] // sems.shape[0]
    copies = [
        pltpu.make_async_copy(source.at[pl.ds(i * rows, rows)], held.at[pl.ds(i * rows, rows)], sem)
        for i, sem in enumerate(sems.at[j] for j in range(sems.shape[0]))
    ]
    for c in copies:
        c.start()
    for c in copies:
        c.wait()


def terms_kernel(combine, near_terms, far_terms):
    slots = combine.shape[0] // 2
    same = (iota((slots, slots), 0) == iota((slots, slots), 1)).astype(jnp.float32)
    for start, out in ((0, near_terms), (slots, far_terms)):
        rest = combine[pl.ds(start, slots), :]
        terms = []
        for _ in range(3):
            term = rest.astype(jnp.bfloat16).astype(jnp.float32)
            rest = rest - term
            terms.append(
                lax.dot_general(
                    term, same, (((0,), (0,)), ((), ())), preferred_element_type=jnp.float32
                )
            )
        out[...] = jnp.concatenate(terms, axis=0).astype(jnp.bfloat16)


def stack_kernel(count, *refs):
    refs[-1][...] = stack(refs[:count]).astype(jnp.bfloat16)


def expert_kernel(count, *refs):
    blocks, (w_in, w_out), outs = refs[:count], refs[count : count + 2], refs[count + 2 :]
    rows = stack(blocks).astype(jnp.bfloat16)
    gate = jnp.dot(rows, w_in[0], preferred_element_type=jnp.float32)
    upper = jnp.dot(rows, w_in[1], preferred_element_type=jnp.float32)
    hidden = (gate / (1.0 + jnp.exp(-gate)) * upper).astype(jnp.bfloat16)
    unstack(jnp.dot(hidden, w_out[...], preferred_element_type=jnp.float32), outs)


def sum_kernel(count, *refs):
    total = refs[0][...].astype(jnp.float32)
    for r in refs[1:count]:
        total = total + r[...].astype(jnp.float32)
    unstack(total, refs[count:])


def combined(terms, parts, rows):
    values = stack(parts).astype(jnp.bfloat16)
    product = jnp.dot(terms[...], values, preferred_element_type=jnp.float32)
    return product[2 * rows :] + product[rows : 2 * rows] + product[:rows]


def near_kernel(terms, *refs):
    refs[-1][...] = combined(terms, refs[:-1], refs[-1].shape[0])


def far_kernel(terms, near, *refs):
    total = near[...] + combined(terms, refs[:-1], refs[-1].shape[0])
    refs[-1][...] = total.astype(jnp.bfloat16)


def call(kernel, inputs, in_specs, outs, limit, scratch=(), moved=0):
    return pl.pallas_call(
        kernel,
        out_shape=outs,
        in_specs=in_specs,
        out_specs=jax.tree.map(lambda _: VMEM, outs),
        scratch_shapes=scratch,
        compiler_params=pltpu.CompilerParams(vmem_limit_bytes=limit),
        cost_estimate=pl.CostEstimate(flops=0, bytes_accessed=moved, transcendentals=0)
        if moved
        else None,
    )(*inputs)


def body(tokens, expert_ids, gate_weights, replica_pick, placement, w_in, w_out):
    n_devices = lax.axis_size("expert")
    group_size = min(8, n_devices // 4)
    slot_count = n_devices // group_size
    tok_count, width = tokens.shape
    capacity = tok_count * expert_ids.shape[1] // slot_count
    slots = slot_count * capacity
    offsets = [*range(0, slot_count, 2), *range(1, slot_count, 2)]
    bf16 = jnp.bfloat16
    chunk = jax.ShapeDtypeStruct((capacity, width), bf16)
    half = jax.ShapeDtypeStruct((slots // 2, width), bf16)

    def swap(value, offset):
        return lax.ppermute(value, "expert", [(e, e ^ offset) for e in range(n_devices)])

    def local(kernel, inputs, outs, limit=16 * MIB):
        return call(kernel, inputs, [VMEM] * len(inputs), outs, limit)

    def in_hbm(*arrays):
        return [pltpu.with_memory_space_constraint(a, pltpu.HBM) for a in arrays]

    sources = in_hbm(placement, expert_ids.T, replica_pick.T, gate_weights.T, tokens)
    *chunks, combine = call(
        functools.partial(route_kernel, group_size, slot_count),
        sources,
        [HBM] * 5,
        [chunk] * slot_count + [jax.ShapeDtypeStruct((slots, tok_count), jnp.float32)],
        16 * MIB,
        [pltpu.SMEM(placement.shape, jnp.int32)]
        + [pltpu.VMEM(s.shape, s.dtype) for s in sources[1:]]
        + [pltpu.SemaphoreType.DMA((5,))],
    )
    chunks = [swap(c, d * group_size) if d else c for d, c in zip(offsets, chunks)]
    terms = jax.ShapeDtypeStruct((3 * tok_count, slots // 2), bf16)
    terms = local(terms_kernel, [combine], [terms, terms])

    def fetch(array, after):
        return call(
            fetch_kernel,
            (*in_hbm(array), after),
            [HBM, VMEM],
            jax.ShapeDtypeStruct(array.shape, bf16),
            16 * MIB,
            [pltpu.SemaphoreType.DMA((2,))],
            2 * array.size,
        )

    w_in = fetch(w_in, terms[0])
    w_out = fetch(w_out, terms[1])

    square = group_size == 4
    count = slot_count // 2
    sides = ((1, 2), (2, 1))
    earlier = []
    summed = []
    for h in range(2):
        a, b = sides[h]
        own = local(
            functools.partial(stack_kernel, count), chunks[h * count :][:count] + earlier, half
        )
        if square:
            held = {a: swap(own, a), b: swap(own, b)}
            held = [own, held[a], held[b], swap(held[a], b)]
        else:
            held = [swap(own, q) if q else own for q in range(group_size)]
        earlier = [w_in]
        result = local(
            functools.partial(expert_kernel, group_size),
            held + [w_in, w_out],
            [half] * group_size,
            40 * MIB,
        )
        if square:
            mine, first, second, cross = result
            cross = swap(cross, a)
            first = swap(first, a)
            second = local(functools.partial(sum_kernel, 2), [second, cross], [half])[0]
            result = [mine, first, swap(second, b)]
        else:
            result = [swap(v, q) if q else v for q, v in enumerate(result)]
        summed += local(functools.partial(sum_kernel, len(result)), result, [chunk] * count)
    summed = [swap(v, d * group_size) if d else v for d, v in zip(offsets, summed)]
    near = local(
        near_kernel,
        [terms[0]] + summed[:count],
        jax.ShapeDtypeStruct((tok_count, width), jnp.float32),
    )
    return local(
        far_kernel,
        [terms[1], near] + summed[count:],
        jax.ShapeDtypeStruct((tok_count, width), bf16),
    )


def solution(mesh):
    in_specs = (
        P(("dp", "expert"), None),
        P(("dp", "expert"), None),
        P(("dp", "expert"), None),
        P(("dp", "expert"), None),
        P(),
        P(None, None, "expert"),
        P("expert", None),
    )
    out_specs = P(("dp", "expert"), None)
    return jax.shard_map(body, mesh=mesh, in_specs=in_specs, out_specs=out_specs, check_vma=False)
```

```python
import functools

import jax
import jax.numpy as jnp
from jax import lax
from jax.experimental import pallas as pl
from jax.experimental.pallas import tpu as pltpu
from jax.sharding import PartitionSpec as P

VMEM = pl.BlockSpec(memory_space=pltpu.VMEM)
HBM = pl.BlockSpec(memory_space=pltpu.HBM)
MIB = 1 << 20


def iota(shape, axis):
    return lax.broadcasted_iota(jnp.int32, shape, axis)


def stack(refs):
    return jnp.concatenate([r[...].astype(jnp.float32) for r in refs], axis=0)


def unstack(value, outs):
    start = 0
    for out in outs:
        out[...] = value[start : start + out.shape[0]].astype(out.dtype)
        start += out.shape[0]


def route_kernel(group_size, slot_count, *refs):
    sources, refs = refs[:5], refs[5:]
    row_outs, combine_out, refs = refs[:slot_count], refs[slot_count], refs[slot_count + 1 :]
    scratch, sems = refs[:5], refs[5]
    copies_in = [
        pltpu.make_async_copy(s, t, sems.at[i]) for i, (s, t) in enumerate(zip(sources, scratch))
    ]
    for c in copies_in:
        c.start()
    placement, expert_ids, replica_pick, gate_weights, tokens = scratch
    capacity = row_outs[0].shape[0]
    top_count, tok_count = expert_ids.shape
    own = lax.axis_index("expert") // group_size
    copy_row = iota((slot_count, tok_count), 0)
    named = jnp.zeros_like(copy_row)
    before = jnp.zeros_like(copy_row)
    relative = jnp.zeros_like(copy_row)
    for c in copies_in[:4]:
        c.wait()
    for p in range(slot_count):
        here = copy_row == p
        named = jnp.where(here, placement[p], named)
        d = lax.bitwise_xor(own, p)
        relative = jnp.where(here, d, relative)
        seen = jnp.int32(0)
        for q in range(p):
            seen = seen + (placement[q] == placement[p]).astype(jnp.int32)
        before = jnp.where(here, seen, before)
    chosen = []
    for k in range(top_count):
        matches = named == expert_ids[pl.ds(k, 1), :]
        copies = jnp.sum(matches.astype(jnp.int32), axis=0, keepdims=True)
        pick = replica_pick[pl.ds(k, 1), :]
        wanted = jnp.where(pick >= copies, pick - copies, pick)
        chosen.append((matches & (before == wanted)).astype(jnp.int32))
    total = sum(chosen[1:], chosen[0])
    ahead = (iota((tok_count, tok_count), 0) < iota((tok_count, tok_count), 1)).astype(jnp.bfloat16)
    earlier = jnp.dot(
        total.astype(jnp.bfloat16), ahead, preferred_element_type=jnp.float32
    ).astype(jnp.int32)
    half = slot_count * capacity // 2
    slot_row = iota((slot_count * capacity, tok_count), 0)
    pick_rows = jnp.zeros((slot_count * capacity, tok_count), jnp.float32)
    combine = jnp.zeros((slot_count * capacity, tok_count), jnp.float32)
    for k in range(top_count):
        rank = jnp.sum(chosen[k] * earlier, axis=0, keepdims=True)
        place = jnp.sum(chosen[k] * relative, axis=0, keepdims=True)
        slot = jnp.where(rank < capacity, place * capacity + rank, -1)
        hot = slot_row == slot
        pick_rows = pick_rows + hot.astype(jnp.float32)
        turned = jnp.where(slot < half, slot + half, slot - half)
        turned = slot_row == jnp.where(slot < 0, -1, turned)
        combine = combine + jnp.where(turned, gate_weights[pl.ds(k, 1), :], 0.0)
        earlier = earlier + chosen[k]
    combine_out[...] = combine
    copies_in[4].wait()
    rows = jnp.dot(pick_rows.astype(jnp.bfloat16), tokens[...], preferred_element_type=jnp.float32)
    unstack(rows, row_outs)


def fetch_kernel(*refs):
    source, held, sems = refs[0], refs[-2], refs[-1]
    rows = held.shape[0] // sems.shape[0]
    copies = [
        pltpu.make_async_copy(source.at[pl.ds(i * rows, rows)], held.at[pl.ds(i * rows, rows)], sem)
        for i, sem in enumerate(sems.at[j] for j in range(sems.shape[0]))
    ]
    for c in copies:
        c.start()
    for c in copies:
        c.wait()


def terms_kernel(combine, near_terms, far_terms):
    slots = combine.shape[0] // 2
    same = (iota((slots, slots), 0) == iota((slots, slots), 1)).astype(jnp.float32)
    for start, out in ((0, near_terms), (slots, far_terms)):
        rest = combine[pl.ds(start, slots), :]
        terms = []
        for _ in range(3):
            term = rest.astype(jnp.bfloat16).astype(jnp.float32)
            rest = rest - term
            terms.append(
                lax.dot_general(
                    term, same, (((0,), (0,)), ((), ())), preferred_element_type=jnp.float32
                )
            )
        out[...] = jnp.concatenate(terms, axis=0).astype(jnp.bfloat16)


def stack_kernel(count, *refs):
    refs[-1][...] = stack(refs[:count]).astype(jnp.bfloat16)


def expert_kernel(count, *refs):
    rests, firsts = refs[:count], refs[count : 2 * count]
    (w_in, w_out), outs = refs[2 * count : 2 * count + 2], refs[2 * count + 2 :]
    rests = [r[...].astype(jnp.float32) for r in rests]
    cut = rests[0].shape[0] - outs[0].shape[0]
    rows = [r[cut:] for r in rests]
    for first, rest in zip(firsts, rests):
        rows += [first[...].astype(jnp.float32), rest[:cut]]
    rows = jnp.concatenate(rows, axis=0).astype(jnp.bfloat16)
    gate = jnp.dot(rows, w_in[0], preferred_element_type=jnp.float32)
    upper = jnp.dot(rows, w_in[1], preferred_element_type=jnp.float32)
    hidden = (gate / (1.0 + jnp.exp(-gate)) * upper).astype(jnp.bfloat16)
    unstack(jnp.dot(hidden, w_out[...], preferred_element_type=jnp.float32), outs)


def sum_kernel(count, *refs):
    total = refs[0][...].astype(jnp.float32)
    for r in refs[1:count]:
        total = total + r[...].astype(jnp.float32)
    unstack(total, refs[count:])


def combined(terms, parts, rows):
    values = stack(parts).astype(jnp.bfloat16)
    product = jnp.dot(terms[...], values, preferred_element_type=jnp.float32)
    return product[2 * rows :] + product[rows : 2 * rows] + product[:rows]


def near_kernel(terms, *refs):
    refs[-1][...] = combined(terms, refs[:-1], refs[-1].shape[0])


def far_kernel(terms, near, *refs):
    total = near[...] + combined(terms, refs[:-1], refs[-1].shape[0])
    refs[-1][...] = total.astype(jnp.bfloat16)


def call(kernel, inputs, in_specs, outs, limit, scratch=(), moved=0):
    return pl.pallas_call(
        kernel,
        out_shape=outs,
        in_specs=in_specs,
        out_specs=jax.tree.map(lambda _: VMEM, outs),
        scratch_shapes=scratch,
        compiler_params=pltpu.CompilerParams(vmem_limit_bytes=limit),
        cost_estimate=pl.CostEstimate(flops=0, bytes_accessed=moved, transcendentals=0)
        if moved
        else None,
    )(*inputs)


def body(tokens, expert_ids, gate_weights, replica_pick, placement, w_in, w_out):
    n_devices = lax.axis_size("expert")
    group_size = min(8, n_devices // 4)
    slot_count = n_devices // group_size
    tok_count, width = tokens.shape
    capacity = tok_count * expert_ids.shape[1] // slot_count
    slots = slot_count * capacity
    bf16 = jnp.bfloat16
    chunk = jax.ShapeDtypeStruct((capacity, width), bf16)
    half = jax.ShapeDtypeStruct((slots // 2, width), bf16)

    def swap(value, offset):
        return lax.ppermute(value, "expert", [(e, e ^ offset) for e in range(n_devices)])

    def turn(value, even, odd):
        parts = lax.axis_size("dp")
        pairs = [
            (e * parts + part, (e ^ (odd if part % 2 else even)) * parts + part)
            for e in range(n_devices)
            for part in range(parts)
        ]
        return lax.ppermute(value, ("expert", "dp"), pairs)

    def local(kernel, inputs, outs, limit=16 * MIB):
        return call(kernel, inputs, [VMEM] * len(inputs), outs, limit)

    def in_hbm(*arrays):
        return [pltpu.with_memory_space_constraint(a, pltpu.HBM) for a in arrays]

    sources = in_hbm(placement, expert_ids.T, replica_pick.T, gate_weights.T, tokens)
    *chunks, combine = call(
        functools.partial(route_kernel, group_size, slot_count),
        sources,
        [HBM] * 5,
        [chunk] * slot_count + [jax.ShapeDtypeStruct((slots, tok_count), jnp.float32)],
        16 * MIB,
        [pltpu.SMEM(placement.shape, jnp.int32)]
        + [pltpu.VMEM(s.shape, s.dtype) for s in sources[1:]]
        + [pltpu.SemaphoreType.DMA((5,))],
    )
    chunks = [swap(c, d * group_size) if d else c for d, c in enumerate(chunks)]
    terms = jax.ShapeDtypeStruct((3 * tok_count, slots // 2), bf16)
    terms = local(terms_kernel, [combine], [terms, terms])

    def fetch(array, after):
        return call(
            fetch_kernel,
            (*in_hbm(array), after),
            [HBM, VMEM],
            jax.ShapeDtypeStruct(array.shape, bf16),
            16 * MIB,
            [pltpu.SemaphoreType.DMA((2,))],
            4 * array.size,
        )

    w_in = fetch(w_in, terms[0])
    w_out = fetch(w_out, terms[1])

    square = group_size == 4

    def spread(own):
        if not square:
            return [swap(own, q) if q else own for q in range(group_size)]
        return [own, turn(own, 1, 2), turn(own, 2, 1)]

    firsts = spread(chunks[0])
    rest = jax.ShapeDtypeStruct((slots - capacity, width), bf16)
    rest = local(
        functools.partial(stack_kernel, slot_count - 1), chunks[1:] + [w_in] + firsts[1:], rest
    )
    rests = spread(rest)
    if square:
        firsts.append(turn(firsts[1], 2, 1))
        rests.append(turn(rests[1], 2, 1))
    result = local(
        functools.partial(expert_kernel, group_size),
        rests + firsts + [w_in, w_out],
        [half] * (2 * group_size),
        40 * MIB,
    )
    count = slot_count // 2
    offsets = [*range(count, slot_count), *range(count)]
    summed = []
    for h, (a, b) in enumerate(((1, 2), (2, 1))):
        part = result[h * group_size : (h + 1) * group_size]
        if square:
            mine, first, second, cross = part if h == 0 else [part[i] for i in (0, 2, 1, 3)]
            cross = turn(cross, a, b)
            first = turn(first, a, b)
            second = local(functools.partial(sum_kernel, 2), [second, cross], [half])[0]
            part = [mine, first, turn(second, b, a)]
        else:
            part = [swap(v, q) if q else v for q, v in enumerate(part)]
        summed += local(functools.partial(sum_kernel, len(part)), part, [chunk] * count)
    summed = [swap(v, d * group_size) if d else v for d, v in zip(offsets, summed)]
    near = local(
        near_kernel,
        [terms[0]] + summed[:count],
        jax.ShapeDtypeStruct((tok_count, width), jnp.float32),
    )
    return local(
        far_kernel,
        [terms[1], near] + summed[count:],
        jax.ShapeDtypeStruct((tok_count, width), bf16),
    )


def solution(mesh):
    in_specs = (
        P(("dp", "expert"), None),
        P(("dp", "expert"), None),
        P(("dp", "expert"), None),
        P(("dp", "expert"), None),
        P(),
        P(None, None, "expert"),
        P("expert", None),
    )
    out_specs = P(("dp", "expert"), None)
    return jax.shard_map(body, mesh=mesh, in_specs=in_specs, out_specs=out_specs, check_vma=False)
```

```python
import functools

import jax
import jax.numpy as jnp
from jax import lax
from jax.experimental import pallas as pl
from jax.experimental.pallas import tpu as pltpu
from jax.sharding import PartitionSpec as P

VMEM = pl.BlockSpec(memory_space=pltpu.VMEM)
HBM = pl.BlockSpec(memory_space=pltpu.HBM)
MIB = 1 << 20


def iota(shape, axis):
    return lax.broadcasted_iota(jnp.int32, shape, axis)


def stack(refs):
    return jnp.concatenate([r[...].astype(jnp.float32) for r in refs], axis=0)


def unstack(value, outs):
    start = 0
    for out in outs:
        out[...] = value[start : start + out.shape[0]].astype(out.dtype)
        start += out.shape[0]


def route_kernel(group_size, slot_count, *refs):
    sources, refs = refs[:5], refs[5:]
    row_outs, combine_out, refs = refs[:slot_count], refs[slot_count], refs[slot_count + 1 :]
    scratch, sems = refs[:5], refs[5]
    copies_in = [
        pltpu.make_async_copy(s, t, sems.at[i]) for i, (s, t) in enumerate(zip(sources, scratch))
    ]
    for c in copies_in:
        c.start()
    placement, expert_ids, replica_pick, gate_weights, tokens = scratch
    capacity = row_outs[0].shape[0]
    top_count, tok_count = expert_ids.shape
    own = lax.axis_index("expert") // group_size
    copy_row = iota((slot_count, tok_count), 0)
    named = jnp.zeros_like(copy_row)
    before = jnp.zeros_like(copy_row)
    relative = jnp.zeros_like(copy_row)
    for c in copies_in[:4]:
        c.wait()
    for p in range(slot_count):
        here = copy_row == p
        named = jnp.where(here, placement[p], named)
        d = lax.bitwise_xor(own, p)
        relative = jnp.where(here, (d + slot_count - 1) % slot_count, relative)
        seen = jnp.int32(0)
        for q in range(p):
            seen = seen + (placement[q] == placement[p]).astype(jnp.int32)
        before = jnp.where(here, seen, before)
    chosen = []
    for k in range(top_count):
        matches = named == expert_ids[pl.ds(k, 1), :]
        copies = jnp.sum(matches.astype(jnp.int32), axis=0, keepdims=True)
        pick = replica_pick[pl.ds(k, 1), :]
        wanted = jnp.where(pick >= copies, pick - copies, pick)
        chosen.append((matches & (before == wanted)).astype(jnp.int32))
    total = sum(chosen[1:], chosen[0])
    ahead = (iota((tok_count, tok_count), 0) < iota((tok_count, tok_count), 1)).astype(jnp.bfloat16)
    earlier = jnp.dot(
        total.astype(jnp.bfloat16), ahead, preferred_element_type=jnp.float32
    ).astype(jnp.int32)
    slot_row = iota((slot_count * capacity, tok_count), 0)
    pick_rows = jnp.zeros((slot_count * capacity, tok_count), jnp.float32)
    combine = jnp.zeros((slot_count * capacity, tok_count), jnp.float32)
    for k in range(top_count):
        rank = jnp.sum(chosen[k] * earlier, axis=0, keepdims=True)
        place = jnp.sum(chosen[k] * relative, axis=0, keepdims=True)
        slot = jnp.where(rank < capacity, place * capacity + rank, -1)
        hot = slot_row == slot
        pick_rows = pick_rows + hot.astype(jnp.float32)
        combine = combine + jnp.where(hot, gate_weights[pl.ds(k, 1), :], 0.0)
        earlier = earlier + chosen[k]
    combine_out[...] = combine
    copies_in[4].wait()
    rows = jnp.dot(pick_rows.astype(jnp.bfloat16), tokens[...], preferred_element_type=jnp.float32)
    unstack(rows, row_outs)


def fetch_kernel(*refs):
    source, held, sems = refs[0], refs[-2], refs[-1]
    rows = held.shape[0] // sems.shape[0]
    copies = [
        pltpu.make_async_copy(source.at[pl.ds(i * rows, rows)], held.at[pl.ds(i * rows, rows)], sem)
        for i, sem in enumerate(sems.at[j] for j in range(sems.shape[0]))
    ]
    for c in copies:
        c.start()
    for c in copies:
        c.wait()


def terms_kernel(combine, near_terms, far_terms):
    slots = combine.shape[0] // 2
    same = (iota((slots, slots), 0) == iota((slots, slots), 1)).astype(jnp.float32)
    for start, out in ((0, near_terms), (slots, far_terms)):
        rest = combine[pl.ds(start, slots), :]
        terms = []
        for _ in range(3):
            term = rest.astype(jnp.bfloat16).astype(jnp.float32)
            rest = rest - term
            terms.append(
                lax.dot_general(
                    term, same, (((0,), (0,)), ((), ())), preferred_element_type=jnp.float32
                )
            )
        out[...] = jnp.concatenate(terms, axis=0).astype(jnp.bfloat16)


def stack_kernel(count, *refs):
    refs[-1][...] = stack(refs[:count]).astype(jnp.bfloat16)


def expert_kernel(count, *refs):
    blocks, (w_in, w_out), outs = refs[:count], refs[count : count + 2], refs[count + 2 :]
    rows = stack(blocks).astype(jnp.bfloat16)
    gate = jnp.dot(rows, w_in[0], preferred_element_type=jnp.float32)
    upper = jnp.dot(rows, w_in[1], preferred_element_type=jnp.float32)
    hidden = (gate / (1.0 + jnp.exp(-gate)) * upper).astype(jnp.bfloat16)
    unstack(jnp.dot(hidden, w_out[...], preferred_element_type=jnp.float32), outs)


def sum_kernel(count, *refs):
    total = refs[0][...].astype(jnp.float32)
    for r in refs[1:count]:
        total = total + r[...].astype(jnp.float32)
    unstack(total, refs[count:])


def combined(terms, parts, rows):
    values = stack(parts).astype(jnp.bfloat16)
    product = jnp.dot(terms[...], values, preferred_element_type=jnp.float32)
    return product[2 * rows :] + product[rows : 2 * rows] + product[:rows]


def near_kernel(terms, *refs):
    refs[-1][...] = combined(terms, refs[:-1], refs[-1].shape[0])


def far_kernel(terms, near, *refs):
    total = near[...] + combined(terms, refs[:-1], refs[-1].shape[0])
    refs[-1][...] = total.astype(jnp.bfloat16)


def call(kernel, inputs, in_specs, outs, limit, scratch=(), moved=0):
    return pl.pallas_call(
        kernel,
        out_shape=outs,
        in_specs=in_specs,
        out_specs=jax.tree.map(lambda _: VMEM, outs),
        scratch_shapes=scratch,
        compiler_params=pltpu.CompilerParams(vmem_limit_bytes=limit),
        cost_estimate=pl.CostEstimate(flops=0, bytes_accessed=moved, transcendentals=0)
        if moved
        else None,
    )(*inputs)


def body(tokens, expert_ids, gate_weights, replica_pick, placement, w_in, w_out):
    n_devices = lax.axis_size("expert")
    group_size = min(8, n_devices // 4)
    slot_count = n_devices // group_size
    tok_count, width = tokens.shape
    capacity = tok_count * expert_ids.shape[1] // slot_count
    slots = slot_count * capacity
    offsets = [*range(1, slot_count), 0]
    bf16 = jnp.bfloat16
    chunk = jax.ShapeDtypeStruct((capacity, width), bf16)
    half = jax.ShapeDtypeStruct((slots // 2, width), bf16)

    def swap(value, offset):
        return lax.ppermute(value, "expert", [(e, e ^ offset) for e in range(n_devices)])

    def local(kernel, inputs, outs, limit=16 * MIB):
        return call(kernel, inputs, [VMEM] * len(inputs), outs, limit)

    def in_hbm(*arrays):
        return [pltpu.with_memory_space_constraint(a, pltpu.HBM) for a in arrays]

    sources = in_hbm(placement, expert_ids.T, replica_pick.T, gate_weights.T, tokens)
    *chunks, combine = call(
        functools.partial(route_kernel, group_size, slot_count),
        sources,
        [HBM] * 5,
        [chunk] * slot_count + [jax.ShapeDtypeStruct((slots, tok_count), jnp.float32)],
        16 * MIB,
        [pltpu.SMEM(placement.shape, jnp.int32)]
        + [pltpu.VMEM(s.shape, s.dtype) for s in sources[1:]]
        + [pltpu.SemaphoreType.DMA((5,))],
    )
    chunks = [swap(c, d * group_size) if d else c for d, c in zip(offsets, chunks)]
    terms = jax.ShapeDtypeStruct((3 * tok_count, slots // 2), bf16)
    terms = local(terms_kernel, [combine], [terms, terms])

    def fetch(array, after):
        return call(
            fetch_kernel,
            (*in_hbm(array), after),
            [HBM, VMEM],
            jax.ShapeDtypeStruct(array.shape, bf16),
            16 * MIB,
            [pltpu.SemaphoreType.DMA((2,))],
            2 * array.size,
        )

    w_in = fetch(w_in, terms[0])
    w_out = fetch(w_out, terms[1])

    square = group_size == 4
    count = slot_count // 2
    sides = ((1, 2), (2, 1))
    earlier = [w_in]
    summed = []
    for h in range(2):
        a, b = sides[h]
        own = local(
            functools.partial(stack_kernel, count), chunks[h * count :][:count] + earlier, half
        )
        if square:
            held = {a: swap(own, a), b: swap(own, b)}
            held = [own, held[a], held[b], swap(held[a], b)]
        else:
            held = [swap(own, q) if q else own for q in range(group_size)]
        earlier = [w_out]
        result = local(
            functools.partial(expert_kernel, group_size),
            held + [w_in, w_out],
            [half] * group_size,
            40 * MIB,
        )
        if square:
            mine, first, second, cross = result
            cross = swap(cross, a)
            first = swap(first, a)
            second = local(functools.partial(sum_kernel, 2), [second, cross], [half])[0]
            result = [mine, first, swap(second, b)]
        else:
            result = [swap(v, q) if q else v for q, v in enumerate(result)]
        summed += local(functools.partial(sum_kernel, len(result)), result, [chunk] * count)
    summed = [swap(v, d * group_size) if d else v for d, v in zip(offsets, summed)]
    near = local(
        near_kernel,
        [terms[0]] + summed[:count],
        jax.ShapeDtypeStruct((tok_count, width), jnp.float32),
    )
    return local(
        far_kernel,
        [terms[1], near] + summed[count:],
        jax.ShapeDtypeStruct((tok_count, width), bf16),
    )


def solution(mesh):
    in_specs = (
        P(("dp", "expert"), None),
        P(("dp", "expert"), None),
        P(("dp", "expert"), None),
        P(("dp", "expert"), None),
        P(),
        P(None, None, "expert"),
        P("expert", None),
    )
    out_specs = P(("dp", "expert"), None)
    return jax.shard_map(body, mesh=mesh, in_specs=in_specs, out_specs=out_specs, check_vma=False)
```

```python
import functools

import jax
import jax.numpy as jnp
from jax import lax
from jax.experimental import pallas as pl
from jax.experimental.pallas import tpu as pltpu
from jax.sharding import PartitionSpec as P

VMEM = pl.BlockSpec(memory_space=pltpu.VMEM)
HBM = pl.BlockSpec(memory_space=pltpu.HBM)
MIB = 1 << 20


def iota(shape, axis):
    return lax.broadcasted_iota(jnp.int32, shape, axis)


def stack(refs):
    return jnp.concatenate([r[...].astype(jnp.float32) for r in refs], axis=0)


def unstack(value, outs):
    start = 0
    for out in outs:
        out[...] = value[start : start + out.shape[0]].astype(out.dtype)
        start += out.shape[0]


def route_kernel(group_size, slot_count, *refs):
    sources, refs = refs[:5], refs[5:]
    row_outs, combine_out, refs = refs[:slot_count], refs[slot_count], refs[slot_count + 1 :]
    scratch, sems = refs[:5], refs[5]
    copies_in = [
        pltpu.make_async_copy(s, t, sems.at[i]) for i, (s, t) in enumerate(zip(sources, scratch))
    ]
    for c in copies_in:
        c.start()
    placement, expert_ids, replica_pick, gate_weights, tokens = scratch
    capacity = row_outs[0].shape[0]
    top_count, tok_count = expert_ids.shape
    own = lax.axis_index("expert") // group_size
    copy_row = iota((slot_count, tok_count), 0)
    named = jnp.zeros_like(copy_row)
    before = jnp.zeros_like(copy_row)
    relative = jnp.zeros_like(copy_row)
    for c in copies_in[:4]:
        c.wait()
    for p in range(slot_count):
        here = copy_row == p
        named = jnp.where(here, placement[p], named)
        d = lax.bitwise_xor(own, p)
        near = jnp.where(d == 0, slot_count - 1, d + slot_count // 2 - 1)
        place = jnp.where(d < slot_count // 2, near, d - slot_count // 2)
        relative = jnp.where(here, place, relative)
        seen = jnp.int32(0)
        for q in range(p):
            seen = seen + (placement[q] == placement[p]).astype(jnp.int32)
        before = jnp.where(here, seen, before)
    chosen = []
    for k in range(top_count):
        matches = named == expert_ids[pl.ds(k, 1), :]
        copies = jnp.sum(matches.astype(jnp.int32), axis=0, keepdims=True)
        pick = replica_pick[pl.ds(k, 1), :]
        wanted = jnp.where(pick >= copies, pick - copies, pick)
        chosen.append((matches & (before == wanted)).astype(jnp.int32))
    total = sum(chosen[1:], chosen[0])
    ahead = (iota((tok_count, tok_count), 0) < iota((tok_count, tok_count), 1)).astype(jnp.bfloat16)
    earlier = jnp.dot(
        total.astype(jnp.bfloat16), ahead, preferred_element_type=jnp.float32
    ).astype(jnp.int32)
    slot_row = iota((slot_count * capacity, tok_count), 0)
    pick_rows = jnp.zeros((slot_count * capacity, tok_count), jnp.float32)
    combine = jnp.zeros((slot_count * capacity, tok_count), jnp.float32)
    for k in range(top_count):
        rank = jnp.sum(chosen[k] * earlier, axis=0, keepdims=True)
        place = jnp.sum(chosen[k] * relative, axis=0, keepdims=True)
        slot = jnp.where(rank < capacity, place * capacity + rank, -1)
        hot = slot_row == slot
        pick_rows = pick_rows + hot.astype(jnp.float32)
        combine = combine + jnp.where(hot, gate_weights[pl.ds(k, 1), :], 0.0)
        earlier = earlier + chosen[k]
    combine_out[...] = combine
    copies_in[4].wait()
    rows = jnp.dot(pick_rows.astype(jnp.bfloat16), tokens[...], preferred_element_type=jnp.float32)
    unstack(rows, row_outs)


def fetch_kernel(*refs):
    source, held, sems = refs[0], refs[-2], refs[-1]
    rows = held.shape[0] // sems.shape[0]
    copies = [
        pltpu.make_async_copy(source.at[pl.ds(i * rows, rows)], held.at[pl.ds(i * rows, rows)], sem)
        for i, sem in enumerate(sems.at[j] for j in range(sems.shape[0]))
    ]
    for c in copies:
        c.start()
    for c in copies:
        c.wait()


def terms_kernel(combine, near_terms, far_terms):
    slots = combine.shape[0] // 2
    same = (iota((slots, slots), 0) == iota((slots, slots), 1)).astype(jnp.float32)
    for start, out in ((0, near_terms), (slots, far_terms)):
        rest = combine[pl.ds(start, slots), :]
        terms = []
        for _ in range(3):
            term = rest.astype(jnp.bfloat16).astype(jnp.float32)
            rest = rest - term
            terms.append(
                lax.dot_general(
                    term, same, (((0,), (0,)), ((), ())), preferred_element_type=jnp.float32
                )
            )
        out[...] = jnp.concatenate(terms, axis=0).astype(jnp.bfloat16)


def stack_kernel(count, *refs):
    refs[-1][...] = stack(refs[:count]).astype(jnp.bfloat16)


def expert_kernel(count, *refs):
    blocks, (w_in, w_out), outs = refs[:count], refs[count : count + 2], refs[count + 2 :]
    rows = stack(blocks).astype(jnp.bfloat16)
    gate = jnp.dot(rows, w_in[0], preferred_element_type=jnp.float32)
    upper = jnp.dot(rows, w_in[1], preferred_element_type=jnp.float32)
    hidden = (gate / (1.0 + jnp.exp(-gate)) * upper).astype(jnp.bfloat16)
    unstack(jnp.dot(hidden, w_out[...], preferred_element_type=jnp.float32), outs)


def sum_kernel(count, *refs):
    total = refs[0][...].astype(jnp.float32)
    for r in refs[1:count]:
        total = total + r[...].astype(jnp.float32)
    unstack(total, refs[count:])


def combined(terms, parts, rows):
    values = stack(parts).astype(jnp.bfloat16)
    product = jnp.dot(terms[...], values, preferred_element_type=jnp.float32)
    return product[2 * rows :] + product[rows : 2 * rows] + product[:rows]


def near_kernel(terms, *refs):
    refs[-1][...] = combined(terms, refs[:-1], refs[-1].shape[0])


def far_kernel(terms, near, *refs):
    total = near[...] + combined(terms, refs[:-1], refs[-1].shape[0])
    refs[-1][...] = total.astype(jnp.bfloat16)


def call(kernel, inputs, in_specs, outs, limit, scratch=(), moved=0):
    return pl.pallas_call(
        kernel,
        out_shape=outs,
        in_specs=in_specs,
        out_specs=jax.tree.map(lambda _: VMEM, outs),
        scratch_shapes=scratch,
        compiler_params=pltpu.CompilerParams(vmem_limit_bytes=limit),
        cost_estimate=pl.CostEstimate(flops=0, bytes_accessed=moved, transcendentals=0)
        if moved
        else None,
    )(*inputs)


def body(tokens, expert_ids, gate_weights, replica_pick, placement, w_in, w_out):
    n_devices = lax.axis_size("expert")
    group_size = min(8, n_devices // 4)
    slot_count = n_devices // group_size
    tok_count, width = tokens.shape
    capacity = tok_count * expert_ids.shape[1] // slot_count
    slots = slot_count * capacity
    offsets = [*range(slot_count // 2, slot_count), *range(1, slot_count // 2), 0]
    bf16 = jnp.bfloat16
    chunk = jax.ShapeDtypeStruct((capacity, width), bf16)
    half = jax.ShapeDtypeStruct((slots // 2, width), bf16)

    def swap(value, offset):
        return lax.ppermute(value, "expert", [(e, e ^ offset) for e in range(n_devices)])

    def local(kernel, inputs, outs, limit=16 * MIB):
        return call(kernel, inputs, [VMEM] * len(inputs), outs, limit)

    def in_hbm(*arrays):
        return [pltpu.with_memory_space_constraint(a, pltpu.HBM) for a in arrays]

    sources = in_hbm(placement, expert_ids.T, replica_pick.T, gate_weights.T, tokens)
    *chunks, combine = call(
        functools.partial(route_kernel, group_size, slot_count),
        sources,
        [HBM] * 5,
        [chunk] * slot_count + [jax.ShapeDtypeStruct((slots, tok_count), jnp.float32)],
        16 * MIB,
        [pltpu.SMEM(placement.shape, jnp.int32)]
        + [pltpu.VMEM(s.shape, s.dtype) for s in sources[1:]]
        + [pltpu.SemaphoreType.DMA((5,))],
    )
    chunks = [swap(c, d * group_size) if d else c for d, c in zip(offsets, chunks)]
    terms = jax.ShapeDtypeStruct((3 * tok_count, slots // 2), bf16)
    terms = local(terms_kernel, [combine], [terms, terms])

    def fetch(array, after):
        return call(
            fetch_kernel,
            (*in_hbm(array), after),
            [HBM, VMEM],
            jax.ShapeDtypeStruct(array.shape, bf16),
            16 * MIB,
            [pltpu.SemaphoreType.DMA((2,))],
            2 * array.size,
        )

    w_in = fetch(w_in, terms[0])
    w_out = fetch(w_out, terms[1])

    square = group_size == 4
    count = slot_count // 2
    sides = ((1, 2), (2, 1))
    earlier = [w_in]
    summed = []
    for h in range(2):
        a, b = sides[h]
        own = local(
            functools.partial(stack_kernel, count), chunks[h * count :][:count] + earlier, half
        )
        if square:
            held = {a: swap(own, a), b: swap(own, b)}
            held = [own, held[a], held[b], swap(held[a], b)]
        else:
            held = [swap(own, q) if q else own for q in range(group_size)]
        earlier = []
        result = local(
            functools.partial(expert_kernel, group_size),
            held + [w_in, w_out],
            [half] * group_size,
            40 * MIB,
        )
        if square:
            mine, first, second, cross = result
            cross = swap(cross, a)
            first = swap(first, a)
            second = local(functools.partial(sum_kernel, 2), [second, cross], [half])[0]
            result = [mine, first, swap(second, b)]
        else:
            result = [swap(v, q) if q else v for q, v in enumerate(result)]
        summed += local(functools.partial(sum_kernel, len(result)), result, [chunk] * count)
    summed = [swap(v, d * group_size) if d else v for d, v in zip(offsets, summed)]
    near = local(
        near_kernel,
        [terms[0]] + summed[:count],
        jax.ShapeDtypeStruct((tok_count, width), jnp.float32),
    )
    return local(
        far_kernel,
        [terms[1], near] + summed[count:],
        jax.ShapeDtypeStruct((tok_count, width), bf16),
    )


def solution(mesh):
    in_specs = (
        P(("dp", "expert"), None),
        P(("dp", "expert"), None),
        P(("dp", "expert"), None),
        P(("dp", "expert"), None),
        P(),
        P(None, None, "expert"),
        P("expert", None),
    )
    out_specs = P(("dp", "expert"), None)
    return jax.shard_map(body, mesh=mesh, in_specs=in_specs, out_specs=out_specs, check_vma=False)
```

```python
import functools

import jax
import jax.numpy as jnp
from jax import lax
from jax.experimental import pallas as pl
from jax.experimental.pallas import tpu as pltpu
from jax.sharding import PartitionSpec as P

VMEM = pl.BlockSpec(memory_space=pltpu.VMEM)
HBM = pl.BlockSpec(memory_space=pltpu.HBM)
MIB = 1 << 20


def iota(shape, axis):
    return lax.broadcasted_iota(jnp.int32, shape, axis)


def stack(refs):
    return jnp.concatenate([r[...].astype(jnp.float32) for r in refs], axis=0)


def unstack(value, outs):
    start = 0
    for out in outs:
        out[...] = value[start : start + out.shape[0]].astype(out.dtype)
        start += out.shape[0]


def route_kernel(group_size, slot_count, *refs):
    sources, refs = refs[:5], refs[5:]
    row_outs, combine_out, refs = refs[:slot_count], refs[slot_count], refs[slot_count + 1 :]
    scratch, sems = refs[:5], refs[5]
    copies_in = [
        pltpu.make_async_copy(s, t, sems.at[i]) for i, (s, t) in enumerate(zip(sources, scratch))
    ]
    for c in copies_in:
        c.start()
    placement, expert_ids, replica_pick, gate_weights, tokens = scratch
    capacity = row_outs[0].shape[0]
    top_count, tok_count = expert_ids.shape
    own = lax.axis_index("expert") // group_size
    copy_row = iota((slot_count, tok_count), 0)
    named = jnp.zeros_like(copy_row)
    before = jnp.zeros_like(copy_row)
    relative = jnp.zeros_like(copy_row)
    for c in copies_in[:4]:
        c.wait()
    for p in range(slot_count):
        here = copy_row == p
        named = jnp.where(here, placement[p], named)
        d = lax.bitwise_xor(own, p)
        near = jnp.where(d == 0, slot_count - 1, d + slot_count // 2 - 1)
        place = jnp.where(d < slot_count // 2, near, d - slot_count // 2)
        relative = jnp.where(here, place, relative)
        seen = jnp.int32(0)
        for q in range(p):
            seen = seen + (placement[q] == placement[p]).astype(jnp.int32)
        before = jnp.where(here, seen, before)
    chosen = []
    for k in range(top_count):
        matches = named == expert_ids[pl.ds(k, 1), :]
        copies = jnp.sum(matches.astype(jnp.int32), axis=0, keepdims=True)
        pick = replica_pick[pl.ds(k, 1), :]
        wanted = jnp.where(pick >= copies, pick - copies, pick)
        chosen.append((matches & (before == wanted)).astype(jnp.int32))
    total = sum(chosen[1:], chosen[0])
    ahead = (iota((tok_count, tok_count), 0) < iota((tok_count, tok_count), 1)).astype(jnp.bfloat16)
    earlier = jnp.dot(
        total.astype(jnp.bfloat16), ahead, preferred_element_type=jnp.float32
    ).astype(jnp.int32)
    slot_row = iota((slot_count * capacity, tok_count), 0)
    pick_rows = jnp.zeros((slot_count * capacity, tok_count), jnp.float32)
    combine = jnp.zeros((slot_count * capacity, tok_count), jnp.float32)
    for k in range(top_count):
        rank = jnp.sum(chosen[k] * earlier, axis=0, keepdims=True)
        place = jnp.sum(chosen[k] * relative, axis=0, keepdims=True)
        slot = jnp.where(rank < capacity, place * capacity + rank, -1)
        hot = slot_row == slot
        pick_rows = pick_rows + hot.astype(jnp.float32)
        combine = combine + jnp.where(hot, gate_weights[pl.ds(k, 1), :], 0.0)
        earlier = earlier + chosen[k]
    combine_out[...] = combine
    copies_in[4].wait()
    rows = jnp.dot(pick_rows.astype(jnp.bfloat16), tokens[...], preferred_element_type=jnp.float32)
    unstack(rows, row_outs)


def fetch_kernel(*refs):
    source, held, sems = refs[0], refs[-2], refs[-1]
    rows = held.shape[0] // sems.shape[0]
    copies = [
        pltpu.make_async_copy(source.at[pl.ds(i * rows, rows)], held.at[pl.ds(i * rows, rows)], sem)
        for i, sem in enumerate(sems.at[j] for j in range(sems.shape[0]))
    ]
    for c in copies:
        c.start()
    for c in copies:
        c.wait()


def terms_kernel(combine, near_terms, far_terms):
    slots = combine.shape[0] // 2
    same = (iota((slots, slots), 0) == iota((slots, slots), 1)).astype(jnp.float32)
    for start, out in ((0, near_terms), (slots, far_terms)):
        rest = combine[pl.ds(start, slots), :]
        terms = []
        for _ in range(3):
            term = rest.astype(jnp.bfloat16).astype(jnp.float32)
            rest = rest - term
            terms.append(
                lax.dot_general(
                    term, same, (((0,), (0,)), ((), ())), preferred_element_type=jnp.float32
                )
            )
        out[...] = jnp.concatenate(terms, axis=0).astype(jnp.bfloat16)


def stack_kernel(count, *refs):
    refs[-1][...] = stack(refs[:count]).astype(jnp.bfloat16)


def expert_kernel(count, *refs):
    blocks, (w_in, w_out), outs = refs[:count], refs[count : count + 2], refs[count + 2 :]
    rows = stack(blocks).astype(jnp.bfloat16)
    gate = jnp.dot(rows, w_in[0], preferred_element_type=jnp.float32)
    upper = jnp.dot(rows, w_in[1], preferred_element_type=jnp.float32)
    hidden = (gate / (1.0 + jnp.exp(-gate)) * upper).astype(jnp.bfloat16)
    unstack(jnp.dot(hidden, w_out[...], preferred_element_type=jnp.float32), outs)


def sum_kernel(count, *refs):
    total = refs[0][...].astype(jnp.float32)
    for r in refs[1:count]:
        total = total + r[...].astype(jnp.float32)
    unstack(total, refs[count:])


def combined(terms, parts, rows):
    values = stack(parts).astype(jnp.bfloat16)
    product = jnp.dot(terms[...], values, preferred_element_type=jnp.float32)
    return product[2 * rows :] + product[rows : 2 * rows] + product[:rows]


def near_kernel(terms, *refs):
    refs[-1][...] = combined(terms, refs[:-1], refs[-1].shape[0])


def far_kernel(terms, near, *refs):
    total = near[...] + combined(terms, refs[:-1], refs[-1].shape[0])
    refs[-1][...] = total.astype(jnp.bfloat16)


def call(kernel, inputs, in_specs, outs, limit, scratch=(), moved=0):
    return pl.pallas_call(
        kernel,
        out_shape=outs,
        in_specs=in_specs,
        out_specs=jax.tree.map(lambda _: VMEM, outs),
        scratch_shapes=scratch,
        compiler_params=pltpu.CompilerParams(vmem_limit_bytes=limit),
        cost_estimate=pl.CostEstimate(flops=0, bytes_accessed=moved, transcendentals=0)
        if moved
        else None,
    )(*inputs)


def body(tokens, expert_ids, gate_weights, replica_pick, placement, w_in, w_out):
    n_devices = lax.axis_size("expert")
    group_size = min(8, n_devices // 4)
    slot_count = n_devices // group_size
    tok_count, width = tokens.shape
    capacity = tok_count * expert_ids.shape[1] // slot_count
    slots = slot_count * capacity
    offsets = [*range(slot_count // 2, slot_count), *range(1, slot_count // 2), 0]
    bf16 = jnp.bfloat16
    chunk = jax.ShapeDtypeStruct((capacity, width), bf16)
    half = jax.ShapeDtypeStruct((slots // 2, width), bf16)

    def swap(value, offset):
        return lax.ppermute(value, "expert", [(e, e ^ offset) for e in range(n_devices)])

    def turn(value, even, odd):
        parts = lax.axis_size("dp")
        pairs = [
            (e * parts + part, (e ^ (odd if part % 2 else even)) * parts + part)
            for e in range(n_devices)
            for part in range(parts)
        ]
        return lax.ppermute(value, ("expert", "dp"), pairs)

    def local(kernel, inputs, outs, limit=16 * MIB):
        return call(kernel, inputs, [VMEM] * len(inputs), outs, limit)

    def in_hbm(*arrays):
        return [pltpu.with_memory_space_constraint(a, pltpu.HBM) for a in arrays]

    sources = in_hbm(placement, expert_ids.T, replica_pick.T, gate_weights.T, tokens)
    *chunks, combine = call(
        functools.partial(route_kernel, group_size, slot_count),
        sources,
        [HBM] * 5,
        [chunk] * slot_count + [jax.ShapeDtypeStruct((slots, tok_count), jnp.float32)],
        16 * MIB,
        [pltpu.SMEM(placement.shape, jnp.int32)]
        + [pltpu.VMEM(s.shape, s.dtype) for s in sources[1:]]
        + [pltpu.SemaphoreType.DMA((5,))],
    )
    chunks = [swap(c, d * group_size) if d else c for d, c in zip(offsets, chunks)]
    terms = jax.ShapeDtypeStruct((3 * tok_count, slots // 2), bf16)
    terms = local(terms_kernel, [combine], [terms, terms])

    def fetch(array, after):
        return call(
            fetch_kernel,
            (*in_hbm(array), after),
            [HBM, VMEM],
            jax.ShapeDtypeStruct(array.shape, bf16),
            16 * MIB,
            [pltpu.SemaphoreType.DMA((2,))],
            2 * array.size,
        )

    w_in = fetch(w_in, terms[0])
    w_out = fetch(w_out, terms[1])

    square = group_size == 4
    count = slot_count // 2
    sides = ((1, 2), (2, 1))
    earlier = [w_in]
    summed = []
    for h in range(2):
        a, b = sides[h]
        own = local(
            functools.partial(stack_kernel, count), chunks[h * count :][:count] + earlier, half
        )
        if square:
            first = turn(own, a, b)
            held = [own, first, turn(own, b, a), turn(first, b, a)]
        else:
            held = [swap(own, q) if q else own for q in range(group_size)]
        earlier = []
        result = local(
            functools.partial(expert_kernel, group_size),
            held + [w_in, w_out],
            [half] * group_size,
            40 * MIB,
        )
        if square:
            mine, first, second, cross = result
            cross = turn(cross, a, b)
            first = turn(first, a, b)
            second = local(functools.partial(sum_kernel, 2), [second, cross], [half])[0]
            result = [mine, first, turn(second, b, a)]
        else:
            result = [swap(v, q) if q else v for q, v in enumerate(result)]
        summed += local(functools.partial(sum_kernel, len(result)), result, [chunk] * count)
    summed = [swap(v, d * group_size) if d else v for d, v in zip(offsets, summed)]
    near = local(
        near_kernel,
        [terms[0]] + summed[:count],
        jax.ShapeDtypeStruct((tok_count, width), jnp.float32),
    )
    return local(
        far_kernel,
        [terms[1], near] + summed[count:],
        jax.ShapeDtypeStruct((tok_count, width), bf16),
    )


def solution(mesh):
    in_specs = (
        P(("dp", "expert"), None),
        P(("dp", "expert"), None),
        P(("dp", "expert"), None),
        P(("dp", "expert"), None),
        P(),
        P(None, None, "expert"),
        P("expert", None),
    )
    out_specs = P(("dp", "expert"), None)
    return jax.shard_map(body, mesh=mesh, in_specs=in_specs, out_specs=out_specs, check_vma=False)
```

```python
import functools

import jax
import jax.numpy as jnp
from jax import lax
from jax.experimental import pallas as pl
from jax.experimental.pallas import tpu as pltpu
from jax.sharding import PartitionSpec as P

VMEM = pl.BlockSpec(memory_space=pltpu.VMEM)
HBM = pl.BlockSpec(memory_space=pltpu.HBM)
MIB = 1 << 20


def iota(shape, axis):
    return lax.broadcasted_iota(jnp.int32, shape, axis)


def stack(refs):
    return jnp.concatenate([r[...].astype(jnp.float32) for r in refs], axis=0)


def unstack(value, outs):
    start = 0
    for out in outs:
        out[...] = value[start : start + out.shape[0]].astype(out.dtype)
        start += out.shape[0]


def route_kernel(group_size, slot_count, *refs):
    sources, refs = refs[:5], refs[5:]
    row_outs, combine_out, refs = refs[:slot_count], refs[slot_count], refs[slot_count + 1 :]
    scratch, sems = refs[:5], refs[5]
    copies_in = [
        pltpu.make_async_copy(s, t, sems.at[i]) for i, (s, t) in enumerate(zip(sources, scratch))
    ]
    for c in copies_in:
        c.start()
    placement, expert_ids, replica_pick, gate_weights, tokens = scratch
    capacity = row_outs[0].shape[0]
    top_count, tok_count = expert_ids.shape
    own = lax.axis_index("expert") // group_size
    copy_row = iota((slot_count, tok_count), 0)
    named = jnp.zeros_like(copy_row)
    before = jnp.zeros_like(copy_row)
    relative = jnp.zeros_like(copy_row)
    for c in copies_in[:4]:
        c.wait()
    for p in range(slot_count):
        here = copy_row == p
        named = jnp.where(here, placement[p], named)
        d = lax.bitwise_xor(own, p)
        relative = jnp.where(here, slot_count - 1 - d, relative)
        seen = jnp.int32(0)
        for q in range(p):
            seen = seen + (placement[q] == placement[p]).astype(jnp.int32)
        before = jnp.where(here, seen, before)
    chosen = []
    for k in range(top_count):
        matches = named == expert_ids[pl.ds(k, 1), :]
        copies = jnp.sum(matches.astype(jnp.int32), axis=0, keepdims=True)
        pick = replica_pick[pl.ds(k, 1), :]
        wanted = jnp.where(pick >= copies, pick - copies, pick)
        chosen.append((matches & (before == wanted)).astype(jnp.int32))
    total = sum(chosen[1:], chosen[0])
    ahead = (iota((tok_count, tok_count), 0) < iota((tok_count, tok_count), 1)).astype(jnp.bfloat16)
    earlier = jnp.dot(
        total.astype(jnp.bfloat16), ahead, preferred_element_type=jnp.float32
    ).astype(jnp.int32)
    slot_row = iota((slot_count * capacity, tok_count), 0)
    pick_rows = jnp.zeros((slot_count * capacity, tok_count), jnp.float32)
    combine = jnp.zeros((slot_count * capacity, tok_count), jnp.float32)
    for k in range(top_count):
        rank = jnp.sum(chosen[k] * earlier, axis=0, keepdims=True)
        place = jnp.sum(chosen[k] * relative, axis=0, keepdims=True)
        slot = jnp.where(rank < capacity, place * capacity + rank, -1)
        hot = slot_row == slot
        pick_rows = pick_rows + hot.astype(jnp.float32)
        combine = combine + jnp.where(hot, gate_weights[pl.ds(k, 1), :], 0.0)
        earlier = earlier + chosen[k]
    combine_out[...] = combine
    copies_in[4].wait()
    rows = jnp.dot(pick_rows.astype(jnp.bfloat16), tokens[...], preferred_element_type=jnp.float32)
    unstack(rows, row_outs)


def fetch_kernel(*refs):
    source, held, sems = refs[0], refs[-2], refs[-1]
    rows = held.shape[0] // sems.shape[0]
    copies = [
        pltpu.make_async_copy(source.at[pl.ds(i * rows, rows)], held.at[pl.ds(i * rows, rows)], sem)
        for i, sem in enumerate(sems.at[j] for j in range(sems.shape[0]))
    ]
    for c in copies:
        c.start()
    for c in copies:
        c.wait()


def terms_kernel(combine, near_terms, far_terms):
    slots = combine.shape[0] // 2
    same = (iota((slots, slots), 0) == iota((slots, slots), 1)).astype(jnp.float32)
    for start, out in ((0, near_terms), (slots, far_terms)):
        rest = combine[pl.ds(start, slots), :]
        terms = []
        for _ in range(3):
            term = rest.astype(jnp.bfloat16).astype(jnp.float32)
            rest = rest - term
            terms.append(
                lax.dot_general(
                    term, same, (((0,), (0,)), ((), ())), preferred_element_type=jnp.float32
                )
            )
        out[...] = jnp.concatenate(terms, axis=0).astype(jnp.bfloat16)


def stack_kernel(count, *refs):
    refs[-1][...] = stack(refs[:count]).astype(jnp.bfloat16)


def expert_kernel(count, *refs):
    blocks, (w_in, w_out), outs = refs[:count], refs[count : count + 2], refs[count + 2 :]
    rows = stack(blocks).astype(jnp.bfloat16)
    gate = jnp.dot(rows, w_in[0], preferred_element_type=jnp.float32)
    upper = jnp.dot(rows, w_in[1], preferred_element_type=jnp.float32)
    hidden = (gate / (1.0 + jnp.exp(-gate)) * upper).astype(jnp.bfloat16)
    unstack(jnp.dot(hidden, w_out[...], preferred_element_type=jnp.float32), outs)


def sum_kernel(count, *refs):
    total = refs[0][...].astype(jnp.float32)
    for r in refs[1:count]:
        total = total + r[...].astype(jnp.float32)
    unstack(total, refs[count:])


def combined(terms, parts, rows):
    values = stack(parts).astype(jnp.bfloat16)
    product = jnp.dot(terms[...], values, preferred_element_type=jnp.float32)
    return product[2 * rows :] + product[rows : 2 * rows] + product[:rows]


def near_kernel(terms, *refs):
    refs[-1][...] = combined(terms, refs[:-1], refs[-1].shape[0])


def far_kernel(terms, near, *refs):
    total = near[...] + combined(terms, refs[:-1], refs[-1].shape[0])
    refs[-1][...] = total.astype(jnp.bfloat16)


def call(kernel, inputs, in_specs, outs, limit, scratch=(), moved=0):
    return pl.pallas_call(
        kernel,
        out_shape=outs,
        in_specs=in_specs,
        out_specs=jax.tree.map(lambda _: VMEM, outs),
        scratch_shapes=scratch,
        compiler_params=pltpu.CompilerParams(vmem_limit_bytes=limit),
        cost_estimate=pl.CostEstimate(flops=0, bytes_accessed=moved, transcendentals=0)
        if moved
        else None,
    )(*inputs)


def body(tokens, expert_ids, gate_weights, replica_pick, placement, w_in, w_out):
    n_devices = lax.axis_size("expert")
    group_size = min(8, n_devices // 4)
    slot_count = n_devices // group_size
    tok_count, width = tokens.shape
    capacity = tok_count * expert_ids.shape[1] // slot_count
    slots = slot_count * capacity
    offsets = range(slot_count - 1, -1, -1)
    bf16 = jnp.bfloat16
    chunk = jax.ShapeDtypeStruct((capacity, width), bf16)
    half = jax.ShapeDtypeStruct((slots // 2, width), bf16)

    def swap(value, offset):
        return lax.ppermute(value, "expert", [(e, e ^ offset) for e in range(n_devices)])

    def local(kernel, inputs, outs, limit=16 * MIB):
        return call(kernel, inputs, [VMEM] * len(inputs), outs, limit)

    def in_hbm(*arrays):
        return [pltpu.with_memory_space_constraint(a, pltpu.HBM) for a in arrays]

    sources = in_hbm(placement, expert_ids.T, replica_pick.T, gate_weights.T, tokens)
    *chunks, combine = call(
        functools.partial(route_kernel, group_size, slot_count),
        sources,
        [HBM] * 5,
        [chunk] * slot_count + [jax.ShapeDtypeStruct((slots, tok_count), jnp.float32)],
        16 * MIB,
        [pltpu.SMEM(placement.shape, jnp.int32)]
        + [pltpu.VMEM(s.shape, s.dtype) for s in sources[1:]]
        + [pltpu.SemaphoreType.DMA((5,))],
    )
    chunks = [swap(c, d * group_size) if d else c for d, c in zip(offsets, chunks)]
    terms = jax.ShapeDtypeStruct((3 * tok_count, slots // 2), bf16)
    terms = local(terms_kernel, [combine], [terms, terms])

    def fetch(array, after):
        return call(
            fetch_kernel,
            (*in_hbm(array), after),
            [HBM, VMEM],
            jax.ShapeDtypeStruct(array.shape, bf16),
            16 * MIB,
            [pltpu.SemaphoreType.DMA((2,))],
            2 * array.size,
        )

    w_in = fetch(w_in, terms[0])
    w_out = fetch(w_out, terms[1])

    square = group_size == 4
    count = slot_count // 2
    sides = ((1, 2), (2, 1))
    earlier = [w_in]
    summed = []
    for h in range(2):
        a, b = sides[h]
        own = local(
            functools.partial(stack_kernel, count), chunks[h * count :][:count] + earlier, half
        )
        if square:
            held = {a: swap(own, a), b: swap(own, b)}
            held = [own, held[a], held[b], swap(held[a], b)]
        else:
            held = [swap(own, q) if q else own for q in range(group_size)]
        earlier = []
        result = local(
            functools.partial(expert_kernel, group_size),
            held + [w_in, w_out],
            [half] * group_size,
            40 * MIB,
        )
        if square:
            mine, first, second, cross = result
            cross = swap(cross, a)
            first = swap(first, a)
            second = local(functools.partial(sum_kernel, 2), [second, cross], [half])[0]
            result = [mine, first, swap(second, b)]
        else:
            result = [swap(v, q) if q else v for q, v in enumerate(result)]
        summed += local(functools.partial(sum_kernel, len(result)), result, [chunk] * count)
    summed = [swap(v, d * group_size) if d else v for d, v in zip(offsets, summed)]
    near = local(
        near_kernel,
        [terms[0]] + summed[:count],
        jax.ShapeDtypeStruct((tok_count, width), jnp.float32),
    )
    return local(
        far_kernel,
        [terms[1], near] + summed[count:],
        jax.ShapeDtypeStruct((tok_count, width), bf16),
    )


def solution(mesh):
    in_specs = (
        P(("dp", "expert"), None),
        P(("dp", "expert"), None),
        P(("dp", "expert"), None),
        P(("dp", "expert"), None),
        P(),
        P(None, None, "expert"),
        P("expert", None),
    )
    out_specs = P(("dp", "expert"), None)
    return jax.shard_map(body, mesh=mesh, in_specs=in_specs, out_specs=out_specs, check_vma=False)
```

```python
import functools

import jax
import jax.numpy as jnp
from jax import lax
from jax.experimental import pallas as pl
from jax.experimental.pallas import tpu as pltpu
from jax.sharding import PartitionSpec as P

VMEM = pl.BlockSpec(memory_space=pltpu.VMEM)
HBM = pl.BlockSpec(memory_space=pltpu.HBM)
MIB = 1 << 20


def iota(shape, axis):
    return lax.broadcasted_iota(jnp.int32, shape, axis)


def stack(refs):
    return jnp.concatenate([r[...].astype(jnp.float32) for r in refs], axis=0)


def unstack(value, outs):
    start = 0
    for out in outs:
        out[...] = value[start : start + out.shape[0]].astype(out.dtype)
        start += out.shape[0]


def route_kernel(group_size, slot_count, *refs):
    sources, refs = refs[:5], refs[5:]
    row_outs, combine_out, refs = refs[:slot_count], refs[slot_count], refs[slot_count + 1 :]
    scratch, sems = refs[:5], refs[5]
    copies_in = [
        pltpu.make_async_copy(s, t, sems.at[i]) for i, (s, t) in enumerate(zip(sources, scratch))
    ]
    for c in copies_in:
        c.start()
    placement, expert_ids, replica_pick, gate_weights, tokens = scratch
    capacity = row_outs[0].shape[0]
    top_count, tok_count = expert_ids.shape
    own = lax.axis_index("expert") // group_size
    copy_row = iota((slot_count, tok_count), 0)
    named = jnp.zeros_like(copy_row)
    before = jnp.zeros_like(copy_row)
    relative = jnp.zeros_like(copy_row)
    for c in copies_in[:4]:
        c.wait()
    for p in range(slot_count):
        here = copy_row == p
        named = jnp.where(here, placement[p], named)
        d = lax.bitwise_xor(own, p)
        relative = jnp.where(here, slot_count - 1 - d, relative)
        seen = jnp.int32(0)
        for q in range(p):
            seen = seen + (placement[q] == placement[p]).astype(jnp.int32)
        before = jnp.where(here, seen, before)
    chosen = []
    for k in range(top_count):
        matches = named == expert_ids[pl.ds(k, 1), :]
        copies = jnp.sum(matches.astype(jnp.int32), axis=0, keepdims=True)
        pick = replica_pick[pl.ds(k, 1), :]
        wanted = jnp.where(pick >= copies, pick - copies, pick)
        chosen.append((matches & (before == wanted)).astype(jnp.int32))
    total = sum(chosen[1:], chosen[0])
    ahead = (iota((tok_count, tok_count), 0) < iota((tok_count, tok_count), 1)).astype(jnp.bfloat16)
    earlier = jnp.dot(
        total.astype(jnp.bfloat16), ahead, preferred_element_type=jnp.float32
    ).astype(jnp.int32)
    slot_row = iota((slot_count * capacity, tok_count), 0)
    pick_rows = jnp.zeros((slot_count * capacity, tok_count), jnp.float32)
    combine = jnp.zeros((slot_count * capacity, tok_count), jnp.float32)
    for k in range(top_count):
        rank = jnp.sum(chosen[k] * earlier, axis=0, keepdims=True)
        place = jnp.sum(chosen[k] * relative, axis=0, keepdims=True)
        slot = jnp.where(rank < capacity, place * capacity + rank, -1)
        hot = slot_row == slot
        pick_rows = pick_rows + hot.astype(jnp.float32)
        combine = combine + jnp.where(hot, gate_weights[pl.ds(k, 1), :], 0.0)
        earlier = earlier + chosen[k]
    combine_out[...] = combine
    copies_in[4].wait()
    rows = jnp.dot(pick_rows.astype(jnp.bfloat16), tokens[...], preferred_element_type=jnp.float32)
    unstack(rows, row_outs)


def fetch_kernel(*refs):
    source, held, sems = refs[0], refs[-2], refs[-1]
    rows = held.shape[0] // sems.shape[0]
    copies = [
        pltpu.make_async_copy(source.at[pl.ds(i * rows, rows)], held.at[pl.ds(i * rows, rows)], sem)
        for i, sem in enumerate(sems.at[j] for j in range(sems.shape[0]))
    ]
    for c in copies:
        c.start()
    for c in copies:
        c.wait()


def terms_kernel(combine, near_terms, far_terms):
    slots = combine.shape[0] // 2
    same = (iota((slots, slots), 0) == iota((slots, slots), 1)).astype(jnp.float32)
    for start, out in ((0, near_terms), (slots, far_terms)):
        rest = combine[pl.ds(start, slots), :]
        terms = []
        for _ in range(3):
            term = rest.astype(jnp.bfloat16).astype(jnp.float32)
            rest = rest - term
            terms.append(
                lax.dot_general(
                    term, same, (((0,), (0,)), ((), ())), preferred_element_type=jnp.float32
                )
            )
        out[...] = jnp.concatenate(terms, axis=0).astype(jnp.bfloat16)


def stack_kernel(count, *refs):
    refs[-1][...] = stack(refs[:count]).astype(jnp.bfloat16)


def expert_kernel(count, *refs):
    blocks, (w_in, w_out), outs = refs[:count], refs[count : count + 2], refs[count + 2 :]
    rows = stack(blocks).astype(jnp.bfloat16)
    gate = jnp.dot(rows, w_in[0], preferred_element_type=jnp.float32)
    upper = jnp.dot(rows, w_in[1], preferred_element_type=jnp.float32)
    hidden = (gate / (1.0 + jnp.exp(-gate)) * upper).astype(jnp.bfloat16)
    unstack(jnp.dot(hidden, w_out[...], preferred_element_type=jnp.float32), outs)


def sum_kernel(count, *refs):
    total = refs[0][...].astype(jnp.float32)
    for r in refs[1:count]:
        total = total + r[...].astype(jnp.float32)
    unstack(total, refs[count:])


def combined(terms, parts, rows):
    values = stack(parts).astype(jnp.bfloat16)
    product = jnp.dot(terms[...], values, preferred_element_type=jnp.float32)
    return product[2 * rows :] + product[rows : 2 * rows] + product[:rows]


def near_kernel(terms, *refs):
    refs[-1][...] = combined(terms, refs[:-1], refs[-1].shape[0])


def far_kernel(terms, near, *refs):
    total = near[...] + combined(terms, refs[:-1], refs[-1].shape[0])
    refs[-1][...] = total.astype(jnp.bfloat16)


def call(kernel, inputs, in_specs, outs, limit, scratch=(), moved=0):
    return pl.pallas_call(
        kernel,
        out_shape=outs,
        in_specs=in_specs,
        out_specs=jax.tree.map(lambda _: VMEM, outs),
        scratch_shapes=scratch,
        compiler_params=pltpu.CompilerParams(vmem_limit_bytes=limit),
        cost_estimate=pl.CostEstimate(flops=0, bytes_accessed=moved, transcendentals=0)
        if moved
        else None,
    )(*inputs)


def body(tokens, expert_ids, gate_weights, replica_pick, placement, w_in, w_out):
    n_devices = lax.axis_size("expert")
    group_size = min(8, n_devices // 4)
    slot_count = n_devices // group_size
    tok_count, width = tokens.shape
    capacity = tok_count * expert_ids.shape[1] // slot_count
    slots = slot_count * capacity
    offsets = range(slot_count - 1, -1, -1)
    bf16 = jnp.bfloat16
    chunk = jax.ShapeDtypeStruct((capacity, width), bf16)
    half = jax.ShapeDtypeStruct((slots // 2, width), bf16)

    def swap(value, offset):
        return lax.ppermute(value, "expert", [(e, e ^ offset) for e in range(n_devices)])

    def local(kernel, inputs, outs, limit=16 * MIB):
        return call(kernel, inputs, [VMEM] * len(inputs), outs, limit)

    def in_hbm(*arrays):
        return [pltpu.with_memory_space_constraint(a, pltpu.HBM) for a in arrays]

    sources = in_hbm(placement, expert_ids.T, replica_pick.T, gate_weights.T, tokens)
    *chunks, combine = call(
        functools.partial(route_kernel, group_size, slot_count),
        sources,
        [HBM] * 5,
        [chunk] * slot_count + [jax.ShapeDtypeStruct((slots, tok_count), jnp.float32)],
        16 * MIB,
        [pltpu.SMEM(placement.shape, jnp.int32)]
        + [pltpu.VMEM(s.shape, s.dtype) for s in sources[1:]]
        + [pltpu.SemaphoreType.DMA((5,))],
    )
    chunks = [swap(c, d * group_size) if d else c for d, c in zip(offsets, chunks)]
    terms = jax.ShapeDtypeStruct((3 * tok_count, slots // 2), bf16)
    terms = local(terms_kernel, [combine], [terms, terms])

    def fetch(array, after):
        return call(
            fetch_kernel,
            (*in_hbm(array), after),
            [HBM, VMEM],
            jax.ShapeDtypeStruct(array.shape, bf16),
            16 * MIB,
            [pltpu.SemaphoreType.DMA((2,))],
            2 * array.size,
        )

    w_in = fetch(w_in, terms[0])
    w_out = fetch(w_out, terms[1])

    square = group_size == 4
    count = slot_count // 2
    sides = ((1, 2), (2, 1))
    earlier = [w_in]
    summed = []
    for h in range(2):
        a, b = sides[h]
        own = local(
            functools.partial(stack_kernel, count), chunks[h * count :][:count] + earlier, half
        )
        if square:
            held = {a: swap(own, a), b: swap(own, b)}
            held = [own, held[a], held[b], swap(held[a], b)]
        else:
            held = [swap(own, q) if q else own for q in range(group_size)]
        earlier = []
        result = local(
            functools.partial(expert_kernel, group_size),
            held + [w_in, w_out],
            [half] * group_size,
            40 * MIB,
        )
        if square:
            mine, first, second, cross = result
            cross = swap(cross, b)
            second = swap(second, b)
            first = local(functools.partial(sum_kernel, 2), [first, cross], [half])[0]
            result = [mine, second, swap(first, a)]
        else:
            result = [swap(v, q) if q else v for q, v in enumerate(result)]
        summed += local(functools.partial(sum_kernel, len(result)), result, [chunk] * count)
    summed = [swap(v, d * group_size) if d else v for d, v in zip(offsets, summed)]
    near = local(
        near_kernel,
        [terms[0]] + summed[:count],
        jax.ShapeDtypeStruct((tok_count, width), jnp.float32),
    )
    return local(
        far_kernel,
        [terms[1], near] + summed[count:],
        jax.ShapeDtypeStruct((tok_count, width), bf16),
    )


def solution(mesh):
    in_specs = (
        P(("dp", "expert"), None),
        P(("dp", "expert"), None),
        P(("dp", "expert"), None),
        P(("dp", "expert"), None),
        P(),
        P(None, None, "expert"),
        P("expert", None),
    )
    out_specs = P(("dp", "expert"), None)
    return jax.shard_map(body, mesh=mesh, in_specs=in_specs, out_specs=out_specs, check_vma=False)
```

```python
import functools

import jax
import jax.numpy as jnp
from jax import lax
from jax.experimental import pallas as pl
from jax.experimental.pallas import tpu as pltpu
from jax.sharding import PartitionSpec as P

VMEM = pl.BlockSpec(memory_space=pltpu.VMEM)
HBM = pl.BlockSpec(memory_space=pltpu.HBM)
MIB = 1 << 20


def iota(shape, axis):
    return lax.broadcasted_iota(jnp.int32, shape, axis)


def stack(refs):
    return jnp.concatenate([r[...].astype(jnp.float32) for r in refs], axis=0)


def unstack(value, outs):
    start = 0
    for out in outs:
        out[...] = value[start : start + out.shape[0]].astype(out.dtype)
        start += out.shape[0]


def route_kernel(group_size, slot_count, *refs):
    sources, refs = refs[:5], refs[5:]
    row_outs, combine_out, refs = refs[:slot_count], refs[slot_count], refs[slot_count + 1 :]
    scratch, sems = refs[:5], refs[5]
    copies_in = [
        pltpu.make_async_copy(s, t, sems.at[i]) for i, (s, t) in enumerate(zip(sources, scratch))
    ]
    for c in copies_in:
        c.start()
    placement, expert_ids, replica_pick, gate_weights, tokens = scratch
    capacity = row_outs[0].shape[0]
    top_count, tok_count = expert_ids.shape
    own = lax.axis_index("expert") // group_size
    copy_row = iota((slot_count, tok_count), 0)
    named = jnp.zeros_like(copy_row)
    before = jnp.zeros_like(copy_row)
    relative = jnp.zeros_like(copy_row)
    for c in copies_in[:4]:
        c.wait()
    for p in range(slot_count):
        here = copy_row == p
        named = jnp.where(here, placement[p], named)
        d = lax.bitwise_xor(own, p)
        relative = jnp.where(here, slot_count - 1 - d, relative)
        seen = jnp.int32(0)
        for q in range(p):
            seen = seen + (placement[q] == placement[p]).astype(jnp.int32)
        before = jnp.where(here, seen, before)
    chosen = []
    for k in range(top_count):
        matches = named == expert_ids[pl.ds(k, 1), :]
        copies = jnp.sum(matches.astype(jnp.int32), axis=0, keepdims=True)
        pick = replica_pick[pl.ds(k, 1), :]
        wanted = jnp.where(pick >= copies, pick - copies, pick)
        chosen.append((matches & (before == wanted)).astype(jnp.int32))
    total = sum(chosen[1:], chosen[0])
    ahead = (iota((tok_count, tok_count), 0) < iota((tok_count, tok_count), 1)).astype(jnp.bfloat16)
    earlier = jnp.dot(
        total.astype(jnp.bfloat16), ahead, preferred_element_type=jnp.float32
    ).astype(jnp.int32)
    slot_row = iota((slot_count * capacity, tok_count), 0)
    pick_rows = jnp.zeros((slot_count * capacity, tok_count), jnp.float32)
    combine = jnp.zeros((slot_count * capacity, tok_count), jnp.float32)
    for k in range(top_count):
        rank = jnp.sum(chosen[k] * earlier, axis=0, keepdims=True)
        place = jnp.sum(chosen[k] * relative, axis=0, keepdims=True)
        slot = jnp.where(rank < capacity, place * capacity + rank, -1)
        hot = slot_row == slot
        pick_rows = pick_rows + hot.astype(jnp.float32)
        combine = combine + jnp.where(hot, gate_weights[pl.ds(k, 1), :], 0.0)
        earlier = earlier + chosen[k]
    combine_out[...] = combine
    copies_in[4].wait()
    rows = jnp.dot(pick_rows.astype(jnp.bfloat16), tokens[...], preferred_element_type=jnp.float32)
    unstack(rows, row_outs)


def fetch_kernel(*refs):
    source, held, sems = refs[0], refs[-2], refs[-1]
    rows = held.shape[0] // sems.shape[0]
    copies = [
        pltpu.make_async_copy(source.at[pl.ds(i * rows, rows)], held.at[pl.ds(i * rows, rows)], sem)
        for i, sem in enumerate(sems.at[j] for j in range(sems.shape[0]))
    ]
    for c in copies:
        c.start()
    for c in copies:
        c.wait()


def terms_kernel(combine, near_terms, far_terms):
    slots = combine.shape[0] // 2
    same = (iota((slots, slots), 0) == iota((slots, slots), 1)).astype(jnp.float32)
    for start, out in ((0, near_terms), (slots, far_terms)):
        rest = combine[pl.ds(start, slots), :]
        terms = []
        for _ in range(3):
            term = rest.astype(jnp.bfloat16).astype(jnp.float32)
            rest = rest - term
            terms.append(
                lax.dot_general(
                    term, same, (((0,), (0,)), ((), ())), preferred_element_type=jnp.float32
                )
            )
        out[...] = jnp.concatenate(terms, axis=0).astype(jnp.bfloat16)


def stack_kernel(count, *refs):
    refs[-1][...] = stack(refs[:count]).astype(jnp.bfloat16)


def expert_kernel(count, *refs):
    blocks, (w_in, w_out), outs = refs[:count], refs[count : count + 2], refs[count + 2 :]
    rows = stack(blocks).astype(jnp.bfloat16)
    gate = jnp.dot(rows, w_in[0], preferred_element_type=jnp.float32)
    upper = jnp.dot(rows, w_in[1], preferred_element_type=jnp.float32)
    hidden = (gate / (1.0 + jnp.exp(-gate)) * upper).astype(jnp.bfloat16)
    unstack(jnp.dot(hidden, w_out[...], preferred_element_type=jnp.float32), outs)


def sum_kernel(count, *refs):
    total = refs[0][...].astype(jnp.float32)
    for r in refs[1:count]:
        total = total + r[...].astype(jnp.float32)
    unstack(total, refs[count:])


def combined(terms, parts, rows):
    values = stack(parts).astype(jnp.bfloat16)
    product = jnp.dot(terms[...], values, preferred_element_type=jnp.float32)
    return product[2 * rows :] + product[rows : 2 * rows] + product[:rows]


def near_kernel(terms, *refs):
    refs[-1][...] = combined(terms, refs[:-1], refs[-1].shape[0])


def far_kernel(terms, near, *refs):
    total = near[...] + combined(terms, refs[:-1], refs[-1].shape[0])
    refs[-1][...] = total.astype(jnp.bfloat16)


def call(kernel, inputs, in_specs, outs, limit, scratch=(), moved=0):
    return pl.pallas_call(
        kernel,
        out_shape=outs,
        in_specs=in_specs,
        out_specs=jax.tree.map(lambda _: VMEM, outs),
        scratch_shapes=scratch,
        compiler_params=pltpu.CompilerParams(vmem_limit_bytes=limit),
        cost_estimate=pl.CostEstimate(flops=0, bytes_accessed=moved, transcendentals=0)
        if moved
        else None,
    )(*inputs)


def body(tokens, expert_ids, gate_weights, replica_pick, placement, w_in, w_out):
    n_devices = lax.axis_size("expert")
    group_size = min(8, n_devices // 4)
    slot_count = n_devices // group_size
    tok_count, width = tokens.shape
    capacity = tok_count * expert_ids.shape[1] // slot_count
    slots = slot_count * capacity
    offsets = range(slot_count - 1, -1, -1)
    bf16 = jnp.bfloat16
    chunk = jax.ShapeDtypeStruct((capacity, width), bf16)
    half = jax.ShapeDtypeStruct((slots // 2, width), bf16)

    def swap(value, offset):
        return lax.ppermute(value, "expert", [(e, e ^ offset) for e in range(n_devices)])

    def local(kernel, inputs, outs, limit=16 * MIB):
        return call(kernel, inputs, [VMEM] * len(inputs), outs, limit)

    def in_hbm(*arrays):
        return [pltpu.with_memory_space_constraint(a, pltpu.HBM) for a in arrays]

    sources = in_hbm(placement, expert_ids.T, replica_pick.T, gate_weights.T, tokens)
    *chunks, combine = call(
        functools.partial(route_kernel, group_size, slot_count),
        sources,
        [HBM] * 5,
        [chunk] * slot_count + [jax.ShapeDtypeStruct((slots, tok_count), jnp.float32)],
        16 * MIB,
        [pltpu.SMEM(placement.shape, jnp.int32)]
        + [pltpu.VMEM(s.shape, s.dtype) for s in sources[1:]]
        + [pltpu.SemaphoreType.DMA((5,))],
    )
    chunks = [swap(c, d * group_size) if d else c for d, c in zip(offsets, chunks)]
    terms = jax.ShapeDtypeStruct((3 * tok_count, slots // 2), bf16)
    terms = local(terms_kernel, [combine], [terms, terms])

    def fetch(array, after):
        return call(
            fetch_kernel,
            (*in_hbm(array), after),
            [HBM, VMEM],
            jax.ShapeDtypeStruct(array.shape, bf16),
            16 * MIB,
            [pltpu.SemaphoreType.DMA((2,))],
            2 * array.size,
        )

    w_in = fetch(w_in, terms[0])
    w_out = fetch(w_out, terms[1])

    square = group_size == 4
    count = slot_count // 2
    sides = ((1, 2), (2, 1))
    earlier = [w_in]
    summed = []
    for h in range(2):
        a, b = sides[h]
        own = local(
            functools.partial(stack_kernel, count), chunks[h * count :][:count] + earlier, half
        )
        if square:
            held = {a: swap(own, a), b: swap(own, b)}
            cross = swap(own, 3) if h == 0 else swap(held[a], b)
            held = [own, held[a], held[b], cross]
        else:
            held = [swap(own, q) if q else own for q in range(group_size)]
        earlier = [own]
        result = local(
            functools.partial(expert_kernel, group_size),
            held + [w_in, w_out],
            [half] * group_size,
            40 * MIB,
        )
        if square:
            mine, first, second, cross = result
            cross = swap(cross, b)
            second = swap(second, b)
            first = local(functools.partial(sum_kernel, 2), [first, cross], [half])[0]
            result = [mine, second, swap(first, a)]
        else:
            result = [swap(v, q) if q else v for q, v in enumerate(result)]
        summed += local(functools.partial(sum_kernel, len(result)), result, [chunk] * count)
    summed = [swap(v, d * group_size) if d else v for d, v in zip(offsets, summed)]
    near = local(
        near_kernel,
        [terms[0]] + summed[:count],
        jax.ShapeDtypeStruct((tok_count, width), jnp.float32),
    )
    return local(
        far_kernel,
        [terms[1], near] + summed[count:],
        jax.ShapeDtypeStruct((tok_count, width), bf16),
    )


def solution(mesh):
    in_specs = (
        P(("dp", "expert"), None),
        P(("dp", "expert"), None),
        P(("dp", "expert"), None),
        P(("dp", "expert"), None),
        P(),
        P(None, None, "expert"),
        P("expert", None),
    )
    out_specs = P(("dp", "expert"), None)
    return jax.shard_map(body, mesh=mesh, in_specs=in_specs, out_specs=out_specs, check_vma=False)
```

```python
import functools

import jax
import jax.numpy as jnp
from jax import lax
from jax.experimental import pallas as pl
from jax.experimental.pallas import tpu as pltpu
from jax.sharding import PartitionSpec as P

VMEM = pl.BlockSpec(memory_space=pltpu.VMEM)
HBM = pl.BlockSpec(memory_space=pltpu.HBM)
MIB = 1 << 20


def iota(shape, axis):
    return lax.broadcasted_iota(jnp.int32, shape, axis)


def stack(refs):
    return jnp.concatenate([r[...].astype(jnp.float32) for r in refs], axis=0)


def unstack(value, outs):
    start = 0
    for out in outs:
        out[...] = value[start : start + out.shape[0]].astype(out.dtype)
        start += out.shape[0]


def route_kernel(group_size, slot_count, *refs):
    sources, refs = refs[:5], refs[5:]
    row_outs, combine_out, refs = refs[:slot_count], refs[slot_count], refs[slot_count + 1 :]
    scratch, sems = refs[:5], refs[5]
    copies_in = [
        pltpu.make_async_copy(s, t, sems.at[i]) for i, (s, t) in enumerate(zip(sources, scratch))
    ]
    for c in copies_in:
        c.start()
    placement, expert_ids, replica_pick, gate_weights, tokens = scratch
    capacity = row_outs[0].shape[0]
    top_count, tok_count = expert_ids.shape
    own = lax.axis_index("expert") // group_size
    core = lax.axis_index("dp") % 2
    copy_row = iota((slot_count, tok_count), 0)
    named = jnp.zeros_like(copy_row)
    before = jnp.zeros_like(copy_row)
    relative = jnp.zeros_like(copy_row)
    for c in copies_in[:4]:
        c.wait()
    for p in range(slot_count):
        here = copy_row == p
        named = jnp.where(here, placement[p], named)
        d = lax.bitwise_xor(own, p)
        place = jnp.where(core == 0, slot_count - 1 - d, (d + slot_count - 1) % slot_count)
        relative = jnp.where(here, place, relative)
        seen = jnp.int32(0)
        for q in range(p):
            seen = seen + (placement[q] == placement[p]).astype(jnp.int32)
        before = jnp.where(here, seen, before)
    chosen = []
    for k in range(top_count):
        matches = named == expert_ids[pl.ds(k, 1), :]
        copies = jnp.sum(matches.astype(jnp.int32), axis=0, keepdims=True)
        pick = replica_pick[pl.ds(k, 1), :]
        wanted = jnp.where(pick >= copies, pick - copies, pick)
        chosen.append((matches & (before == wanted)).astype(jnp.int32))
    total = sum(chosen[1:], chosen[0])
    ahead = (iota((tok_count, tok_count), 0) < iota((tok_count, tok_count), 1)).astype(jnp.bfloat16)
    earlier = jnp.dot(
        total.astype(jnp.bfloat16), ahead, preferred_element_type=jnp.float32
    ).astype(jnp.int32)
    slot_row = iota((slot_count * capacity, tok_count), 0)
    pick_rows = jnp.zeros((slot_count * capacity, tok_count), jnp.float32)
    combine = jnp.zeros((slot_count * capacity, tok_count), jnp.float32)
    for k in range(top_count):
        rank = jnp.sum(chosen[k] * earlier, axis=0, keepdims=True)
        place = jnp.sum(chosen[k] * relative, axis=0, keepdims=True)
        slot = jnp.where(rank < capacity, place * capacity + rank, -1)
        hot = slot_row == slot
        pick_rows = pick_rows + hot.astype(jnp.float32)
        combine = combine + jnp.where(hot, gate_weights[pl.ds(k, 1), :], 0.0)
        earlier = earlier + chosen[k]
    combine_out[...] = combine
    copies_in[4].wait()
    rows = jnp.dot(pick_rows.astype(jnp.bfloat16), tokens[...], preferred_element_type=jnp.float32)
    unstack(rows, row_outs)


def fetch_kernel(*refs):
    source, held, sems = refs[0], refs[-2], refs[-1]
    rows = held.shape[0] // sems.shape[0]
    copies = [
        pltpu.make_async_copy(source.at[pl.ds(i * rows, rows)], held.at[pl.ds(i * rows, rows)], sem)
        for i, sem in enumerate(sems.at[j] for j in range(sems.shape[0]))
    ]
    for c in copies:
        c.start()
    for c in copies:
        c.wait()


def terms_kernel(combine, near_terms, far_terms):
    slots = combine.shape[0] // 2
    same = (iota((slots, slots), 0) == iota((slots, slots), 1)).astype(jnp.float32)
    for start, out in ((0, near_terms), (slots, far_terms)):
        rest = combine[pl.ds(start, slots), :]
        terms = []
        for _ in range(3):
            term = rest.astype(jnp.bfloat16).astype(jnp.float32)
            rest = rest - term
            terms.append(
                lax.dot_general(
                    term, same, (((0,), (0,)), ((), ())), preferred_element_type=jnp.float32
                )
            )
        out[...] = jnp.concatenate(terms, axis=0).astype(jnp.bfloat16)


def stack_kernel(count, *refs):
    refs[-1][...] = stack(refs[:count]).astype(jnp.bfloat16)


def expert_kernel(count, *refs):
    blocks, (w_in, w_out), outs = refs[:count], refs[count : count + 2], refs[count + 2 :]
    rows = stack(blocks).astype(jnp.bfloat16)
    gate = jnp.dot(rows, w_in[0], preferred_element_type=jnp.float32)
    upper = jnp.dot(rows, w_in[1], preferred_element_type=jnp.float32)
    hidden = (gate / (1.0 + jnp.exp(-gate)) * upper).astype(jnp.bfloat16)
    unstack(jnp.dot(hidden, w_out[...], preferred_element_type=jnp.float32), outs)


def sum_kernel(count, *refs):
    total = refs[0][...].astype(jnp.float32)
    for r in refs[1:count]:
        total = total + r[...].astype(jnp.float32)
    unstack(total, refs[count:])


def combined(terms, parts, rows):
    values = stack(parts).astype(jnp.bfloat16)
    product = jnp.dot(terms[...], values, preferred_element_type=jnp.float32)
    return product[2 * rows :] + product[rows : 2 * rows] + product[:rows]


def near_kernel(terms, *refs):
    refs[-1][...] = combined(terms, refs[:-1], refs[-1].shape[0])


def far_kernel(terms, near, *refs):
    total = near[...] + combined(terms, refs[:-1], refs[-1].shape[0])
    refs[-1][...] = total.astype(jnp.bfloat16)


def call(kernel, inputs, in_specs, outs, limit, scratch=(), moved=0):
    return pl.pallas_call(
        kernel,
        out_shape=outs,
        in_specs=in_specs,
        out_specs=jax.tree.map(lambda _: VMEM, outs),
        scratch_shapes=scratch,
        compiler_params=pltpu.CompilerParams(vmem_limit_bytes=limit),
        cost_estimate=pl.CostEstimate(flops=0, bytes_accessed=moved, transcendentals=0)
        if moved
        else None,
    )(*inputs)


def body(tokens, expert_ids, gate_weights, replica_pick, placement, w_in, w_out):
    n_devices = lax.axis_size("expert")
    group_size = min(8, n_devices // 4)
    slot_count = n_devices // group_size
    tok_count, width = tokens.shape
    capacity = tok_count * expert_ids.shape[1] // slot_count
    slots = slot_count * capacity
    offsets = [(slot_count - 1 - i, (i + 1) % slot_count) for i in range(slot_count)]
    bf16 = jnp.bfloat16
    chunk = jax.ShapeDtypeStruct((capacity, width), bf16)
    half = jax.ShapeDtypeStruct((slots // 2, width), bf16)

    def swap(value, offset):
        return lax.ppermute(value, "expert", [(e, e ^ offset) for e in range(n_devices)])

    def across(value, even, odd):
        parts = lax.axis_size("dp")
        pairs = [
            (e * parts + part, (e ^ (group_size * (odd if part % 2 else even))) * parts + part)
            for e in range(n_devices)
            for part in range(parts)
        ]
        return lax.ppermute(value, ("expert", "dp"), pairs) if even else value

    def local(kernel, inputs, outs, limit=16 * MIB):
        return call(kernel, inputs, [VMEM] * len(inputs), outs, limit)

    def in_hbm(*arrays):
        return [pltpu.with_memory_space_constraint(a, pltpu.HBM) for a in arrays]

    sources = in_hbm(placement, expert_ids.T, replica_pick.T, gate_weights.T, tokens)
    *chunks, combine = call(
        functools.partial(route_kernel, group_size, slot_count),
        sources,
        [HBM] * 5,
        [chunk] * slot_count + [jax.ShapeDtypeStruct((slots, tok_count), jnp.float32)],
        16 * MIB,
        [pltpu.SMEM(placement.shape, jnp.int32)]
        + [pltpu.VMEM(s.shape, s.dtype) for s in sources[1:]]
        + [pltpu.SemaphoreType.DMA((5,))],
    )
    chunks = [across(c, *d) for c, d in zip(chunks, offsets)]
    terms = jax.ShapeDtypeStruct((3 * tok_count, slots // 2), bf16)
    terms = local(terms_kernel, [combine], [terms, terms])

    def fetch(array, after):
        return call(
            fetch_kernel,
            (*in_hbm(array), after),
            [HBM, VMEM],
            jax.ShapeDtypeStruct(array.shape, bf16),
            16 * MIB,
            [pltpu.SemaphoreType.DMA((2,))],
            2 * array.size,
        )

    w_in = fetch(w_in, terms[0])
    w_out = fetch(w_out, terms[1])

    square = group_size == 4
    count = slot_count // 2
    sides = ((1, 2), (2, 1))
    earlier = [w_in]
    summed = []
    for h in range(2):
        a, b = sides[h]
        own = local(
            functools.partial(stack_kernel, count), chunks[h * count :][:count] + earlier, half
        )
        if square:
            held = {a: swap(own, a), b: swap(own, b)}
            held = [own, held[a], held[b], swap(held[a], b)]
        else:
            held = [swap(own, q) if q else own for q in range(group_size)]
        earlier = []
        result = local(
            functools.partial(expert_kernel, group_size),
            held + [w_in, w_out],
            [half] * group_size,
            40 * MIB,
        )
        if square:
            mine, first, second, cross = result
            cross = swap(cross, b)
            second = swap(second, b)
            first = local(functools.partial(sum_kernel, 2), [first, cross], [half])[0]
            result = [mine, second, swap(first, a)]
        else:
            result = [swap(v, q) if q else v for q, v in enumerate(result)]
        summed += local(functools.partial(sum_kernel, len(result)), result, [chunk] * count)
    summed = [across(v, *d) for v, d in zip(summed, offsets)]
    near = local(
        near_kernel,
        [terms[0]] + summed[:count],
        jax.ShapeDtypeStruct((tok_count, width), jnp.float32),
    )
    return local(
        far_kernel,
        [terms[1], near] + summed[count:],
        jax.ShapeDtypeStruct((tok_count, width), bf16),
    )


def solution(mesh):
    in_specs = (
        P(("dp", "expert"), None),
        P(("dp", "expert"), None),
        P(("dp", "expert"), None),
        P(("dp", "expert"), None),
        P(),
        P(None, None, "expert"),
        P("expert", None),
    )
    out_specs = P(("dp", "expert"), None)
    return jax.shard_map(body, mesh=mesh, in_specs=in_specs, out_specs=out_specs, check_vma=False)
```

```python
import functools

import jax
import jax.numpy as jnp
from jax import lax
from jax.experimental import pallas as pl
from jax.experimental.pallas import tpu as pltpu
from jax.sharding import PartitionSpec as P

VMEM = pl.BlockSpec(memory_space=pltpu.VMEM)
HBM = pl.BlockSpec(memory_space=pltpu.HBM)
MIB = 1 << 20


def iota(shape, axis):
    return lax.broadcasted_iota(jnp.int32, shape, axis)


def stack(refs):
    return jnp.concatenate([r[...].astype(jnp.float32) for r in refs], axis=0)


def unstack(value, outs):
    start = 0
    for out in outs:
        out[...] = value[start : start + out.shape[0]].astype(out.dtype)
        start += out.shape[0]


def route_kernel(group_size, slot_count, *refs):
    sources, refs = refs[:5], refs[5:]
    row_outs, combine_out, refs = refs[:slot_count], refs[slot_count], refs[slot_count + 1 :]
    scratch, sems = refs[:5], refs[5]
    copies_in = [
        pltpu.make_async_copy(s, t, sems.at[i]) for i, (s, t) in enumerate(zip(sources, scratch))
    ]
    for c in copies_in:
        c.start()
    placement, expert_ids, replica_pick, gate_weights, tokens = scratch
    capacity = row_outs[0].shape[0]
    top_count, tok_count = expert_ids.shape
    own = lax.axis_index("expert") // group_size
    copy_row = iota((slot_count, tok_count), 0)
    named = jnp.zeros_like(copy_row)
    before = jnp.zeros_like(copy_row)
    relative = jnp.zeros_like(copy_row)
    for c in copies_in[:4]:
        c.wait()
    for p in range(slot_count):
        here = copy_row == p
        named = jnp.where(here, placement[p], named)
        d = lax.bitwise_xor(own, p)
        relative = jnp.where(here, slot_count - 1 - d, relative)
        seen = jnp.int32(0)
        for q in range(p):
            seen = seen + (placement[q] == placement[p]).astype(jnp.int32)
        before = jnp.where(here, seen, before)
    chosen = []
    for k in range(top_count):
        matches = named == expert_ids[pl.ds(k, 1), :]
        copies = jnp.sum(matches.astype(jnp.int32), axis=0, keepdims=True)
        pick = replica_pick[pl.ds(k, 1), :]
        wanted = jnp.where(pick >= copies, pick - copies, pick)
        chosen.append((matches & (before == wanted)).astype(jnp.int32))
    total = sum(chosen[1:], chosen[0])
    ahead = (iota((tok_count, tok_count), 0) < iota((tok_count, tok_count), 1)).astype(jnp.bfloat16)
    earlier = jnp.dot(
        total.astype(jnp.bfloat16), ahead, preferred_element_type=jnp.float32
    ).astype(jnp.int32)
    slot_row = iota((slot_count * capacity, tok_count), 0)
    pick_rows = jnp.zeros((slot_count * capacity, tok_count), jnp.float32)
    combine = jnp.zeros((slot_count * capacity, tok_count), jnp.float32)
    for k in range(top_count):
        rank = jnp.sum(chosen[k] * earlier, axis=0, keepdims=True)
        place = jnp.sum(chosen[k] * relative, axis=0, keepdims=True)
        slot = jnp.where(rank < capacity, place * capacity + rank, -1)
        hot = slot_row == slot
        pick_rows = pick_rows + hot.astype(jnp.float32)
        combine = combine + jnp.where(hot, gate_weights[pl.ds(k, 1), :], 0.0)
        earlier = earlier + chosen[k]
    combine_out[...] = combine
    copies_in[4].wait()
    rows = jnp.dot(pick_rows.astype(jnp.bfloat16), tokens[...], preferred_element_type=jnp.float32)
    unstack(rows, row_outs)


def fetch_kernel(*refs):
    source, held, sems = refs[0], refs[-2], refs[-1]
    rows = held.shape[0] // sems.shape[0]
    copies = [
        pltpu.make_async_copy(source.at[pl.ds(i * rows, rows)], held.at[pl.ds(i * rows, rows)], sem)
        for i, sem in enumerate(sems.at[j] for j in range(sems.shape[0]))
    ]
    for c in copies:
        c.start()
    for c in copies:
        c.wait()


def terms_kernel(combine, near_terms, far_terms):
    slots = combine.shape[0] // 2
    same = (iota((slots, slots), 0) == iota((slots, slots), 1)).astype(jnp.float32)
    for start, out in ((0, near_terms), (slots, far_terms)):
        rest = combine[pl.ds(start, slots), :]
        terms = []
        for _ in range(3):
            term = rest.astype(jnp.bfloat16).astype(jnp.float32)
            rest = rest - term
            terms.append(
                lax.dot_general(
                    term, same, (((0,), (0,)), ((), ())), preferred_element_type=jnp.float32
                )
            )
        out[...] = jnp.concatenate(terms, axis=0).astype(jnp.bfloat16)


def stack_kernel(count, *refs):
    refs[-1][...] = stack(refs[:count]).astype(jnp.bfloat16)


def expert_kernel(count, *refs):
    blocks, (w_in, w_out), outs = refs[:count], refs[count : count + 2], refs[count + 2 :]
    rows = stack(blocks).astype(jnp.bfloat16)
    gate = jnp.dot(rows, w_in[0], preferred_element_type=jnp.float32)
    upper = jnp.dot(rows, w_in[1], preferred_element_type=jnp.float32)
    hidden = (gate / (1.0 + jnp.exp(-gate)) * upper).astype(jnp.bfloat16)
    unstack(jnp.dot(hidden, w_out[...], preferred_element_type=jnp.float32), outs)


def sum_kernel(count, *refs):
    total = refs[0][...].astype(jnp.float32)
    for r in refs[1:count]:
        total = total + r[...].astype(jnp.float32)
    unstack(total, refs[count:])


def combined(terms, parts, rows):
    values = stack(parts).astype(jnp.bfloat16)
    product = jnp.dot(terms[...], values, preferred_element_type=jnp.float32)
    return product[2 * rows :] + product[rows : 2 * rows] + product[:rows]


def near_kernel(terms, *refs):
    refs[-1][...] = combined(terms, refs[:-1], refs[-1].shape[0])


def far_kernel(terms, near, *refs):
    total = near[...] + combined(terms, refs[:-1], refs[-1].shape[0])
    refs[-1][...] = total.astype(jnp.bfloat16)


def call(kernel, inputs, in_specs, outs, limit, scratch=(), moved=0):
    return pl.pallas_call(
        kernel,
        out_shape=outs,
        in_specs=in_specs,
        out_specs=jax.tree.map(lambda _: VMEM, outs),
        scratch_shapes=scratch,
        compiler_params=pltpu.CompilerParams(vmem_limit_bytes=limit),
        cost_estimate=pl.CostEstimate(flops=0, bytes_accessed=moved, transcendentals=0)
        if moved
        else None,
    )(*inputs)


def body(tokens, expert_ids, gate_weights, replica_pick, placement, w_in, w_out):
    n_devices = lax.axis_size("expert")
    group_size = min(8, n_devices // 4)
    slot_count = n_devices // group_size
    tok_count, width = tokens.shape
    capacity = tok_count * expert_ids.shape[1] // slot_count
    slots = slot_count * capacity
    offsets = range(slot_count - 1, -1, -1)
    bf16 = jnp.bfloat16
    chunk = jax.ShapeDtypeStruct((capacity, width), bf16)
    half = jax.ShapeDtypeStruct((slots // 2, width), bf16)

    def swap(value, offset):
        return lax.ppermute(value, "expert", [(e, e ^ offset) for e in range(n_devices)])

    def local(kernel, inputs, outs, limit=16 * MIB):
        return call(kernel, inputs, [VMEM] * len(inputs), outs, limit)

    def in_hbm(*arrays):
        return [pltpu.with_memory_space_constraint(a, pltpu.HBM) for a in arrays]

    sources = in_hbm(placement, expert_ids.T, replica_pick.T, gate_weights.T, tokens)
    *chunks, combine = call(
        functools.partial(route_kernel, group_size, slot_count),
        sources,
        [HBM] * 5,
        [chunk] * slot_count + [jax.ShapeDtypeStruct((slots, tok_count), jnp.float32)],
        16 * MIB,
        [pltpu.SMEM(placement.shape, jnp.int32)]
        + [pltpu.VMEM(s.shape, s.dtype) for s in sources[1:]]
        + [pltpu.SemaphoreType.DMA((5,))],
    )
    chunks = [swap(c, d * group_size) if d else c for d, c in zip(offsets, chunks)]
    terms = jax.ShapeDtypeStruct((3 * tok_count, slots // 2), bf16)
    terms = local(terms_kernel, [combine], [terms, terms])

    def fetch(array, after):
        return call(
            fetch_kernel,
            (*in_hbm(array), after),
            [HBM, VMEM],
            jax.ShapeDtypeStruct(array.shape, bf16),
            16 * MIB,
            [pltpu.SemaphoreType.DMA((2,))],
            2 * array.size,
        )

    w_in = fetch(w_in, terms[0])
    w_out = fetch(w_out, terms[1])

    square = group_size == 4
    count = slot_count // 2
    sides = ((1, 2), (2, 1))
    earlier = [w_in]
    summed = []
    for h in range(2):
        a, b = sides[h]
        own = local(
            functools.partial(stack_kernel, count), chunks[h * count :][:count] + earlier, half
        )
        if square:
            held = {a: swap(own, a), b: swap(own, b)}
            held = [own, held[a], held[b], swap(held[a], b)]
        else:
            held = [swap(own, q) if q else own for q in range(group_size)]
        earlier = held[1:3]
        result = local(
            functools.partial(expert_kernel, group_size),
            held + [w_in, w_out],
            [half] * group_size,
            40 * MIB,
        )
        if square:
            mine, first, second, cross = result
            cross = swap(cross, b)
            second = swap(second, b)
            first = local(functools.partial(sum_kernel, 2), [first, cross], [half])[0]
            result = [mine, second, swap(first, a)]
        else:
            result = [swap(v, q) if q else v for q, v in enumerate(result)]
        summed += local(functools.partial(sum_kernel, len(result)), result, [chunk] * count)
    summed = [swap(v, d * group_size) if d else v for d, v in zip(offsets, summed)]
    near = local(
        near_kernel,
        [terms[0]] + summed[:count],
        jax.ShapeDtypeStruct((tok_count, width), jnp.float32),
    )
    return local(
        far_kernel,
        [terms[1], near] + summed[count:],
        jax.ShapeDtypeStruct((tok_count, width), bf16),
    )


def solution(mesh):
    in_specs = (
        P(("dp", "expert"), None),
        P(("dp", "expert"), None),
        P(("dp", "expert"), None),
        P(("dp", "expert"), None),
        P(),
        P(None, None, "expert"),
        P("expert", None),
    )
    out_specs = P(("dp", "expert"), None)
    return jax.shard_map(body, mesh=mesh, in_specs=in_specs, out_specs=out_specs, check_vma=False)
```

```python
import functools

import jax
import jax.numpy as jnp
from jax import lax
from jax.experimental import pallas as pl
from jax.experimental.pallas import tpu as pltpu
from jax.sharding import PartitionSpec as P

VMEM = pl.BlockSpec(memory_space=pltpu.VMEM)
HBM = pl.BlockSpec(memory_space=pltpu.HBM)
MIB = 1 << 20


def iota(shape, axis):
    return lax.broadcasted_iota(jnp.int32, shape, axis)


def stack(refs):
    return jnp.concatenate([r[...].astype(jnp.float32) for r in refs], axis=0)


def unstack(value, outs):
    start = 0
    for out in outs:
        out[...] = value[start : start + out.shape[0]].astype(out.dtype)
        start += out.shape[0]


def route_kernel(group_size, slot_count, *refs):
    sources, refs = refs[:5], refs[5:]
    row_outs, combine_out, refs = refs[:slot_count], refs[slot_count], refs[slot_count + 1 :]
    scratch, sems = refs[:5], refs[5]
    copies_in = [
        pltpu.make_async_copy(s, t, sems.at[i]) for i, (s, t) in enumerate(zip(sources, scratch))
    ]
    for c in copies_in:
        c.start()
    placement, expert_ids, replica_pick, gate_weights, tokens = scratch
    capacity = row_outs[0].shape[0]
    top_count, tok_count = expert_ids.shape
    own = lax.axis_index("expert") // group_size
    copy_row = iota((slot_count, tok_count), 0)
    named = jnp.zeros_like(copy_row)
    before = jnp.zeros_like(copy_row)
    relative = jnp.zeros_like(copy_row)
    for c in copies_in[:4]:
        c.wait()
    for p in range(slot_count):
        here = copy_row == p
        named = jnp.where(here, placement[p], named)
        d = lax.bitwise_xor(own, p)
        relative = jnp.where(here, slot_count - 1 - d, relative)
        seen = jnp.int32(0)
        for q in range(p):
            seen = seen + (placement[q] == placement[p]).astype(jnp.int32)
        before = jnp.where(here, seen, before)
    chosen = []
    for k in range(top_count):
        matches = named == expert_ids[pl.ds(k, 1), :]
        copies = jnp.sum(matches.astype(jnp.int32), axis=0, keepdims=True)
        pick = replica_pick[pl.ds(k, 1), :]
        wanted = jnp.where(pick >= copies, pick - copies, pick)
        chosen.append((matches & (before == wanted)).astype(jnp.int32))
    total = sum(chosen[1:], chosen[0])
    ahead = (iota((tok_count, tok_count), 0) < iota((tok_count, tok_count), 1)).astype(jnp.bfloat16)
    earlier = jnp.dot(
        total.astype(jnp.bfloat16), ahead, preferred_element_type=jnp.float32
    ).astype(jnp.int32)
    slot_row = iota((slot_count * capacity, tok_count), 0)
    pick_rows = jnp.zeros((slot_count * capacity, tok_count), jnp.float32)
    combine = jnp.zeros((slot_count * capacity, tok_count), jnp.float32)
    for k in range(top_count):
        rank = jnp.sum(chosen[k] * earlier, axis=0, keepdims=True)
        place = jnp.sum(chosen[k] * relative, axis=0, keepdims=True)
        slot = jnp.where(rank < capacity, place * capacity + rank, -1)
        hot = slot_row == slot
        pick_rows = pick_rows + hot.astype(jnp.float32)
        combine = combine + jnp.where(hot, gate_weights[pl.ds(k, 1), :], 0.0)
        earlier = earlier + chosen[k]
    combine_out[...] = combine
    copies_in[4].wait()
    rows = jnp.dot(pick_rows.astype(jnp.bfloat16), tokens[...], preferred_element_type=jnp.float32)
    unstack(rows, row_outs)


def fetch_kernel(*refs):
    source, held, sems = refs[0], refs[-2], refs[-1]
    rows = held.shape[0] // sems.shape[0]
    copies = [
        pltpu.make_async_copy(source.at[pl.ds(i * rows, rows)], held.at[pl.ds(i * rows, rows)], sem)
        for i, sem in enumerate(sems.at[j] for j in range(sems.shape[0]))
    ]
    for c in copies:
        c.start()
    for c in copies:
        c.wait()


def terms_kernel(combine, first_terms, rest_terms):
    start = 0
    for out in (first_terms, rest_terms):
        slots = out.shape[1]
        same = (iota((slots, slots), 0) == iota((slots, slots), 1)).astype(jnp.float32)
        rest = combine[pl.ds(start, slots), :]
        terms = []
        for _ in range(3):
            term = rest.astype(jnp.bfloat16).astype(jnp.float32)
            rest = rest - term
            terms.append(
                lax.dot_general(
                    term, same, (((0,), (0,)), ((), ())), preferred_element_type=jnp.float32
                )
            )
        out[...] = jnp.concatenate(terms, axis=0).astype(jnp.bfloat16)
        start += slots


def stack_kernel(count, *refs):
    refs[-1][...] = stack(refs[:count]).astype(jnp.bfloat16)


def expert_kernel(count, *refs):
    blocks, (w_in, w_out), outs = refs[:count], refs[count : count + 2], refs[count + 2 :]
    rows = stack(blocks).astype(jnp.bfloat16)
    gate = jnp.dot(rows, w_in[0], preferred_element_type=jnp.float32)
    upper = jnp.dot(rows, w_in[1], preferred_element_type=jnp.float32)
    hidden = (gate / (1.0 + jnp.exp(-gate)) * upper).astype(jnp.bfloat16)
    unstack(jnp.dot(hidden, w_out[...], preferred_element_type=jnp.float32), outs)


def sum_kernel(count, *refs):
    total = refs[0][...].astype(jnp.float32)
    for r in refs[1:count]:
        total = total + r[...].astype(jnp.float32)
    unstack(total, refs[count:])


def combined(terms, parts, rows):
    values = stack(parts).astype(jnp.bfloat16)
    product = jnp.dot(terms[...], values, preferred_element_type=jnp.float32)
    return product[2 * rows :] + product[rows : 2 * rows] + product[:rows]


def first_kernel(terms, *refs):
    refs[-1][...] = combined(terms, refs[:-1], refs[-1].shape[0])


def rest_kernel(terms, first, *refs):
    total = first[...] + combined(terms, refs[:-1], refs[-1].shape[0])
    refs[-1][...] = total.astype(jnp.bfloat16)


def call(kernel, inputs, in_specs, outs, limit, scratch=(), moved=0):
    return pl.pallas_call(
        kernel,
        out_shape=outs,
        in_specs=in_specs,
        out_specs=jax.tree.map(lambda _: VMEM, outs),
        scratch_shapes=scratch,
        compiler_params=pltpu.CompilerParams(vmem_limit_bytes=limit),
        cost_estimate=pl.CostEstimate(flops=0, bytes_accessed=moved, transcendentals=0)
        if moved
        else None,
    )(*inputs)


def body(tokens, expert_ids, gate_weights, replica_pick, placement, w_in, w_out):
    n_devices = lax.axis_size("expert")
    group_size = min(8, n_devices // 4)
    slot_count = n_devices // group_size
    tok_count, width = tokens.shape
    capacity = tok_count * expert_ids.shape[1] // slot_count
    slots = slot_count * capacity
    offsets = range(slot_count - 1, -1, -1)
    bf16 = jnp.bfloat16
    chunk = jax.ShapeDtypeStruct((capacity, width), bf16)
    half = jax.ShapeDtypeStruct((slots // 2, width), bf16)

    def swap(value, offset):
        return lax.ppermute(value, "expert", [(e, e ^ offset) for e in range(n_devices)])

    def local(kernel, inputs, outs, limit=16 * MIB):
        return call(kernel, inputs, [VMEM] * len(inputs), outs, limit)

    def in_hbm(*arrays):
        return [pltpu.with_memory_space_constraint(a, pltpu.HBM) for a in arrays]

    sources = in_hbm(placement, expert_ids.T, replica_pick.T, gate_weights.T, tokens)
    *chunks, combine = call(
        functools.partial(route_kernel, group_size, slot_count),
        sources,
        [HBM] * 5,
        [chunk] * slot_count + [jax.ShapeDtypeStruct((slots, tok_count), jnp.float32)],
        16 * MIB,
        [pltpu.SMEM(placement.shape, jnp.int32)]
        + [pltpu.VMEM(s.shape, s.dtype) for s in sources[1:]]
        + [pltpu.SemaphoreType.DMA((5,))],
    )
    chunks = [swap(c, d * group_size) if d else c for d, c in zip(offsets, chunks)]
    terms = [
        jax.ShapeDtypeStruct((3 * tok_count, n), bf16) for n in (capacity, slots - capacity)
    ]
    terms = local(terms_kernel, [combine], terms)

    def fetch(array, after):
        return call(
            fetch_kernel,
            (*in_hbm(array), after),
            [HBM, VMEM],
            jax.ShapeDtypeStruct(array.shape, bf16),
            16 * MIB,
            [pltpu.SemaphoreType.DMA((2,))],
            2 * array.size,
        )

    w_in = fetch(w_in, terms[0])
    w_out = fetch(w_out, terms[1])

    square = group_size == 4
    count = slot_count // 2
    sides = ((1, 2), (2, 1))
    earlier = [w_in]
    summed = []
    for h in range(2):
        a, b = sides[h]
        own = local(
            functools.partial(stack_kernel, count), chunks[h * count :][:count] + earlier, half
        )
        if square:
            held = {a: swap(own, a), b: swap(own, b)}
            held = [own, held[a], held[b], swap(held[a], b)]
        else:
            held = [swap(own, q) if q else own for q in range(group_size)]
        earlier = []
        result = local(
            functools.partial(expert_kernel, group_size),
            held + [w_in, w_out],
            [half] * group_size,
            40 * MIB,
        )
        if square:
            mine, first, second, cross = result
            cross = swap(cross, b)
            second = swap(second, b)
            first = local(functools.partial(sum_kernel, 2), [first, cross], [half])[0]
            result = [mine, second, swap(first, a)]
        else:
            result = [swap(v, q) if q else v for q, v in enumerate(result)]
        summed += local(functools.partial(sum_kernel, len(result)), result, [chunk] * count)
    summed = [swap(v, d * group_size) if d else v for d, v in zip(offsets, summed)]
    first = local(
        first_kernel,
        [terms[0]] + summed[:1],
        jax.ShapeDtypeStruct((tok_count, width), jnp.float32),
    )
    return local(
        rest_kernel,
        [terms[1], first] + summed[1:],
        jax.ShapeDtypeStruct((tok_count, width), bf16),
    )


def solution(mesh):
    in_specs = (
        P(("dp", "expert"), None),
        P(("dp", "expert"), None),
        P(("dp", "expert"), None),
        P(("dp", "expert"), None),
        P(),
        P(None, None, "expert"),
        P("expert", None),
    )
    out_specs = P(("dp", "expert"), None)
    return jax.shard_map(body, mesh=mesh, in_specs=in_specs, out_specs=out_specs, check_vma=False)
```

```python
import functools

import jax
import jax.numpy as jnp
from jax import lax
from jax.experimental import pallas as pl
from jax.experimental.pallas import tpu as pltpu
from jax.sharding import PartitionSpec as P

VMEM = pl.BlockSpec(memory_space=pltpu.VMEM)
HBM = pl.BlockSpec(memory_space=pltpu.HBM)
MIB = 1 << 20


def iota(shape, axis):
    return lax.broadcasted_iota(jnp.int32, shape, axis)


def stack(refs):
    return jnp.concatenate([r[...].astype(jnp.float32) for r in refs], axis=0)


def unstack(value, outs):
    start = 0
    for out in outs:
        out[...] = value[start : start + out.shape[0]].astype(out.dtype)
        start += out.shape[0]


def route_kernel(group_size, slot_count, *refs):
    sources, refs = refs[:5], refs[5:]
    row_outs, combine_out, refs = refs[:slot_count], refs[slot_count], refs[slot_count + 1 :]
    scratch, sems = refs[:5], refs[5]
    copies_in = [
        pltpu.make_async_copy(s, t, sems.at[i]) for i, (s, t) in enumerate(zip(sources, scratch))
    ]
    for c in copies_in:
        c.start()
    placement, expert_ids, replica_pick, gate_weights, tokens = scratch
    capacity = row_outs[0].shape[0]
    top_count, tok_count = expert_ids.shape
    own = lax.axis_index("expert") // group_size
    copy_row = iota((slot_count, tok_count), 0)
    named = jnp.zeros_like(copy_row)
    before = jnp.zeros_like(copy_row)
    relative = jnp.zeros_like(copy_row)
    weighed = jnp.zeros_like(copy_row)
    for c in copies_in[:4]:
        c.wait()
    for p in range(slot_count):
        here = copy_row == p
        named = jnp.where(here, placement[p], named)
        d = lax.bitwise_xor(own, p)
        weighed = jnp.where(here, slot_count - 1 - d, weighed)
        far = d >= slot_count // 2
        place = jnp.where(far, d - slot_count // 2, slot_count - 1 - d)
        relative = jnp.where(here, place, relative)
        seen = jnp.int32(0)
        for q in range(p):
            seen = seen + (placement[q] == placement[p]).astype(jnp.int32)
        before = jnp.where(here, seen, before)
    chosen = []
    for k in range(top_count):
        matches = named == expert_ids[pl.ds(k, 1), :]
        copies = jnp.sum(matches.astype(jnp.int32), axis=0, keepdims=True)
        pick = replica_pick[pl.ds(k, 1), :]
        wanted = jnp.where(pick >= copies, pick - copies, pick)
        chosen.append((matches & (before == wanted)).astype(jnp.int32))
    total = sum(chosen[1:], chosen[0])
    ahead = (iota((tok_count, tok_count), 0) < iota((tok_count, tok_count), 1)).astype(jnp.bfloat16)
    earlier = jnp.dot(
        total.astype(jnp.bfloat16), ahead, preferred_element_type=jnp.float32
    ).astype(jnp.int32)
    slot_row = iota((slot_count * capacity, tok_count), 0)
    pick_rows = jnp.zeros((slot_count * capacity, tok_count), jnp.float32)
    combine = jnp.zeros((slot_count * capacity, tok_count), jnp.float32)
    for k in range(top_count):
        rank = jnp.sum(chosen[k] * earlier, axis=0, keepdims=True)
        place = jnp.sum(chosen[k] * relative, axis=0, keepdims=True)
        slot = jnp.where(rank < capacity, place * capacity + rank, -1)
        hot = slot_row == slot
        pick_rows = pick_rows + hot.astype(jnp.float32)
        place = jnp.sum(chosen[k] * weighed, axis=0, keepdims=True)
        hot = slot_row == jnp.where(rank < capacity, place * capacity + rank, -1)
        combine = combine + jnp.where(hot, gate_weights[pl.ds(k, 1), :], 0.0)
        earlier = earlier + chosen[k]
    combine_out[...] = combine
    copies_in[4].wait()
    rows = jnp.dot(pick_rows.astype(jnp.bfloat16), tokens[...], preferred_element_type=jnp.float32)
    unstack(rows, row_outs)


def fetch_kernel(*refs):
    source, held, sems = refs[0], refs[-2], refs[-1]
    rows = held.shape[0] // sems.shape[0]
    copies = [
        pltpu.make_async_copy(source.at[pl.ds(i * rows, rows)], held.at[pl.ds(i * rows, rows)], sem)
        for i, sem in enumerate(sems.at[j] for j in range(sems.shape[0]))
    ]
    for c in copies:
        c.start()
    for c in copies:
        c.wait()


def terms_kernel(combine, first_terms, rest_terms):
    start = 0
    for out in (first_terms, rest_terms):
        slots = out.shape[1]
        same = (iota((slots, slots), 0) == iota((slots, slots), 1)).astype(jnp.float32)
        rest = combine[pl.ds(start, slots), :]
        terms = []
        for _ in range(3):
            term = rest.astype(jnp.bfloat16).astype(jnp.float32)
            rest = rest - term
            terms.append(
                lax.dot_general(
                    term, same, (((0,), (0,)), ((), ())), preferred_element_type=jnp.float32
                )
            )
        out[...] = jnp.concatenate(terms, axis=0).astype(jnp.bfloat16)
        start += slots


def stack_kernel(count, *refs):
    refs[-1][...] = stack(refs[:count]).astype(jnp.bfloat16)


def expert_kernel(count, *refs):
    blocks, (w_in, w_out), outs = refs[:count], refs[count : count + 2], refs[count + 2 :]
    rows = stack(blocks).astype(jnp.bfloat16)
    gate = jnp.dot(rows, w_in[0], preferred_element_type=jnp.float32)
    upper = jnp.dot(rows, w_in[1], preferred_element_type=jnp.float32)
    hidden = (gate / (1.0 + jnp.exp(-gate)) * upper).astype(jnp.bfloat16)
    unstack(jnp.dot(hidden, w_out[...], preferred_element_type=jnp.float32), outs)


def sum_kernel(count, *refs):
    total = refs[0][...].astype(jnp.float32)
    for r in refs[1:count]:
        total = total + r[...].astype(jnp.float32)
    unstack(total, refs[count:])


def combined(terms, parts, rows):
    values = stack(parts).astype(jnp.bfloat16)
    product = jnp.dot(terms[...], values, preferred_element_type=jnp.float32)
    return product[2 * rows :] + product[rows : 2 * rows] + product[:rows]


def first_kernel(terms, *refs):
    refs[-1][...] = combined(terms, refs[:-1], refs[-1].shape[0])


def rest_kernel(terms, first, *refs):
    total = first[...] + combined(terms, refs[:-1], refs[-1].shape[0])
    refs[-1][...] = total.astype(jnp.bfloat16)


def call(kernel, inputs, in_specs, outs, limit, scratch=(), moved=0):
    return pl.pallas_call(
        kernel,
        out_shape=outs,
        in_specs=in_specs,
        out_specs=jax.tree.map(lambda _: VMEM, outs),
        scratch_shapes=scratch,
        compiler_params=pltpu.CompilerParams(vmem_limit_bytes=limit),
        cost_estimate=pl.CostEstimate(flops=0, bytes_accessed=moved, transcendentals=0)
        if moved
        else None,
    )(*inputs)


def body(tokens, expert_ids, gate_weights, replica_pick, placement, w_in, w_out):
    n_devices = lax.axis_size("expert")
    group_size = min(8, n_devices // 4)
    slot_count = n_devices // group_size
    tok_count, width = tokens.shape
    capacity = tok_count * expert_ids.shape[1] // slot_count
    slots = slot_count * capacity
    offsets = [*range(slot_count // 2, slot_count)] + [*range(slot_count // 2)][::-1]
    bf16 = jnp.bfloat16
    chunk = jax.ShapeDtypeStruct((capacity, width), bf16)
    half = jax.ShapeDtypeStruct((slots // 2, width), bf16)

    def swap(value, offset):
        return lax.ppermute(value, "expert", [(e, e ^ offset) for e in range(n_devices)])

    def local(kernel, inputs, outs, limit=16 * MIB):
        return call(kernel, inputs, [VMEM] * len(inputs), outs, limit)

    def in_hbm(*arrays):
        return [pltpu.with_memory_space_constraint(a, pltpu.HBM) for a in arrays]

    sources = in_hbm(placement, expert_ids.T, replica_pick.T, gate_weights.T, tokens)
    *chunks, combine = call(
        functools.partial(route_kernel, group_size, slot_count),
        sources,
        [HBM] * 5,
        [chunk] * slot_count + [jax.ShapeDtypeStruct((slots, tok_count), jnp.float32)],
        16 * MIB,
        [pltpu.SMEM(placement.shape, jnp.int32)]
        + [pltpu.VMEM(s.shape, s.dtype) for s in sources[1:]]
        + [pltpu.SemaphoreType.DMA((5,))],
    )
    chunks = [swap(c, d * group_size) if d else c for d, c in zip(offsets, chunks)]
    terms = [
        jax.ShapeDtypeStruct((3 * tok_count, n), bf16) for n in (capacity, slots - capacity)
    ]
    terms = local(terms_kernel, [combine], terms)

    def fetch(array, after):
        return call(
            fetch_kernel,
            (*in_hbm(array), after),
            [HBM, VMEM],
            jax.ShapeDtypeStruct(array.shape, bf16),
            16 * MIB,
            [pltpu.SemaphoreType.DMA((2,))],
            2 * array.size,
        )

    w_in = fetch(w_in, terms[0])
    w_out = fetch(w_out, terms[1])

    square = group_size == 4
    count = slot_count // 2
    sides = ((1, 2), (2, 1))
    earlier = [w_in]
    summed = []
    for h in range(2):
        a, b = sides[h]
        own = local(
            functools.partial(stack_kernel, count), chunks[h * count :][:count] + earlier, half
        )
        if square:
            held = {a: swap(own, a), b: swap(own, b)}
            held = [own, held[a], held[b], swap(held[a], b)]
        else:
            held = [swap(own, q) if q else own for q in range(group_size)]
        earlier = []
        result = local(
            functools.partial(expert_kernel, group_size),
            held + [w_in, w_out],
            [half] * group_size,
            40 * MIB,
        )
        if square:
            mine, first, second, cross = result
            cross = swap(cross, b)
            second = swap(second, b)
            first = local(functools.partial(sum_kernel, 2), [first, cross], [half])[0]
            result = [mine, second, swap(first, a)]
        else:
            result = [swap(v, q) if q else v for q, v in enumerate(result)]
        summed += local(functools.partial(sum_kernel, len(result)), result, [chunk] * count)
    summed = [swap(v, d * group_size) if d else v for d, v in zip(offsets, summed)]
    summed = summed[:count][::-1] + summed[count:]
    first = local(
        first_kernel,
        [terms[0]] + summed[:1],
        jax.ShapeDtypeStruct((tok_count, width), jnp.float32),
    )
    return local(
        rest_kernel,
        [terms[1], first] + summed[1:],
        jax.ShapeDtypeStruct((tok_count, width), bf16),
    )


def solution(mesh):
    in_specs = (
        P(("dp", "expert"), None),
        P(("dp", "expert"), None),
        P(("dp", "expert"), None),
        P(("dp", "expert"), None),
        P(),
        P(None, None, "expert"),
        P("expert", None),
    )
    out_specs = P(("dp", "expert"), None)
    return jax.shard_map(body, mesh=mesh, in_specs=in_specs, out_specs=out_specs, check_vma=False)
```

```python
import functools

import jax
import jax.numpy as jnp
from jax import lax
from jax.experimental import pallas as pl
from jax.experimental.pallas import tpu as pltpu
from jax.sharding import PartitionSpec as P

VMEM = pl.BlockSpec(memory_space=pltpu.VMEM)
HBM = pl.BlockSpec(memory_space=pltpu.HBM)
MIB = 1 << 20


def iota(shape, axis):
    return lax.broadcasted_iota(jnp.int32, shape, axis)


def stack(refs):
    return jnp.concatenate([r[...].astype(jnp.float32) for r in refs], axis=0)


def unstack(value, outs):
    start = 0
    for out in outs:
        out[...] = value[start : start + out.shape[0]].astype(out.dtype)
        start += out.shape[0]


def route_kernel(group_size, slot_count, *refs):
    sources, refs = refs[:5], refs[5:]
    row_outs, combine_out, refs = refs[:slot_count], refs[slot_count], refs[slot_count + 1 :]
    scratch, sems = refs[:5], refs[5]
    copies_in = [
        pltpu.make_async_copy(s, t, sems.at[i]) for i, (s, t) in enumerate(zip(sources, scratch))
    ]
    for c in copies_in:
        c.start()
    placement, expert_ids, replica_pick, gate_weights, tokens = scratch
    capacity = row_outs[0].shape[0]
    top_count, tok_count = expert_ids.shape
    own = lax.axis_index("expert") // group_size
    copy_row = iota((slot_count, tok_count), 0)
    named = jnp.zeros_like(copy_row)
    before = jnp.zeros_like(copy_row)
    relative = jnp.zeros_like(copy_row)
    for c in copies_in[:4]:
        c.wait()
    for p in range(slot_count):
        here = copy_row == p
        named = jnp.where(here, placement[p], named)
        d = lax.bitwise_xor(own, p)
        relative = jnp.where(here, slot_count - 1 - d, relative)
        seen = jnp.int32(0)
        for q in range(p):
            seen = seen + (placement[q] == placement[p]).astype(jnp.int32)
        before = jnp.where(here, seen, before)
    chosen = []
    for k in range(top_count):
        matches = named == expert_ids[pl.ds(k, 1), :]
        copies = jnp.sum(matches.astype(jnp.int32), axis=0, keepdims=True)
        pick = replica_pick[pl.ds(k, 1), :]
        wanted = jnp.where(pick >= copies, pick - copies, pick)
        chosen.append((matches & (before == wanted)).astype(jnp.int32))
    total = sum(chosen[1:], chosen[0])
    ahead = (iota((tok_count, tok_count), 0) < iota((tok_count, tok_count), 1)).astype(jnp.bfloat16)
    earlier = jnp.dot(
        total.astype(jnp.bfloat16), ahead, preferred_element_type=jnp.float32
    ).astype(jnp.int32)
    slot_row = iota((slot_count * capacity, tok_count), 0)
    pick_rows = jnp.zeros((slot_count * capacity, tok_count), jnp.float32)
    combine = jnp.zeros((slot_count * capacity, tok_count), jnp.float32)
    for k in range(top_count):
        rank = jnp.sum(chosen[k] * earlier, axis=0, keepdims=True)
        place = jnp.sum(chosen[k] * relative, axis=0, keepdims=True)
        slot = jnp.where(rank < capacity, place * capacity + rank, -1)
        hot = slot_row == slot
        pick_rows = pick_rows + hot.astype(jnp.float32)
        combine = combine + jnp.where(hot, gate_weights[pl.ds(k, 1), :], 0.0)
        earlier = earlier + chosen[k]
    combine_out[...] = combine
    copies_in[4].wait()
    rows = jnp.dot(pick_rows.astype(jnp.bfloat16), tokens[...], preferred_element_type=jnp.float32)
    unstack(rows, row_outs)


def fetch_kernel(*refs):
    source, held, sems = refs[0], refs[-2], refs[-1]
    rows = held.shape[0] // sems.shape[0]
    copies = [
        pltpu.make_async_copy(source.at[pl.ds(i * rows, rows)], held.at[pl.ds(i * rows, rows)], sem)
        for i, sem in enumerate(sems.at[j] for j in range(sems.shape[0]))
    ]
    for c in copies:
        c.start()
    for c in copies:
        c.wait()


def terms_kernel(combine, first_terms, rest_terms):
    start = 0
    for out in (first_terms, rest_terms):
        slots = out.shape[1]
        same = (iota((slots, slots), 0) == iota((slots, slots), 1)).astype(jnp.float32)
        rest = combine[pl.ds(start, slots), :]
        terms = []
        for _ in range(3):
            term = rest.astype(jnp.bfloat16).astype(jnp.float32)
            rest = rest - term
            terms.append(
                lax.dot_general(
                    term, same, (((0,), (0,)), ((), ())), preferred_element_type=jnp.float32
                )
            )
        out[...] = jnp.concatenate(terms, axis=0).astype(jnp.bfloat16)
        start += slots


def stack_kernel(count, *refs):
    refs[-1][...] = stack(refs[:count]).astype(jnp.bfloat16)


def expert_kernel(count, *refs):
    blocks, (w_in, w_out), outs = refs[:count], refs[count : count + 2], refs[count + 2 :]
    rows = stack(blocks).astype(jnp.bfloat16)
    gate = jnp.dot(rows, w_in[0], preferred_element_type=jnp.float32)
    upper = jnp.dot(rows, w_in[1], preferred_element_type=jnp.float32)
    hidden = (gate / (1.0 + jnp.exp(-gate)) * upper).astype(jnp.bfloat16)
    unstack(jnp.dot(hidden, w_out[...], preferred_element_type=jnp.float32), outs)


def fetching_expert_kernel(count, *refs):
    blocks, (w_in, source), outs = refs[:count], refs[count : count + 2], refs[count + 2 : -2]
    held, sem = refs[-2:]
    copy = pltpu.make_async_copy(source, held, sem.at[0])
    copy.start()
    rows = stack(blocks).astype(jnp.bfloat16)
    gate = jnp.dot(rows, w_in[0], preferred_element_type=jnp.float32)
    upper = jnp.dot(rows, w_in[1], preferred_element_type=jnp.float32)
    hidden = (gate / (1.0 + jnp.exp(-gate)) * upper).astype(jnp.bfloat16)
    copy.wait()
    unstack(jnp.dot(hidden, held[...], preferred_element_type=jnp.float32), outs)


def sum_kernel(count, *refs):
    total = refs[0][...].astype(jnp.float32)
    for r in refs[1:count]:
        total = total + r[...].astype(jnp.float32)
    unstack(total, refs[count:])


def combined(terms, parts, rows):
    values = stack(parts).astype(jnp.bfloat16)
    product = jnp.dot(terms[...], values, preferred_element_type=jnp.float32)
    return product[2 * rows :] + product[rows : 2 * rows] + product[:rows]


def first_kernel(terms, *refs):
    refs[-1][...] = combined(terms, refs[:-1], refs[-1].shape[0])


def rest_kernel(terms, first, *refs):
    total = first[...] + combined(terms, refs[:-1], refs[-1].shape[0])
    refs[-1][...] = total.astype(jnp.bfloat16)


def call(kernel, inputs, in_specs, outs, limit, scratch=(), moved=0):
    return pl.pallas_call(
        kernel,
        out_shape=outs,
        in_specs=in_specs,
        out_specs=jax.tree.map(lambda _: VMEM, outs),
        scratch_shapes=scratch,
        compiler_params=pltpu.CompilerParams(vmem_limit_bytes=limit),
        cost_estimate=pl.CostEstimate(flops=0, bytes_accessed=moved, transcendentals=0)
        if moved
        else None,
    )(*inputs)


def body(tokens, expert_ids, gate_weights, replica_pick, placement, w_in, w_out):
    n_devices = lax.axis_size("expert")
    group_size = min(8, n_devices // 4)
    slot_count = n_devices // group_size
    tok_count, width = tokens.shape
    capacity = tok_count * expert_ids.shape[1] // slot_count
    slots = slot_count * capacity
    offsets = range(slot_count - 1, -1, -1)
    bf16 = jnp.bfloat16
    chunk = jax.ShapeDtypeStruct((capacity, width), bf16)
    half = jax.ShapeDtypeStruct((slots // 2, width), bf16)

    def swap(value, offset):
        return lax.ppermute(value, "expert", [(e, e ^ offset) for e in range(n_devices)])

    def local(kernel, inputs, outs, limit=16 * MIB):
        return call(kernel, inputs, [VMEM] * len(inputs), outs, limit)

    def in_hbm(*arrays):
        return [pltpu.with_memory_space_constraint(a, pltpu.HBM) for a in arrays]

    sources = in_hbm(placement, expert_ids.T, replica_pick.T, gate_weights.T, tokens)
    *chunks, combine = call(
        functools.partial(route_kernel, group_size, slot_count),
        sources,
        [HBM] * 5,
        [chunk] * slot_count + [jax.ShapeDtypeStruct((slots, tok_count), jnp.float32)],
        16 * MIB,
        [pltpu.SMEM(placement.shape, jnp.int32)]
        + [pltpu.VMEM(s.shape, s.dtype) for s in sources[1:]]
        + [pltpu.SemaphoreType.DMA((5,))],
    )
    chunks = [swap(c, d * group_size) if d else c for d, c in zip(offsets, chunks)]
    terms = [
        jax.ShapeDtypeStruct((3 * tok_count, n), bf16) for n in (capacity, slots - capacity)
    ]
    terms = local(terms_kernel, [combine], terms)

    def fetch(array, after):
        return call(
            fetch_kernel,
            (*in_hbm(array), after),
            [HBM, VMEM],
            jax.ShapeDtypeStruct(array.shape, bf16),
            16 * MIB,
            [pltpu.SemaphoreType.DMA((2,))],
            2 * array.size,
        )

    w_in = fetch(w_in, terms[0])

    square = group_size == 4
    count = slot_count // 2
    sides = ((1, 2), (2, 1))
    earlier = [w_in]
    summed = []
    for h in range(2):
        a, b = sides[h]
        own = local(
            functools.partial(stack_kernel, count), chunks[h * count :][:count] + earlier, half
        )
        if square:
            held = {a: swap(own, a), b: swap(own, b)}
            held = [own, held[a], held[b], swap(held[a], b)]
        else:
            held = [swap(own, q) if q else own for q in range(group_size)]
        earlier = []
        if h == 0:
            *result, w_out = call(
                functools.partial(fetching_expert_kernel, group_size),
                held + [w_in, *in_hbm(w_out)],
                [VMEM] * (group_size + 1) + [HBM],
                [half] * group_size + [jax.ShapeDtypeStruct(w_out.shape, bf16)],
                40 * MIB,
                [pltpu.SemaphoreType.DMA((1,))],
            )
        else:
            result = local(
                functools.partial(expert_kernel, group_size),
                held + [w_in, w_out],
                [half] * group_size,
                40 * MIB,
            )
        if square:
            mine, first, second, cross = result
            cross = swap(cross, b)
            second = swap(second, b)
            first = local(functools.partial(sum_kernel, 2), [first, cross], [half])[0]
            result = [mine, second, swap(first, a)]
        else:
            result = [swap(v, q) if q else v for q, v in enumerate(result)]
        summed += local(functools.partial(sum_kernel, len(result)), result, [chunk] * count)
    summed = [swap(v, d * group_size) if d else v for d, v in zip(offsets, summed)]
    first = local(
        first_kernel,
        [terms[0]] + summed[:1],
        jax.ShapeDtypeStruct((tok_count, width), jnp.float32),
    )
    return local(
        rest_kernel,
        [terms[1], first] + summed[1:],
        jax.ShapeDtypeStruct((tok_count, width), bf16),
    )


def solution(mesh):
    in_specs = (
        P(("dp", "expert"), None),
        P(("dp", "expert"), None),
        P(("dp", "expert"), None),
        P(("dp", "expert"), None),
        P(),
        P(None, None, "expert"),
        P("expert", None),
    )
    out_specs = P(("dp", "expert"), None)
    return jax.shard_map(body, mesh=mesh, in_specs=in_specs, out_specs=out_specs, check_vma=False)
```
